128 devices in a mesh: expert: 32 (over x, y, z_lo), tensor: 4 (over z_hi, core).
Axes of the slice: x: 4, y: 4, z: 4 (z_hi: 2, z_lo: 2; z = z_hi * 2 + z_lo), core: 2. Of those that a mesh axis runs over, the one named last changes fastest.
Arguments:
- tokens: bfloat16 [4096, 2560], P('expert', 'tensor'), may hold values from -6 to 6
- slot: int32 [4096, 1], P('expert'), may hold values from 0 to 63; in each aligned block of 128 rows (0 to 127, 128 to 255, ...) at most 4 rows name the same one
- mask: int32 [4096], P('expert'), may hold values 0 or 1
- hot_group: int32 [1], replicated, may hold values from 0 to 31
- router_weight: bfloat16 [2560, 32], replicated, may hold values from -0.125 to 0.125
- exp_gate: bfloat16 [32, 2560, 4096], P('expert', None, 'tensor'), may hold values from -0.125 to 0.125
- exp_up: bfloat16 [32, 2560, 4096], P('expert', None, 'tensor'), may hold values from -0.125 to 0.125
- exp_down: bfloat16 [32, 4096, 2560], P('expert', 'tensor'), may hold values from -0.09375 to 0.09375
- sh_gate: bfloat16 [2560, 4096], P('expert', 'tensor'), may hold values from -0.125 to 0.125
- sh_up: bfloat16 [2560, 4096], P('expert', 'tensor'), may hold values from -0.125 to 0.125
- sh_down: bfloat16 [4096, 2560], P('tensor', 'expert'), may hold values from -0.09375 to 0.09375
Outputs:
- mixed: bfloat16 [4096, 2560], P('expert', 'tensor')
The draws below stay inside these ranges and needn't reach their ends.
Inputs may be any that keep to these rules, and one draw needn't show every extreme that they name: Slot 2 g is the home slot of expert g, slot 2 g + 1 the spare slot of group g. Among the 128 tokens of one group no slot is named by more than 4 tokens, a bound that some block reaches.
All inputs are finite; a program needn't handle non-finite values. No bound on the sum of `mask` on one device may be relied on, other than what follows from the above.
Results may differ from the reference program's by a relative error of at most 0.0052.
Values may be sent and summed in bfloat16 or wider, within the bound.
A program may use at most 192 MiB of HBM per device.

```python
import math
import jax
import jax.numpy as jnp
import numpy as np
from jax import lax

D = 2560
FFE = 4096
FFS = 4096
TOK_DEV = 128
EXPERTS = 32
SLOTS = 64
CAP = 4
TOKENS = 4096
N_EXPERT = 32


def touch_ends(drawn, rng, least, largest):
    longest = drawn.shape.index(max(drawn.shape))
    spots = []
    for shift in (0, 1):
        where = [jax.random.randint(jax.random.fold_in(rng, axis), (), 0, length) for axis, length in enumerate(drawn.shape)]
        where[longest] = (where[longest] + shift) % drawn.shape[longest]
        spots.append(tuple(where))
    return drawn.at[spots[0]].set(least).at[spots[1]].set(largest)


def shard_levels(stream_key, dims, cuts, low, largest):
    def one(dim, parts):
        draws = jax.random.uniform(jax.random.fold_in(jax.random.fold_in(stream_key, 6), dim), (parts,), jnp.float32, low / len(cuts), largest / len(cuts))
        return jnp.repeat(jnp.exp(draws), dims[dim] // parts).reshape((-1,) + (1,) * (len(dims) - dim - 1))

    loudness = one(*cuts[0])
    for cut in cuts[1:]:
        loudness = loudness * one(*cut)
    return loudness


def shared_out(rng, own, number, rows, count, top, bound, lean):
    ranking = jax.random.permutation(rng, count)
    crowded, common = shares(count, rows * top, bound, lean, True), shares(count, rows * top, bound, lean, False)
    places = jnp.arange(count)

    def named(tallies, turn):
        used = int((tallies > 0).sum())
        fixed = max(1, used // 4)
        shifted = fixed + (places - fixed + turn * (used - fixed)) % max(1, count - fixed)
        return jnp.zeros((count,), jnp.int32).at[ranking[jnp.where(places < fixed, places, shifted)]].set(jnp.asarray(tallies, jnp.int32))

    tallies = jnp.where(number % 4 == 0, named(crowded, number // 4), named(common, number - number // 4 - 1))
    mixed = jax.random.permutation(jax.random.fold_in(own, 3), count)
    source_of, receiver = mixed[0:count // 2 * 2:2], mixed[1:count // 2 * 2:2]
    slack = jnp.minimum(tallies[source_of] - 1, bound - tallies[receiver]) // 2
    slack = jnp.where((source_of == ranking[0]) | (receiver == ranking[0]) | (tallies[receiver] == 0), 0, jnp.maximum(slack, 0))
    shifted = jax.random.randint(jax.random.fold_in(own, 4), (count // 2,), 0, 1 << 20) % (slack + 1)
    tallies = tallies.at[source_of].add(-shifted).at[receiver].add(shifted)
    items = jnp.searchsorted(jnp.cumsum(tallies), jnp.arange(rows * top), side="right").astype(jnp.int32)
    grid = items.reshape(top, rows).T
    grid = grid[jax.random.permutation(jax.random.fold_in(own, 1), rows)]
    turn = jax.random.randint(jax.random.fold_in(own, 2), (rows, 1), 0, top)
    return jnp.take_along_axis(grid, (jnp.arange(top)[None, :] + turn) % top, axis=1)


def shares(count, total, bound, lean, full):
    loads = [(1 << 20) // math.isqrt(rank ** lean) + 1 for rank in range(1, count + 1)]
    largest = bound if full else min(bound, max(-(-total // count), total * loads[0] // sum(loads)))
    least = 1 if total - largest >= count - 1 else 0
    given, surplus = [largest] + [least] * (count - 1), total - largest - least * (count - 1)
    while surplus > 0:
        candidates = [i for i in range(1, count) if given[i] < largest] or [i for i in range(1, count) if given[i] < bound]
        pool, budget = sum([loads[i] for i in candidates]), surplus
        for i in candidates:
            more = min(bound - given[i], max(1, budget * loads[i] // pool), surplus)
            given[i] = given[i] + more
            surplus = surplus - more
    return np.array(given)


def normal_values(rng, extent, deviation, bound, pieces=(), kind=jnp.bfloat16):
    factor_of = shard_levels(rng, extent, pieces, -0.22, 0.18) if pieces else 1.0
    array = jax.random.normal(rng, extent, jnp.float32) * deviation * factor_of
    return jnp.minimum(jnp.maximum(array, -bound), bound).astype(kind)


def setup_inputs(seed: int = 0) -> dict:
    splits = jax.random.split(jax.random.key(seed), 12)
    tokens = normal_values(splits[0], (TOKENS, D), 1.0, 6.0, ((0, 32), (1, 4)))
    slot_keys = jax.random.split(jax.random.fold_in(splits[1], 1), TOKENS // TOK_DEV)
    slot_turns = jax.random.permutation(jax.random.fold_in(splits[1], 3), TOKENS // TOK_DEV)
    slot = jax.vmap(lambda own, number: shared_out(jax.random.fold_in(splits[1], 2), own, number, TOK_DEV, SLOTS, 1, CAP, 2))(slot_keys, slot_turns).reshape((TOKENS, 1))
    mask = touch_ends((jax.random.randint(splits[2], (TOKENS,), 0, 8) < 7).astype(jnp.int32), jax.random.fold_in(splits[2], 1), 0, 1)
    hot_group = jax.random.randint(splits[3], (1,), 0, N_EXPERT).astype(jnp.int32)
    router_weight = normal_values(splits[4], (D, EXPERTS), D ** -0.5, 0.125)
    exp_gate = normal_values(splits[5], (EXPERTS, D, FFE), D ** -0.5, 0.125, ((0, 32), (2, 4)))
    exp_up = normal_values(splits[6], (EXPERTS, D, FFE), D ** -0.5, 0.125, ((0, 32), (2, 4)))
    exp_down = normal_values(splits[7], (EXPERTS, FFE, D), FFE ** -0.5, 0.09375, ((0, 32), (1, 4)))
    sh_gate = normal_values(splits[8], (D, FFS), D ** -0.5, 0.125, ((0, 32), (1, 4)))
    sh_up = normal_values(splits[9], (D, FFS), D ** -0.5, 0.125, ((0, 32), (1, 4)))
    sh_down = normal_values(splits[10], (FFS, D), FFS ** -0.5, 0.09375, ((0, 4), (1, 32)))
    return dict(tokens=tokens, slot=slot, mask=mask, hot_group=hot_group, router_weight=router_weight, exp_gate=exp_gate, exp_up=exp_up, exp_down=exp_down, sh_gate=sh_gate, sh_up=sh_up, sh_down=sh_down)


def expert_ffn(batch_rows, w_gate, w_up, w_down):
    gated = jnp.dot(batch_rows, w_gate, preferred_element_type=jnp.float32)
    upward = jnp.dot(batch_rows, w_up, preferred_element_type=jnp.float32)
    hidden = (jax.nn.silu(gated) * upward).astype(jnp.bfloat16)
    return jnp.dot(hidden, w_down, preferred_element_type=jnp.float32)


def reference(tokens, slot, mask, hot_group, router_weight, exp_gate, exp_up, exp_down, sh_gate, sh_up, sh_down):
    slot_ids = slot[:, 0].astype(jnp.int32)
    hot_index = hot_group[0].astype(jnp.int32)
    expert_id = jnp.where(slot_ids % 2 == 0, slot_ids // 2, hot_index).astype(jnp.int32)
    logits = jnp.dot(tokens, router_weight, preferred_element_type=jnp.float32)
    chosen = expert_id[:, None] == jnp.arange(EXPERTS, dtype=jnp.int32)[None, :]
    weighting = jax.nn.sigmoid(jnp.sum(jnp.where(chosen, logits, jnp.zeros_like(logits)), axis=1))
    shared = expert_ffn(tokens, sh_gate, sh_up, sh_down)
    rows_most = N_EXPERT * CAP
    ordering = jnp.argsort(slot_ids, stable=True).astype(jnp.int32)
    counts = jnp.sum((slot_ids[:, None] == jnp.arange(SLOTS, dtype=jnp.int32)[None, :]).astype(jnp.int32), axis=0).astype(jnp.int32)
    starts = (jnp.cumsum(counts) - counts).astype(jnp.int32)
    padded = jnp.concatenate([tokens[ordering], jnp.zeros((rows_most, D), tokens.dtype)], axis=0)

    def per_slot(slot_index):
        batch_rows = lax.dynamic_slice(padded, (starts[slot_index], jnp.int32(0)), (rows_most, D))
        which = jnp.where(slot_index % 2 == 0, slot_index // 2, hot_index).astype(jnp.int32)
        result = expert_ffn(batch_rows, exp_gate[which], exp_up[which], exp_down[which]).astype(jnp.bfloat16)
        within = jnp.arange(rows_most, dtype=jnp.int32) < counts[slot_index]
        return jnp.where(within[:, None], result, jnp.zeros_like(result))

    outputs = lax.map(per_slot, jnp.arange(SLOTS, dtype=jnp.int32))
    sorted_slots = slot_ids[ordering]
    offsets = (jnp.arange(TOKENS, dtype=jnp.int32) - starts[sorted_slots]).astype(jnp.int32)
    in_order = outputs[sorted_slots, offsets]
    routed = jnp.zeros_like(in_order).at[ordering].set(in_order)
    keep_rows = mask.astype(jnp.float32)
    mixed = keep_rows[:, None] * (shared + weighting[:, None] * routed.astype(jnp.float32))
    return mixed.astype(jnp.bfloat16)
```

```python
import functools

import jax
import jax.numpy as jnp
from jax import lax
from jax.experimental import pallas as pl
from jax.experimental.pallas import tpu as pltpu
from jax.sharding import PartitionSpec as P

MESH = pl.DeviceIdType.MESH
NX, NY, NZ, NT, CAP = 4, 4, 2, 4, 4


def coords():
    e = lax.axis_index("expert")
    return lax.div(e, NY * NZ), lax.rem(lax.div(e, NZ), NY), lax.rem(e, NZ)


def group_of(x, y, z):
    return (x * NY + y) * NZ + z


def turn(i, n=4):
    return lax.rem(i + 2 * n, n)


class Copies:
    def __init__(self, send, recv, local):
        self.send, self.recv, self.local = send, recv, local
        self.sent, self.kept = 0, 0
        self.started = []

    def remote(self, src, dst, device):
        c = pltpu.make_async_remote_copy(
            src_ref=src,
            dst_ref=dst,
            send_sem=self.send.at[self.sent],
            recv_sem=self.recv.at[self.sent],
            device_id=device,
            device_id_type=MESH,
        )
        self.sent += 1
        c.start()
        self.started.append(c)
        return c

    def here(self, src, dst):
        c = pltpu.make_async_copy(src, dst, self.local.at[self.kept])
        self.kept += 1
        c.start()
        return c


def entry_barrier(devices):
    barrier = pltpu.get_barrier_semaphore()
    for d in devices:
        pl.semaphore_signal(barrier, inc=1, device_id=d, device_id_type=MESH)
    pl.semaphore_wait(barrier, len(devices))


def choose(flag, rows, step, mine, into):
    def body(i, carry):
        at = pl.ds(pl.multiple_of(i * step, step), step)
        into[at] = jnp.where(flag == 1, mine(at), into[at])
        return carry

    lax.fori_loop(0, rows // step, body, 0)


def spread_kernel(
    flags, gate, up, down, sh_own, tok,
    hg, hu, hd, sh, tk,
    own_g, own_u, own_d, xg, xu, yg, yu, yd, xd, zg, zu, zd,
    send, recv, local,
):
    x, y, z = coords()
    t = lax.axis_index("tensor")
    cp = Copies(send, recv, local)
    rows, cols = xg.shape[2], xg.shape[3]
    quarter = tok.shape[1]

    def at(dx=0, dy=0, dz=0):
        return {"expert": group_of(turn(x + dx), turn(y + dy), turn(z + dz, 2)), "tensor": t}

    def peer(dt):
        return {"expert": group_of(x, y, z), "tensor": turn(t + dt)}

    entry_barrier(
        [at(1), at(-1), at(2), at(0, 1), at(0, -1), at(0, 0, 1), peer(1), peer(2), peer(3)]
    )
    fx, fy, fz = flags[0], flags[1], flags[2]

    streams = ((gate, own_g, xg, yg, zg, hg, 1), (up, own_u, xu, yu, zu, hu, -1))

    def block(sign, j):
        return turn(y - sign * (1 + j))

    def piece(ref, sign, j, xp):
        return ref.at[
            pl.ds(pl.multiple_of(block(sign, j) * rows, rows), rows),
            pl.ds(pl.multiple_of(xp * cols, cols), cols),
        ]

    x_copy = {}

    def x_first(j):
        for s, (w, _, xb, _, _, _, sign) in enumerate(streams):
            x_copy[s, j, 0] = cp.remote(piece(w, sign, j, turn(x - sign)), xb.at[j, 0], at(sign))

    own_copy = {}

    def own_load(j):
        for s, (w, own, _, _, _, _, sign) in enumerate(streams):
            src = w.at[pl.ds(pl.multiple_of(block(sign, j) * rows, rows), rows), :]
            own_copy[s, j] = cp.here(src, own.at[j])

    def x_step(j, step):
        for s, (_, own, xb, _, _, _, sign) in enumerate(streams):
            x_copy[s, j, step].wait_recv()
            if step == 0:
                own_copy[s, j].wait()
            xp = turn(x - sign * (2 + step))
            lanes = pl.ds(pl.multiple_of(xp * cols, cols), cols)
            choose(fx, rows, rows // 4, lambda r, own=own, lanes=lanes: own[j, r, lanes], xb.at[j, step])
            if step < 2:
                x_copy[s, j, step + 1] = cp.remote(xb.at[j, step], xb.at[j, step + 1], at(sign))

    y_copy = {}

    def y_step(j):
        for s, (_, _, xb, yb, _, _, sign) in enumerate(streams):
            if j == 0:
                y_copy[s, 0] = cp.remote(xb.at[0, 2], yb.at[0], at(0, sign))
                continue
            y_copy[s, j - 1].wait_recv()
            choose(fy, rows, rows // 4, lambda r, xb=xb: xb[j, 2, r], yb.at[j - 1])
            if j < 3:
                y_copy[s, j] = cp.remote(yb.at[j - 1], yb.at[j], at(0, sign))

    d_copy = {}

    def d_first():
        for r, sign in ((0, 1), (1, -1)):
            d_copy[r, 0] = cp.remote(down.at[:, turn(y - sign), r], yd.at[r, 0], at(0, sign))

    def d_step(step):
        for r, sign in ((0, 1), (1, -1)):
            d_copy[r, step].wait_recv()
            yp = turn(y - sign * (2 + step))
            choose(fy, NX, 1, lambda i, yp=yp, r=r: own_d[i, yp, r], yd.at[r, step])
            if step < 2:
                d_copy[r, step + 1] = cp.remote(yd.at[r, step], yd.at[r, step + 1], at(0, sign))

    dx_copy = {}

    def dx_step(step):
        for r, sign in ((0, 1), (1, -1)):
            if step == 0:
                dx_copy[r, 0] = cp.remote(yd.at[r, 2, turn(x - sign)], xd.at[r, 0], at(sign))
                continue
            dx_copy[r, step - 1].wait_recv()
            xp = turn(x - sign * (1 + step))
            n = xd.shape[2]
            choose(fx, n, 16, lambda i, xp=xp, r=r: yd[r, 2, xp, i], xd.at[r, step - 1])
            if step < 3:
                dx_copy[r, step] = cp.remote(xd.at[r, step - 1], xd.at[r, step], at(sign))

    x_first(0)
    d_first()
    own_load(0)
    own_d_copy = cp.here(down, own_d)
    k = sh_own.shape[1]

    def sh_piece(xp):
        return sh_own.at[:, :, pl.ds(pl.multiple_of(xp * cols, cols), cols)]

    s_x = [
        cp.remote(sh_piece(turn(x + d)), sh.at[:, x, y, z], at(d)) for d in (1, -1, 2)
    ]
    s_own = cp.here(sh_piece(x), sh.at[:, x, y, z])
    mine = pl.ds(pl.multiple_of(t * quarter, quarter), quarter)
    t_x = [cp.remote(tok, tk.at[x, :, mine], at(d)) for d in (1, -1, 2)]
    t_own = cp.here(tok, tk.at[x, :, mine])
    x_first(1)
    own_load(1)
    own_load(2)
    own_load(3)

    x_step(0, 0)
    for c in t_x:
        c.wait_recv()
    t_own.wait()
    t_t = [cp.remote(tk.at[:, :, mine], tk.at[:, :, mine], peer(d)) for d in (1, 2, 3)]
    for c in s_x:
        c.wait_recv()
    s_own.wait()
    s_y = [cp.remote(sh.at[:, :, y, z], sh.at[:, :, y, z], at(0, d)) for d in (1, -1)]
    s_z = [cp.remote(sh.at[:, :, y, z], sh.at[:, :, y, z], at(0, 0, 1))]
    x_step(1, 0)
    own_d_copy.wait()
    d_step(0)
    x_step(0, 1)
    x_step(1, 1)
    x_first(2)
    x_first(3)
    for c in s_y:
        c.wait_recv()
    lo, hi = turn(y - 1), turn(y + 1)
    s_y2 = [
        cp.remote(sh.at[:, 0:2, lo, z], sh.at[:, 0:2, lo, z], at(0, 1)),
        cp.remote(sh.at[:, 2:4, hi, z], sh.at[:, 2:4, hi, z], at(0, -1)),
    ]
    s_z += [cp.remote(sh.at[:, :, v, z], sh.at[:, :, v, z], at(0, 0, 1)) for v in (lo, hi)]
    d_step(1)
    x_step(0, 2)
    y_step(0)
    x_step(1, 2)
    y_step(1)
    d_step(2)
    dx_step(0)
    for c in s_y2:
        c.wait_recv()
    far = turn(y + 2)
    s_z.append(cp.remote(sh.at[:, :, far, z], sh.at[:, :, far, z], at(0, 0, 1)))
    x_step(2, 0)
    dx_step(1)
    x_step(3, 0)
    dx_step(2)
    x_step(2, 1)
    dx_step(3)
    d_z = [cp.remote(xd.at[r, 2], zd.at[r], at(0, 0, 1)) for r in (0, 1)]
    x_step(3, 1)
    d_y, d_own = [], []
    for r in (0, 1):
        d_z[r].wait_recv()
        choose(fz, zd.shape[1], 16, lambda i, r=r: xd[r, 2, i], zd.at[r])
        d_own.append(cp.here(zd.at[r], hd.at[y, r]))
        d_y.append([cp.remote(zd.at[r], hd.at[y, r], at(0, d)) for d in (1, -1)])
    x_step(2, 2)
    y_step(2)
    d_y[0][0].wait_recv()
    d_y[1][1].wait_recv()
    d_y2 = [
        cp.remote(hd.at[lo, 0], hd.at[lo, 0], at(0, 1)),
        cp.remote(hd.at[hi, 1], hd.at[hi, 1], at(0, -1)),
    ]
    x_step(3, 2)
    y_step(3)
    z_copy = [cp.remote(st[3].at[2], st[4], at(0, 0, 1)) for st in streams]
    a_own, a_y = [], []

    def rows_of(ref, v):
        return ref.at[pl.ds(pl.multiple_of(v * rows, rows), rows)]

    for s, (_, _, _, yb, zb, h, sign) in enumerate(streams):
        z_copy[s].wait_recv()
        choose(fz, rows, rows // 4, lambda r, yb=yb: yb[2, r], zb)
        a_own.append(cp.here(zb, rows_of(h, y)))
        a_y.append([cp.remote(zb, rows_of(h, y), at(0, d)) for d in (sign, -sign)])
    a_y2 = []
    for s, st in enumerate(streams):
        h, sign = st[5], st[6]
        a_y[s][0].wait_recv()
        v = turn(y - sign)
        a_y2.append(cp.remote(rows_of(h, v), rows_of(h, v), at(0, sign)))
    for c in t_t + s_z + d_y2:
        c.wait_recv()
    d_y[0][1].wait_recv()
    d_y[1][0].wait_recv()
    for s in (0, 1):
        a_y[s][1].wait_recv()
        a_y2[s].wait_recv()
    for c in d_own + a_own:
        c.wait()
    for c in cp.started:
        c.wait_send()


def spread(flags, gate, up, down, sh_own, tok):
    d, h = gate.shape
    rows, cols = d // NY, h // NX
    part = cols // (2 * NY)
    down = down.reshape(NX, NY, 2, part, d)
    bf = jnp.bfloat16
    any_spec = pl.BlockSpec(memory_space=pl.ANY)
    return pl.pallas_call(
        spread_kernel,
        out_shape=[
            jax.ShapeDtypeStruct((d, cols), bf),
            jax.ShapeDtypeStruct((d, cols), bf),
            jax.ShapeDtypeStruct((NY, 2, part, d), bf),
            jax.ShapeDtypeStruct((3, NX, NY, NZ, sh_own.shape[1], cols), bf),
            jax.ShapeDtypeStruct((NX, tok.shape[0], NT * tok.shape[1]), bf),
        ],
        in_specs=[pl.BlockSpec(memory_space=pltpu.SMEM)] + [any_spec] * 5,
        out_specs=[any_spec] * 5,
        scratch_shapes=[
            pltpu.VMEM((NY, rows, h), bf),
            pltpu.VMEM((NY, rows, h), bf),
            pltpu.VMEM((NX, NY, 2, part, d), bf),
            pltpu.VMEM((NY, 3, rows, cols), bf),
            pltpu.VMEM((NY, 3, rows, cols), bf),
            pltpu.VMEM((3, rows, cols), bf),
            pltpu.VMEM((3, rows, cols), bf),
            pltpu.VMEM((2, 3, NX, part, d), bf),
            pltpu.VMEM((2, 3, part, d), bf),
            pltpu.VMEM((rows, cols), bf),
            pltpu.VMEM((rows, cols), bf),
            pltpu.VMEM((2, part, d), bf),
            pltpu.SemaphoreType.DMA((80,)),
            pltpu.SemaphoreType.DMA((80,)),
            pltpu.SemaphoreType.DMA((20,)),
        ],
        compiler_params=pltpu.CompilerParams(
            collective_id=0, has_side_effects=True, vmem_limit_bytes=44 * 2**20
        ),
    )(flags, gate, up, down, sh_own, tok)


def sum_kernel(part, out, kept, from_core, mid, from_x, half, from_z, send, recv, local):
    x, y, z = coords()
    t = lax.axis_index("tensor")
    core, z_hi = lax.rem(t, 2), lax.div(t, 2)
    g = group_of(x, y, z)
    cp = Copies(send, recv, local)
    n, width = from_x.shape[1], from_x.shape[2]
    quarter = width // 2
    other = {"expert": g, "tensor": z_hi * 2 + (1 - core)}
    across = {"expert": g, "tensor": (1 - z_hi) * 2 + core}

    def at(dx):
        return {"expert": group_of(turn(x + dx), y, z), "tensor": t}

    entry_barrier([other, across, at(1), at(-1), at(2)])
    order = (2, 1, 3, 0)
    c_copy, k_copy = [], []
    for d in order:
        xp = turn(x + d)
        c_copy.append(
            cp.remote(part.at[xp, 1 - core], from_core.at[d], other)
        )
        k_copy.append(cp.here(part.at[xp, core], kept.at[d]))
    x_copy = []
    for i, d in enumerate(order):
        c_copy[i].wait_recv()
        k_copy[i].wait()

        def body(r, carry, d=d):
            a = pl.ds(pl.multiple_of(r * 32, 32), 32)
            mid[d, a] = (
                kept[d, a].astype(jnp.float32) + from_core[d, a].astype(jnp.float32)
            ).astype(mid.dtype)
            return carry

        lax.fori_loop(0, n // 32, body, 0)
        if d:
            x_copy.append(cp.remote(mid.at[d], from_x.at[(d - 1)], at(d)))
    for c in x_copy:
        c.wait_recv()
    away = pl.ds(pl.multiple_of((1 - z_hi) * quarter, quarter), quarter)
    own = pl.ds(pl.multiple_of(z_hi * quarter, quarter), quarter)

    def total(a, lanes):
        v = kept[0, a, lanes].astype(jnp.float32) + from_core[0, a, lanes].astype(jnp.float32)
        for i in range(3):
            v += from_x[i, a, lanes].astype(jnp.float32)
        return v

    def body2(r, carry):
        a = pl.ds(pl.multiple_of(r * 32, 32), 32)
        half[a] = total(a, away).astype(half.dtype)
        return carry

    lax.fori_loop(0, n // 32, body2, 0)
    z_copy = cp.remote(half, from_z, across)
    z_copy.wait_recv()

    def body3(r, carry):
        a = pl.ds(pl.multiple_of(r * 32, 32), 32)
        out[a] = total(a, own) + from_z[a].astype(jnp.float32)
        return carry

    lax.fori_loop(0, n // 32, body3, 0)
    for c in cp.started:
        c.wait_send()


def summed(part):
    _, _, n, width = part.shape
    bf = jnp.bfloat16
    return pl.pallas_call(
        sum_kernel,
        out_shape=jax.ShapeDtypeStruct((n, width // 2), jnp.float32),
        in_specs=[pl.BlockSpec(memory_space=pl.ANY)],
        out_specs=pl.BlockSpec(memory_space=pltpu.VMEM),
        scratch_shapes=[
            pltpu.VMEM((NX, n, width), bf),
            pltpu.VMEM((NX, n, width), bf),
            pltpu.VMEM((NX, n, width), bf),
            pltpu.VMEM((3, n, width), bf),
            pltpu.VMEM((n, width // 2), bf),
            pltpu.VMEM((n, width // 2), bf),
            pltpu.SemaphoreType.DMA((10,)),
            pltpu.SemaphoreType.DMA((10,)),
            pltpu.SemaphoreType.DMA((5,)),
        ],
        compiler_params=pltpu.CompilerParams(
            collective_id=1, has_side_effects=True, vmem_limit_bytes=24 * 2**20
        ),
    )(part)


def dot(a, b):
    return jnp.dot(a, b, preferred_element_type=jnp.float32)


def hidden_units(rows, w_gate, w_up):
    return jax.nn.silu(dot(rows, w_gate)) * dot(rows, w_up)


def local(
    tokens, slot, mask, hot_group, router_weight,
    exp_gate, exp_up, exp_down, sh_gate, sh_up, sh_down,
):
    n_groups = lax.axis_size("expert")
    bf = jnp.bfloat16
    x, y, z = coords()
    hot = hot_group[0]
    hx, hy, hz = hot // (NY * NZ), (hot // NZ) % NY, hot % NZ
    flags = jnp.stack([hx == x, hy == y, hz == z]).astype(jnp.int32)
    quads = [[(a * NY + b) * NZ + c for a in range(NX)] for b in range(NY) for c in range(NZ)]
    n = tokens.shape[0]

    whole = lax.all_gather(tokens, "tensor", axis=1, tiled=True)
    ids = slot[:, 0]
    same = ids[:, None] == ids[None, :]
    earlier = lax.broadcasted_iota(jnp.int32, (n, n), 1) < lax.broadcasted_iota(jnp.int32, (n, n), 0)
    position = jnp.sum((same & earlier).astype(jnp.int32), axis=1)
    target = jnp.where(ids % 2 == 0, (ids // 2) * CAP + position, -1)
    placing = lax.broadcasted_iota(jnp.int32, (n_groups * CAP, 1), 0) == target[None, :]
    outgoing = dot(placing.astype(bf), whole).astype(bf)
    arrived = lax.all_to_all(outgoing, "expert", split_axis=0, concat_axis=0, tiled=True)
    home_hidden = hidden_units(arrived, exp_gate[0], exp_up[0]).astype(bf)
    home_part = dot(home_hidden, exp_down[0]).astype(bf)
    returned = lax.all_to_all(home_part, "expert", split_axis=0, concat_axis=0, tiled=True)

    sh_own = jnp.stack([sh_gate, sh_up, sh_down.T])
    hot_gate, hot_up, hot_down, sh, quad_tokens = spread(
        flags, exp_gate[0], exp_up[0], exp_down[0], sh_own, tokens
    )
    d = hot_gate.shape[0]
    hot_down = hot_down.reshape(-1, d)
    sh = sh.reshape(3, d, -1)
    quad_tokens = quad_tokens.reshape(NX * n, d)
    quad_ids = lax.all_gather(ids, "expert", axis_index_groups=quads).reshape(-1)
    expert_id = jnp.where(quad_ids % 2 == 0, quad_ids // 2, hot)
    logits = dot(quad_tokens, router_weight)
    chosen = expert_id[:, None] == lax.broadcasted_iota(jnp.int32, (1, router_weight.shape[1]), 1)
    weighting = jax.nn.sigmoid(jnp.sum(jnp.where(chosen, logits, 0.0), axis=1))
    spare = jnp.where(quad_ids % 2 == 1, weighting, 0.0)

    sh_hidden = hidden_units(quad_tokens, sh[0], sh[1]).astype(bf)
    hot_hidden = (hidden_units(quad_tokens, hot_gate, hot_up) * spare[:, None]).astype(bf)
    part = lax.dot_general(
        sh_hidden, sh[2], (((1,), (1,)), ((), ())), preferred_element_type=jnp.float32
    ) + dot(hot_hidden, hot_down)
    back = lax.dot_general(
        placing.astype(bf), returned, (((0,), (0,)), ((), ())), preferred_element_type=jnp.float32
    )
    own_weighting = lax.dynamic_slice_in_dim(weighting, x * n, n)
    here = (lax.broadcasted_iota(jnp.int32, (NX, 1, 1), 0) == x).astype(jnp.float32)
    part = part.reshape(NX, n, d) + here * (own_weighting[:, None] * back)[None]
    part = part.astype(bf).reshape(NX, n, 2, 2, d // 4)
    part = part.transpose(0, 3, 1, 2, 4).reshape(NX, 2, n, d // 2)
    mixed = mask.astype(jnp.float32)[:, None] * summed(part)
    return mixed.astype(bf)


def solution(mesh):
    in_specs = (
        P("expert", "tensor"),
        P("expert", None),
        P("expert"),
        P(),
        P(),
        P("expert", None, "tensor"),
        P("expert", None, "tensor"),
        P("expert", "tensor", None),
        P("expert", "tensor"),
        P("expert", "tensor"),
        P("tensor", "expert"),
    )
    out_specs = P("expert", "tensor")
    return jax.shard_map(local, mesh=mesh, in_specs=in_specs, out_specs=out_specs, check_vma=False)
```

```python
import jax
import jax.numpy as jnp
from jax import lax
from jax.experimental import pallas as pl
from jax.experimental.pallas import tpu as pltpu
from jax.sharding import PartitionSpec as P

MESH = pl.DeviceIdType.MESH
NX, NY, NZ, NT, CAP = 4, 4, 2, 4, 4


def coords():
    e = lax.axis_index("expert")
    return lax.div(e, NY * NZ), lax.rem(lax.div(e, NZ), NY), lax.rem(e, NZ)


def group_of(x, y, z):
    return (x * NY + y) * NZ + z


def turn(i, n=4):
    return lax.rem(i + 2 * n, n)


class Copies:
    def __init__(self, send, recv, local):
        self.send, self.recv, self.local = send, recv, local
        self.sent, self.kept = 0, 0
        self.started = []

    def remote(self, src, dst, device):
        c = pltpu.make_async_remote_copy(
            src_ref=src,
            dst_ref=dst,
            send_sem=self.send.at[self.sent],
            recv_sem=self.recv.at[self.sent],
            device_id=device,
            device_id_type=MESH,
        )
        self.sent += 1
        c.start()
        self.started.append(c)
        return c

    def here(self, src, dst):
        c = pltpu.make_async_copy(src, dst, self.local.at[self.kept])
        self.kept += 1
        c.start()
        return c


def choose(flag, rows, step, mine, into):
    def body(i, carry):
        at = pl.ds(pl.multiple_of(i * step, step), step)
        into[at] = jnp.where(flag == 1, mine(at), into[at])
        return carry

    lax.fori_loop(0, rows // step, body, 0)


def dot(a, b):
    return jnp.dot(a, b, preferred_element_type=jnp.float32)


def silu(v):
    return v / (1.0 + jnp.exp(-v))


def layer_kernel(
    scalars, tok, slot, mask, router, gate, up, down, sh_own,
    out,
    own_g, own_u, own_d, xg, xu, yg, yu, yd, xd, hg, hu, hd, sh, tk, coefs,
    pack1, got1, pack2, got2, rows_in, home_g, home_u, home_hid,
    acc_g, acc_u, sh_hid, hot_hid, psum, to_core, from_core, mid, from_x, half, from_z,
    w_cols, target_cols,
    send, recv, local, a2a_send, a2a_recv,
):
    x, y, z = coords()
    e = lax.axis_index("expert")
    groups = lax.axis_size("expert")
    t = lax.axis_index("tensor")
    core, z_hi = lax.rem(t, 2), lax.div(t, 2)
    cp = Copies(send, recv, local)
    rows, cols = xg.shape[2], xg.shape[3]
    n, quarter = tok.shape
    bf, f32 = jnp.bfloat16, jnp.float32
    parts = ((0, rows * 3 // 5), (rows * 3 // 5, rows * 2 // 5))

    def at(dx=0, dy=0, dz=0):
        return {"expert": group_of(turn(x + dx), turn(y + dy), turn(z + dz, 2)), "tensor": t}

    other_t = z_hi * 2 + (1 - core)
    across_t = (1 - z_hi) * 2 + core
    other = {"expert": e, "tensor": other_t}
    across = {"expert": e, "tensor": across_t}

    def of_quarter(i):
        return pl.ds(pl.multiple_of(i * quarter, quarter), quarter)

    barrier = pltpu.get_barrier_semaphore()

    def greet(k, carry):
        d = {"expert": lax.rem(e + k, groups), "tensor": t}
        pl.semaphore_signal(barrier, inc=1, device_id=d, device_id_type=MESH)
        return carry

    lax.fori_loop(1, groups, greet, 0)
    for d in (other, across):
        pl.semaphore_signal(barrier, inc=1, device_id=d, device_id_type=MESH)
    pl.semaphore_wait(barrier, groups + 1)
    fx, fy, fz, hot = scalars[0], scalars[1], scalars[2], scalars[3]

    streams = ((gate, own_g, xg, yg, hg, 1), (up, own_u, xu, yu, hu, -1))

    def block(sign, j):
        return turn(y - sign * (1 + j))

    x_copy, own_copy, y_copy, z_copy = {}, {}, {}, {}

    def x_first(h, js):
        off, r = parts[h]
        for j in js:
            for s, (w, _, xb, _, _, sign) in enumerate(streams):
                lanes = pl.ds(pl.multiple_of(turn(x - sign) * cols, cols), cols)
                src = w.at[pl.ds(pl.multiple_of(block(sign, j) * rows + off, 128), r), lanes]
                x_copy[h, s, j, 0] = cp.remote(src, xb.at[j, 0, pl.ds(off, r)], at(sign))

    def own_load(j):
        for s, (w, own, _, _, _, sign) in enumerate(streams):
            src = w.at[pl.ds(pl.multiple_of(block(sign, j) * rows, rows), rows), :]
            own_copy[s, j] = cp.here(src, own.at[j])

    def x_step(h, j, step):
        off, r = parts[h]
        for s, (_, own, xb, _, _, sign) in enumerate(streams):
            x_copy[h, s, j, step].wait_recv()
            if h == 0 and step == 0:
                own_copy[s, j].wait()
            lanes = pl.ds(pl.multiple_of(turn(x - sign * (2 + step)) * cols, cols), cols)
            mine = own.at[j, pl.ds(off, r)]
            into = xb.at[j, step, pl.ds(off, r)]
            choose(fx, r, 128, lambda a, mine=mine, lanes=lanes: mine[a, lanes], into)
            if step < 2:
                nxt = xb.at[j, step + 1, pl.ds(off, r)]
                x_copy[h, s, j, step + 1] = cp.remote(into, nxt, at(sign))

    def y_step(h, j):
        off, r = parts[h]
        for s, (_, _, xb, yb, hb, sign) in enumerate(streams):
            mine = xb.at[j, 2, pl.ds(off, r)]
            if j == 0:
                y_copy[h, s, 0] = cp.remote(mine, yb.at[0, pl.ds(off, r)], at(0, sign))
                continue
            into = yb.at[j - 1, pl.ds(off, r)]
            y_copy[h, s, j - 1].wait_recv()
            choose(fy, r, 128, lambda a, mine=mine: mine[a], into)
            if j < 3:
                y_copy[h, s, j] = cp.remote(into, yb.at[j, pl.ds(off, r)], at(0, sign))
            else:
                z_copy[h, s] = cp.remote(into, hot_rows(hb, h, y), at(0, 0, 1))

    def hot_rows(ref, h, v):
        off, r = parts[h]
        return ref.at[pl.ds(pl.multiple_of(v * rows + off, 128), r)]

    near, far2 = {}, {}

    def spread_y(h):
        off, r = parts[h]
        for s, (_, _, _, yb, hb, sign) in enumerate(streams):
            into = hot_rows(hb, h, y)
            mine = yb.at[2, pl.ds(off, r)]
            z_copy[h, s].wait_recv()
            choose(fz, r, 128, lambda a, mine=mine: mine[a], into)
            near[h, s] = [cp.remote(into, into, at(0, d)) for d in (sign, -sign)]

    def forward_y(h):
        for s, (_, _, _, _, hb, sign) in enumerate(streams):
            near[h, s][0].wait_recv()
            a = hot_rows(hb, h, turn(y - sign))
            far2[h, s] = cp.remote(a, a, at(0, sign))

    def hot_arrived(h):
        for s in (0, 1):
            near[h, s][1].wait_recv()
            far2[h, s].wait_recv()

    d_copy, dx_copy = {}, {}

    def d_first():
        for r, sign in ((0, 1), (1, -1)):
            d_copy[r, 0] = cp.remote(down.at[:, turn(y - sign), r], yd.at[r, 0], at(0, sign))

    def d_step(step):
        for r, sign in ((0, 1), (1, -1)):
            d_copy[r, step].wait_recv()
            yp = turn(y - sign * (2 + step))
            choose(fy, NX, 1, lambda i, yp=yp, r=r: own_d[i, yp, r], yd.at[r, step])
            if step < 2:
                d_copy[r, step + 1] = cp.remote(yd.at[r, step], yd.at[r, step + 1], at(0, sign))

    def dx_step(step):
        for r, sign in ((0, 1), (1, -1)):
            if step == 0:
                dx_copy[r, 0] = cp.remote(yd.at[r, 2, turn(x - sign)], xd.at[r, 0], at(sign))
                continue
            dx_copy[r, step - 1].wait_recv()
            xp = turn(x - sign * (1 + step))
            choose(
                fx, xd.shape[2], 16, lambda i, xp=xp, r=r: yd[r, 2, xp, i], xd.at[r, step - 1]
            )
            if step < 3:
                dx_copy[r, step] = cp.remote(xd.at[r, step - 1], xd.at[r, step], at(sign))

    def exchange(src, dst, base):
        def go(k, carry):
            to = lax.rem(e + k, groups)
            pltpu.make_async_remote_copy(
                src_ref=src.at[to], dst_ref=dst.at[e],
                send_sem=a2a_send.at[base + k], recv_sem=a2a_recv.at[base + k],
                device_id={"expert": to, "tensor": t}, device_id_type=MESH,
            ).start()
            return carry

        lax.fori_loop(1, groups, go, 0)
        return cp.here(src.at[e], dst.at[e])

    def exchanged(src, dst, base, sends):
        def done(k, carry):
            to = lax.rem(e + k, groups)
            frm = lax.rem(e + groups - k, groups)
            c = pltpu.make_async_remote_copy(
                src_ref=src.at[to], dst_ref=dst.at[frm],
                send_sem=a2a_send.at[base + k], recv_sem=a2a_recv.at[base + k],
                device_id={"expert": to, "tensor": t}, device_id_type=MESH,
            )
            if sends:
                c.wait_send()
            else:
                c.wait_recv()
            return carry

        lax.fori_loop(1, groups, done, 0)

    def iota(shape, dim):
        return lax.broadcasted_iota(jnp.int32, shape, dim)

    def as_row(col):
        eye = iota((n, n), 0) == iota((n, n), 1)
        return jnp.sum(jnp.where(eye, col, 0.0), axis=0, keepdims=True)

    def as_col(row):
        eye = iota((n, n), 0) == iota((n, n), 1)
        return jnp.sum(jnp.where(eye, row, 0.0), axis=1, keepdims=True)

    blocks_at_once = n // 16

    def packed(c, q, key):
        r = iota((n, n), 0) + c * n
        of = (r // 16) * 4 + r % 4
        return ((of.astype(f32) == key) & ((r // 4) % 4 == q)).astype(bf)

    def unpacked(q, key):
        r = iota((n, 4 * n), 1)
        of = (r // 16) * 4 + r % 4
        return ((of.astype(f32) == key) & ((r // 4) % 4 == q)).astype(bf)

    mine = of_quarter(t)
    t_peer = [cp.remote(tok, tk.at[0, :, mine], d) for d in (other, across)]
    x_first(0, (0, 1))
    d_first()
    t_own = cp.here(tok, tk.at[0, :, mine])
    t_x = [cp.remote(tok, tk.at[(4 - d) % 4, :, mine], at(d)) for d in (1, -1, 2)]

    def sh_piece(xp):
        return sh_own.at[:, :, pl.ds(pl.multiple_of(xp * cols, cols), cols)]

    s_x = [cp.remote(sh_piece(turn(x + d)), sh.at[:, x, y, z], at(d)) for d in (1, -1, 2)]
    s_own = cp.here(sh_piece(x), sh.at[:, x, y, z])
    x_first(0, (2, 3))
    own_load(0)
    own_d_copy = cp.here(down, own_d)
    for j in (1, 2, 3):
        own_load(j)

    ids = slot[...]
    spare = (ids & 1) == 1
    expert = ids >> 1
    ids_f = ids.astype(f32)
    same = jnp.where(
        (ids_f == as_row(ids_f)) & (iota((n, n), 1) < iota((n, n), 0)), 1.0, 0.0
    )
    position = jnp.sum(same, axis=1, keepdims=True)
    target = jnp.where(spare, -1.0, expert.astype(f32) * CAP + position)
    target_cols[...] = jnp.broadcast_to(target, target_cols.shape)

    t_own.wait()
    t_peer[1].wait_recv()
    a = tk.at[0, :, of_quarter(across_t)]
    t_fwd = cp.remote(a, a, other)
    t_peer[0].wait_recv()
    t_fwd.wait_recv()
    target_row = as_row(target)
    for c in range(4):
        acc = jnp.zeros((n, quarter), f32)
        for q in range(4):
            acc += dot(packed(c, q, target_row), tk[0, :, q * quarter : (q + 1) * quarter])
        pack1[c * blocks_at_once : (c + 1) * blocks_at_once] = acc.astype(bf).reshape(
            blocks_at_once, 16, quarter
        )
    own1 = exchange(pack1, got1, 0)
    logits = dot(tk[0], router[...])
    chosen = jnp.where(spare, hot, expert) == iota(logits.shape, 1)
    w = jax.nn.sigmoid(jnp.sum(jnp.where(chosen, logits, 0.0), axis=1, keepdims=True))
    w_cols[...] = jnp.broadcast_to(w, w_cols.shape)
    coefs[0] = jnp.broadcast_to(as_row(jnp.where(spare, w, 0.0)), coefs.shape[1:])
    c_x = [cp.remote(coefs.at[0], coefs.at[(4 - d) % 4], at(d)) for d in (1, -1, 2)]

    def unpack_rows():
        exchanged(pack1, got1, 0, False)
        own1.wait()
        flat = got1[...].reshape(4 * n, quarter)
        key = iota((n, 1), 0).astype(f32)
        for q in range(4):
            rows_in[:, q * quarter : (q + 1) * quarter] = dot(unpacked(q, key), flat).astype(bf)

    def home_in(j):
        for acc, own, sign in ((home_g, own_g, 1), (home_u, own_u, -1)):
            a = rows_in[:, pl.ds(pl.multiple_of(block(sign, j) * rows, rows), rows)]
            v = dot(a, own[j])
            acc[...] = v if j == 0 else acc[...] + v

    def home_mid():
        home_hid[...] = (silu(home_g[...]) * home_u[...]).astype(bf)

    def home_out(q):
        lanes = slice(q * quarter, (q + 1) * quarter)
        v = jnp.zeros((n, quarter), f32)
        for i in range(NX):
            wd = own_d[i, :, :, :, lanes].reshape(cols, quarter)
            v += dot(home_hid[:, i * cols : (i + 1) * cols], wd)
        acc_rows = v.astype(bf)
        row = iota((1, n), 1).astype(f32)
        for c in range(4):
            a = slice(c * blocks_at_once, (c + 1) * blocks_at_once)
            p = dot(packed(c, q, row), acc_rows).astype(bf).reshape(blocks_at_once, 16, quarter)
            pack2[a] = p if q == 0 else pack2[a] + p

    def home_back():
        exchanged(pack2, got2, groups, False)
        own2.wait()
        flat = got2[...].reshape(4 * n, quarter)
        key = target_cols[:, 0:1]
        for q in range(4):
            back = dot(unpacked(q, key), flat)
            psum[0, q] = psum[0, q] + w_cols[:, 0:1] * back

    def quad_in(lanes, w_gate, w_up, first):
        a = tk[:, :, lanes].reshape(NX * n, -1)
        for acc, wt in ((acc_g, w_gate), (acc_u, w_up)):
            v = dot(a, wt)
            acc[...] = v if first else acc[...] + v

    def shared_in(k):
        quad_in(
            slice(k * rows, (k + 1) * rows),
            sh[0, k].reshape(rows, cols), sh[1, k].reshape(rows, cols), k == 0,
        )

    def shared_mid():
        sh_hid[...] = (silu(acc_g[...]) * acc_u[...]).astype(bf)

    def shared_out(q):
        wt = sh[2, q].reshape(quarter, cols)
        v = lax.dot_general(
            sh_hid[...], wt, (((1,), (1,)), ((), ())), preferred_element_type=f32
        )
        psum[:, q] = v.reshape(NX, n, quarter)

    def hot_in(h, k):
        off, r = parts[h]
        lanes = slice(k * rows + off, k * rows + off + r)
        quad_in(lanes, hg[lanes], hu[lanes], h == 0 and k == 0)

    x_step(0, 0, 0)
    x_step(0, 1, 0)
    for c in t_x:
        c.wait_recv()
    t_t = [cp.remote(tk.at[1:4, :, mine], tk.at[1:4, :, mine], d) for d in (other, across)]
    for c in s_x:
        c.wait_recv()
    s_own.wait()
    s_y = [cp.remote(sh.at[:, :, y, z], sh.at[:, :, y, z], at(0, d)) for d in (1, -1)]
    s_z = [cp.remote(sh.at[:, :, y, z], sh.at[:, :, y, z], at(0, 0, 1))]
    x_step(0, 2, 0)
    x_step(0, 3, 0)
    own_d_copy.wait()
    d_step(0)
    x_step(0, 0, 1)
    x_step(0, 1, 1)
    t_t[1].wait_recv()
    a = tk.at[1:4, :, of_quarter(across_t)]
    t_fwd2 = cp.remote(a, a, other)
    unpack_rows()
    x_step(0, 2, 1)
    x_step(0, 3, 1)
    x_first(1, (0, 1, 2, 3))
    home_in(0)
    for c in s_y:
        c.wait_recv()
    lo, hi, opp = turn(y - 1), turn(y + 1), turn(y + 2)
    s_y2 = [
        cp.remote(sh.at[:, 0:2, lo, z], sh.at[:, 0:2, lo, z], at(0, 1)),
        cp.remote(sh.at[:, 2:4, hi, z], sh.at[:, 2:4, hi, z], at(0, -1)),
    ]
    s_z += [cp.remote(sh.at[:, :, v, z], sh.at[:, :, v, z], at(0, 0, 1)) for v in (lo, hi)]
    d_step(1)
    home_in(1)
    x_step(0, 0, 2)
    y_step(0, 0)
    home_in(2)
    x_step(0, 1, 2)
    y_step(0, 1)
    home_in(3)
    home_mid()
    x_step(0, 2, 2)
    y_step(0, 2)
    home_out(0)
    home_out(1)
    x_step(0, 3, 2)
    y_step(0, 3)
    d_step(2)
    dx_step(0)
    home_out(2)
    home_out(3)
    own2 = exchange(pack2, got2, groups)
    for c in s_y2:
        c.wait_recv()
    s_z.append(cp.remote(sh.at[:, :, opp, z], sh.at[:, :, opp, z], at(0, 0, 1)))
    x_step(1, 0, 0)
    x_step(1, 1, 0)
    spread_y(0)
    dx_step(1)
    x_step(1, 2, 0)
    x_step(1, 3, 0)
    dx_step(2)
    x_step(1, 0, 1)
    x_step(1, 1, 1)
    dx_step(3)
    d_z = [cp.remote(xd.at[r, 2], hd.at[y, r], at(0, 0, 1)) for r in (0, 1)]
    forward_y(0)
    x_step(1, 2, 1)
    x_step(1, 3, 1)
    for c in t_t[:1] + [t_fwd2] + s_z:
        c.wait_recv()
    d_y = []
    for r in (0, 1):
        d_z[r].wait_recv()
        choose(fz, xd.shape[2], 16, lambda i, r=r: xd[r, 2, i], hd.at[y, r])
        d_y.append([cp.remote(hd.at[y, r], hd.at[y, r], at(0, d)) for d in (1, -1)])
    shared_in(0)
    shared_in(1)
    x_step(1, 0, 2)
    y_step(1, 0)
    shared_in(2)
    shared_in(3)
    shared_mid()
    x_step(1, 1, 2)
    y_step(1, 1)
    d_y[0][0].wait_recv()
    d_y[1][1].wait_recv()
    d_y2 = [
        cp.remote(hd.at[lo, 0], hd.at[lo, 0], at(0, 1)),
        cp.remote(hd.at[hi, 1], hd.at[hi, 1], at(0, -1)),
    ]
    shared_out(0)
    shared_out(1)
    x_step(1, 2, 2)
    y_step(1, 2)
    shared_out(2)
    shared_out(3)
    x_step(1, 3, 2)
    y_step(1, 3)
    home_back()
    spread_y(1)
    hot_arrived(0)
    for k in range(4):
        hot_in(0, k)
    forward_y(1)
    for c in c_x:
        c.wait_recv()
    hot_arrived(1)
    for k in range(4):
        hot_in(1, k)
    d_y[0][1].wait_recv()
    d_y[1][0].wait_recv()
    for c in d_y2:
        c.wait_recv()
    for d in range(NX):
        a = slice(d * n, (d + 1) * n)
        hot_hid[a] = (
            silu(acc_g[a]) * acc_u[a] * as_col(coefs[d, 0:1])
        ).astype(bf)

    order = (2, 1, 3, 0)
    to_c = {}
    for d in order:
        for q in range(4):
            lanes = slice(q * quarter, (q + 1) * quarter)
            wd = hd[:, :, :, lanes].reshape(cols, quarter)
            psum[d, q] = psum[d, q] + dot(hot_hid[d * n : (d + 1) * n], wd)
        to_core[d, :, 0:quarter] = psum[d, 1 - core].astype(bf)
        to_core[d, :, quarter:] = psum[d, 3 - core].astype(bf)
        to_c[d] = cp.remote(to_core.at[d], from_core.at[d], other)
    to_x = []
    for d in order:
        to_c[d].wait_recv()
        if d:
            for i, q in enumerate((core, 2 + core)):
                lanes = slice(i * quarter, (i + 1) * quarter)
                mid[d - 1, :, lanes] = (psum[d, q] + from_core[d, :, lanes].astype(f32)).astype(bf)
            to_x.append(cp.remote(mid.at[d - 1], from_x.at[d - 1], at(d)))
    for c in to_x:
        c.wait_recv()

    def total(side):
        lanes = of_quarter(side)
        v = psum[0, 2 * side + core] + from_core[0, :, lanes].astype(f32)
        for i in range(3):
            v += from_x[i, :, lanes].astype(f32)
        return v

    half[...] = total(1 - z_hi).astype(bf)
    last = cp.remote(half, from_z, across)
    own_total = total(z_hi)
    last.wait_recv()
    out[...] = (mask[...].astype(f32) * (own_total + from_z[...].astype(f32))).astype(out.dtype)
    for c in cp.started:
        c.wait_send()
    exchanged(pack1, got1, 0, True)
    exchanged(pack2, got2, groups, True)


def local(
    tokens, slot, mask, hot_group, router_weight,
    exp_gate, exp_up, exp_down, sh_gate, sh_up, sh_down,
):
    bf, f32 = jnp.bfloat16, jnp.float32
    x, y, z = coords()
    hot = hot_group[0]
    hx, hy, hz = hot // (NY * NZ), (hot // NZ) % NY, hot % NZ
    scalars = jnp.stack(
        [(hx == x).astype(jnp.int32), (hy == y).astype(jnp.int32), (hz == z).astype(jnp.int32), hot]
    )
    n, quarter = tokens.shape
    d, h = exp_gate.shape[1:]
    rows, cols = d // NY, h // NX
    part = cols // (2 * NY)
    groups = NX * NY * NZ
    sh_own = jnp.stack([sh_gate, sh_up, sh_down.T])
    any_spec = pl.BlockSpec(memory_space=pl.ANY)
    vmem = pl.BlockSpec(memory_space=pltpu.VMEM)
    blocks = pltpu.VMEM((groups, 16, quarter), bf)
    return pl.pallas_call(
        layer_kernel,
        out_shape=jax.ShapeDtypeStruct((n, quarter), bf),
        in_specs=[pl.BlockSpec(memory_space=pltpu.SMEM), any_spec, vmem, vmem, vmem]
        + [any_spec] * 4,
        out_specs=vmem,
        scratch_shapes=[
            pltpu.VMEM((NY, rows, h), bf),
            pltpu.VMEM((NY, rows, h), bf),
            pltpu.VMEM((NX, NY, 2, part, d), bf),
            pltpu.VMEM((NY, 3, rows, cols), bf),
            pltpu.VMEM((NY, 3, rows, cols), bf),
            pltpu.VMEM((3, rows, cols), bf),
            pltpu.VMEM((3, rows, cols), bf),
            pltpu.VMEM((2, 3, NX, part, d), bf),
            pltpu.VMEM((2, 3, part, d), bf),
            pltpu.VMEM((d, cols), bf),
            pltpu.VMEM((d, cols), bf),
            pltpu.VMEM((NY, 2, part, d), bf),
            pltpu.VMEM((3, NX, NY, NZ, sh_own.shape[1], cols), bf),
            pltpu.VMEM((NX, n, d), bf),
            pltpu.VMEM((NX, 8, n), f32),
            blocks, blocks, blocks, blocks,
            pltpu.VMEM((n, d), bf),
            pltpu.VMEM((n, h), f32),
            pltpu.VMEM((n, h), f32),
            pltpu.VMEM((n, h), bf),
            pltpu.VMEM((NX * n, cols), f32),
            pltpu.VMEM((NX * n, cols), f32),
            pltpu.VMEM((NX * n, cols), bf),
            pltpu.VMEM((NX * n, cols), bf),
            pltpu.VMEM((NX, NT, n, quarter), f32),
            pltpu.VMEM((NX, n, 2 * quarter), bf),
            pltpu.VMEM((NX, n, 2 * quarter), bf),
            pltpu.VMEM((3, n, 2 * quarter), bf),
            pltpu.VMEM((3, n, 2 * quarter), bf),
            pltpu.VMEM((n, quarter), bf),
            pltpu.VMEM((n, quarter), bf),
            pltpu.VMEM((n, 128), f32),
            pltpu.VMEM((n, 128), f32),
            pltpu.SemaphoreType.DMA((140,)),
            pltpu.SemaphoreType.DMA((140,)),
            pltpu.SemaphoreType.DMA((16,)),
            pltpu.SemaphoreType.DMA((2 * groups,)),
            pltpu.SemaphoreType.DMA((2 * groups,)),
        ],
        compiler_params=pltpu.CompilerParams(
            collective_id=0, has_side_effects=True, vmem_limit_bytes=62 * 2**20
        ),
    )(
        scalars, tokens, slot, mask.reshape(n, 1), router_weight,
        exp_gate[0], exp_up[0], exp_down[0].reshape(NX, NY, 2, part, d), sh_own,
    )


def solution(mesh):
    in_specs = (
        P("expert", "tensor"),
        P("expert", None),
        P("expert"),
        P(),
        P(),
        P("expert", None, "tensor"),
        P("expert", None, "tensor"),
        P("expert", "tensor", None),
        P("expert", "tensor"),
        P("expert", "tensor"),
        P("tensor", "expert"),
    )
    out_specs = P("expert", "tensor")
    return jax.shard_map(local, mesh=mesh, in_specs=in_specs, out_specs=out_specs, check_vma=False)
```

```python
import jax
import jax.numpy as jnp
from jax import lax
from jax.experimental import pallas as pl
from jax.experimental.pallas import tpu as pltpu
from jax.sharding import PartitionSpec as P

MESH = pl.DeviceIdType.MESH
NX, NY, NZ, NT, CAP = 4, 4, 2, 4, 4

PARTS = ((0, 256), (256, 256), (512, 128))
SPLIT = 384
SENDS = 240
ORDER = (
    "tok0", "df", "own0", "tokx", "sx", "route", "pack", "wts", "tt", "s1", "d0", "xf00", "xf01",
    "xf03", "unpack", "x000", "hi0", "hi1", "x010", "hi2", "hi3", "x030", "hm", "tf", "ho0", "x001",
    "ho1", "ho2", "x011", "ho3", "s2", "ex2", "x031", "tq", "x002", "y00", "x012", "d1", "xf10",
    "xf02", "s3", "x032", "xf11", "x100", "x020", "x110", "y01", "x101", "x021", "x111", "x102",
    "y10", "xf12", "x022", "d2", "dx0", "x112", "y02", "si0", "x120", "si1", "y11", "si2", "dx1",
    "y03", "si3", "xf20", "sm", "x121", "so0", "so1", "dx2", "so2", "so3", "hb", "x122", "y12",
    "sy0", "xf13", "x200", "dx3", "dz0", "xf22", "xf21", "x130", "x201", "fy0", "x220", "x210",
    "dy1", "x131", "hot0", "x202", "y20", "x221", "x211", "dy2", "xf23", "x132", "y13", "x222",
    "x212", "y21", "x230", "y22", "x231", "sy1", "x232", "y23", "fy1", "sy2", "hot1", "fy2", "hot2",
    "end",
)


def coords():
    e = lax.axis_index("expert")
    return lax.div(e, NY * NZ), lax.rem(lax.div(e, NZ), NY), lax.rem(e, NZ)


def group_of(x, y, z):
    return (x * NY + y) * NZ + z


def turn(i, n=4):
    return lax.rem(i + 2 * n, n)


class Copies:
    def __init__(self, send, recv, local):
        self.send, self.recv, self.local = send, recv, local
        self.sent, self.kept = 0, 0
        self.started = []
        self.waited = set()

    def remote(self, src, dst, device):
        c = pltpu.make_async_remote_copy(
            src_ref=src,
            dst_ref=dst,
            send_sem=self.send.at[self.sent],
            recv_sem=self.recv.at[self.sent],
            device_id=device,
            device_id_type=MESH,
        )
        self.sent += 1
        c.start()
        self.started.append(c)
        return c

    def here(self, src, dst):
        c = pltpu.make_async_copy(src, dst, self.local.at[self.kept])
        self.kept += 1
        c.start()
        return c

    def once(self, c, remote):
        if id(c) not in self.waited:
            self.waited.add(id(c))
            if remote:
                c.wait_recv()
            else:
                c.wait()

    def got(self, *copies):
        for c in copies:
            self.once(c, True)

    def placed(self, *copies):
        for c in copies:
            self.once(c, False)


def choose(flag, rows, step, mine, into):
    def body(i, carry):
        at = pl.ds(pl.multiple_of(i * step, step), step)
        into[at] = jnp.where(flag == 1, mine(at), into[at])
        return carry

    lax.fori_loop(0, rows // step, body, 0)


def dot(a, b):
    return jnp.dot(a, b, preferred_element_type=jnp.float32)


def silu(v):
    return v / (1.0 + jnp.exp(-v))


def layer_kernel(
    scalars, tok, slot, router, gate, up, down, sh_gate, sh_up, sh_down,
    out,
    own_g, own_u, own_d, xg, xu, yg, yu, yd, xd, hg, hu, hd, sh, tk, coefs,
    pack1, got1, pack2, got2, rows_in, home_g, home_u, home_hid,
    acc_g, acc_u, sh_hid, hot_hid, psum, to_core, from_core, mid, from_x, half, from_z, from_zb, mid_b, from_xb,
    w_cols, target_cols, expert_cols,
    send, recv, local, a2a_send, a2a_recv,
):
    x, y, z = coords()
    e = lax.axis_index("expert")
    groups = lax.axis_size("expert")
    t = lax.axis_index("tensor")
    core, z_hi = lax.rem(t, 2), lax.div(t, 2)
    cp = Copies(send, recv, local)
    rows, cols = xg.shape[2], xg.shape[3]
    n, quarter = tok.shape
    bf, f32 = jnp.bfloat16, jnp.float32
    parts = PARTS

    def at(dx=0, dy=0, dz=0):
        return {"expert": group_of(turn(x + dx), turn(y + dy), turn(z + dz, 2)), "tensor": t}

    other_t = z_hi * 2 + (1 - core)
    across_t = (1 - z_hi) * 2 + core
    other = {"expert": e, "tensor": other_t}
    across = {"expert": e, "tensor": across_t}

    def of_quarter(i):
        return pl.ds(pl.multiple_of(i * quarter, quarter), quarter)

    barrier = pltpu.get_barrier_semaphore()

    def greet(k, carry):
        d = {"expert": lax.rem(e + k, groups), "tensor": t}
        pl.semaphore_signal(barrier, inc=1, device_id=d, device_id_type=MESH)
        return carry

    lax.fori_loop(1, groups, greet, 0)
    for d in (other, across):
        pl.semaphore_signal(barrier, inc=1, device_id=d, device_id_type=MESH)
    pl.semaphore_wait(barrier, groups + 1)
    fx, fy, fz, hot = scalars[0], scalars[1], scalars[2], scalars[3]

    streams = ((gate, own_g, xg, yg, hg, 1), (up, own_u, xu, yu, hu, -1))

    def block(sign, j):
        return turn(y - sign * (1 + j))

    x_copy, own_copy, y_copy, z_copy = {}, {}, {}, {}

    def x_first(h, js):
        off, r = parts[h]
        for j in js:
            for s, (w, _, xb, _, _, sign) in enumerate(streams):
                lanes = pl.ds(pl.multiple_of(turn(x - sign) * cols, cols), cols)
                src = w.at[pl.ds(pl.multiple_of(block(sign, j) * rows + off, 128), r), lanes]
                x_copy[h, s, j, 0] = cp.remote(src, xb.at[j, 0, pl.ds(off, r)], at(sign))

    def own_load(j):
        for s, (w, own, _, _, _, sign) in enumerate(streams):
            src = w.at[pl.ds(pl.multiple_of(block(sign, j) * rows, rows), rows), :]
            own_copy[s, j] = cp.here(src, own.at[j])

    def x_step(h, j, step):
        off, r = parts[h]
        for s, (_, own, xb, _, _, sign) in enumerate(streams):
            x_copy[h, s, j, step].wait_recv()
            cp.placed(own_copy[s, j])
            lanes = pl.ds(pl.multiple_of(turn(x - sign * (2 + step)) * cols, cols), cols)
            mine = own.at[j, pl.ds(off, r)]
            into = xb.at[j, step, pl.ds(off, r)]
            choose(fx, r, 128, lambda a, mine=mine, lanes=lanes: mine[a, lanes], into)
            if step < 2:
                nxt = xb.at[j, step + 1, pl.ds(off, r)]
                x_copy[h, s, j, step + 1] = cp.remote(into, nxt, at(sign))

    def y_step(h, j):
        off, r = parts[h]
        for s, (_, _, xb, yb, hb, sign) in enumerate(streams):
            mine = xb.at[j, 2, pl.ds(off, r)]
            if j == 0:
                y_copy[h, s, 0] = cp.remote(mine, yb.at[0, pl.ds(off, r)], at(0, sign))
                continue
            into = yb.at[j - 1, pl.ds(off, r)]
            y_copy[h, s, j - 1].wait_recv()
            choose(fy, r, 128, lambda a, mine=mine: mine[a], into)
            if j < 3:
                y_copy[h, s, j] = cp.remote(into, yb.at[j, pl.ds(off, r)], at(0, sign))
            else:
                z_copy[h, s] = cp.remote(into, hot_rows(hb, h, y), at(0, 0, 1))

    def hot_rows(ref, h, v):
        off, r = parts[h]
        return ref.at[pl.ds(pl.multiple_of(v * rows + off, 128), r)]

    near, far2 = {}, {}

    def spread_y(h):
        off, r = parts[h]
        for s, (_, _, _, yb, hb, sign) in enumerate(streams):
            into = hot_rows(hb, h, y)
            mine = yb.at[2, pl.ds(off, r)]
            z_copy[h, s].wait_recv()
            choose(fz, r, 128, lambda a, mine=mine: mine[a], into)
            near[h, s] = [cp.remote(into, into, at(0, d)) for d in (sign, -sign)]

    def forward_y(h):
        for s, (_, _, _, _, hb, sign) in enumerate(streams):
            near[h, s][0].wait_recv()
            a = hot_rows(hb, h, turn(y - sign))
            far2[h, s] = cp.remote(a, a, at(0, sign))

    def hot_arrived(h):
        for s in (0, 1):
            near[h, s][1].wait_recv()
            far2[h, s].wait_recv()

    d_copy, dx_copy = {}, {}

    def d_first():
        for r, sign in ((0, 1), (1, -1)):
            d_copy[r, 0] = cp.remote(down.at[:, turn(y - sign), r], yd.at[r, 0], at(0, sign))

    def d_step(step):
        for r, sign in ((0, 1), (1, -1)):
            d_copy[r, step].wait_recv()
            cp.placed(c_of["down"])
            yp = turn(y - sign * (2 + step))
            choose(fy, NX, 1, lambda i, yp=yp, r=r: own_d[i, yp, r], yd.at[r, step])
            if step < 2:
                d_copy[r, step + 1] = cp.remote(yd.at[r, step], yd.at[r, step + 1], at(0, sign))

    def dx_step(step):
        for r, sign in ((0, 1), (1, -1)):
            if step == 0:
                dx_copy[r, 0] = cp.remote(yd.at[r, 2, turn(x - sign)], xd.at[r, 0], at(sign))
                continue
            dx_copy[r, step - 1].wait_recv()
            xp = turn(x - sign * (1 + step))
            choose(
                fx, xd.shape[2], 16, lambda i, xp=xp, r=r: yd[r, 2, xp, i], xd.at[r, step - 1]
            )
            if step < 3:
                dx_copy[r, step] = cp.remote(xd.at[r, step - 1], xd.at[r, step], at(sign))

    def exchange(src, dst, base):
        def go(k, carry):
            to = lax.rem(e + k, groups)
            pltpu.make_async_remote_copy(
                src_ref=src.at[to], dst_ref=dst.at[e],
                send_sem=a2a_send.at[base + k], recv_sem=a2a_recv.at[base + k],
                device_id={"expert": to, "tensor": t}, device_id_type=MESH,
            ).start()
            return carry

        lax.fori_loop(1, groups, go, 0)
        return cp.here(src.at[e], dst.at[e])

    def exchanged(src, dst, base, sends):
        def done(k, carry):
            to = lax.rem(e + k, groups)
            frm = lax.rem(e + groups - k, groups)
            c = pltpu.make_async_remote_copy(
                src_ref=src.at[to], dst_ref=dst.at[frm],
                send_sem=a2a_send.at[base + k], recv_sem=a2a_recv.at[base + k],
                device_id={"expert": to, "tensor": t}, device_id_type=MESH,
            )
            if sends:
                c.wait_send()
            else:
                c.wait_recv()
            return carry

        lax.fori_loop(1, groups, done, 0)

    def iota(shape, dim):
        return lax.broadcasted_iota(jnp.int32, shape, dim)

    def as_row(col):
        eye = iota((n, n), 0) == iota((n, n), 1)
        return jnp.sum(jnp.where(eye, col, 0.0), axis=0, keepdims=True)

    def as_col(row):
        eye = iota((n, n), 0) == iota((n, n), 1)
        return jnp.sum(jnp.where(eye, row, 0.0), axis=1, keepdims=True)

    blocks_at_once = n // 16

    def packed(c, q, key):
        r = iota((n, n), 0) + c * n
        of = (r // 16) * 4 + r % 4
        return ((of.astype(f32) == key) & ((r // 4) % 4 == q)).astype(bf)

    def unpacked(q, key):
        r = iota((n, 4 * n), 1)
        of = (r // 16) * 4 + r % 4
        return ((of.astype(f32) == key) & ((r // 4) % 4 == q)).astype(bf)

    mine = of_quarter(t)
    theirs = of_quarter(across_t)
    c_of = {}

    def own_tokens():
        c_of["peer"] = [cp.remote(tok, tk.at[0, :, mine], d) for d in (other, across)]
        c_of["own"] = cp.here(tok, tk.at[0, :, mine])

    def quad_tokens():
        c_of["quad"] = [cp.remote(tok, tk.at[(4 - d) % 4, :, mine], at(d)) for d in (2, 1, -1)]

    def quad_across():
        cp.got(*c_of["quad"])
        a = tk.at[1:4, :, mine]
        c_of["quad_peer"] = [cp.remote(a, a, d) for d in (other, across)]

    def quad_relay():
        cp.got(c_of["quad_peer"][1])
        a = tk.at[1:4, :, theirs]
        c_of["quad_relay"] = cp.remote(a, a, other)

    def quad_done():
        cp.got(c_of["quad_peer"][0], c_of["quad_relay"])

    def own_loads():
        for j in range(4):
            own_load(j)
            if j == 0:
                c_of["down"] = cp.here(down, own_d)

    sh_refs = (sh_gate, sh_up, sh_down)

    def sh_piece(i, xp):
        return sh_refs[i].at[:, pl.ds(pl.multiple_of(xp * cols, cols), cols)]

    lo, hi, opp = turn(y - 1), turn(y + 1), turn(y + 2)

    def sh_x():
        c_of["sh_x"] = [
            cp.remote(sh_piece(i, turn(x + d)), sh.at[i, x, y, z], at(d))
            for d in (2, 1, -1)
            for i in range(3)
        ]
        c_of["sh_own"] = [cp.here(sh_piece(i, x), sh.at[i, x, y, z]) for i in range(3)]

    def sh_to(a, device):
        return cp.remote(a, a, device)

    def sh_1():
        cp.got(*c_of["sh_x"])
        cp.placed(*c_of["sh_own"])
        c_of["sh_y"] = [sh_to(sh.at[:, :, y, z], at(0, d)) for d in (1, -1)]
        c_of["sh_z"] = [sh_to(sh.at[:, :, y, z], at(0, 0, 1))]

    def sh_2():
        cp.got(*c_of["sh_y"])
        c_of["sh_y2"] = [
            sh_to(sh.at[:, 0:2, lo, z], at(0, 1)), sh_to(sh.at[:, 2:4, hi, z], at(0, -1))
        ]
        c_of["sh_z"] += [sh_to(sh.at[:, :, v, z], at(0, 0, 1)) for v in (lo, hi)]

    def sh_3():
        cp.got(*c_of["sh_y2"])
        c_of["sh_z"].append(sh_to(sh.at[:, :, opp, z], at(0, 0, 1)))

    def route():
        ids_row = slot[...].astype(f32)
        ids_f = as_col(ids_row)
        ids = ids_f.astype(jnp.int32)
        same = jnp.where((ids_f == ids_row) & (iota((n, n), 1) < iota((n, n), 0)), 1.0, 0.0)
        position = jnp.sum(same, axis=1, keepdims=True)
        spare = (ids & 1) == 1
        target = jnp.where(spare, -1.0, (ids >> 1).astype(f32) * CAP + position)
        target_cols[...] = jnp.broadcast_to(target, target_cols.shape)
        expert = jnp.where(spare, hot, ids >> 1)
        expert_cols[...] = jnp.broadcast_to(expert, expert_cols.shape)
        cp.placed(c_of["own"])
        cp.got(c_of["peer"][1])
        a = tk.at[0, :, theirs]
        c_of["relay"] = cp.remote(a, a, other)

    def pack():
        cp.got(c_of["peer"][0], c_of["relay"])
        target_row = as_row(target_cols[:, 0:1])
        for c in range(4):
            acc = jnp.zeros((n, quarter), f32)
            for q in range(4):
                acc += dot(packed(c, q, target_row), tk[0, :, q * quarter : (q + 1) * quarter])
            pack1[c * blocks_at_once : (c + 1) * blocks_at_once] = acc.astype(bf).reshape(
                blocks_at_once, 16, quarter
            )
        c_of["own1"] = exchange(pack1, got1, 0)

    def weights():
        logits = lax.dot_general(
            tk[0], router[...], (((1,), (1,)), ((), ())), preferred_element_type=f32
        )
        chosen = expert_cols[:, 0 : logits.shape[1]] == iota(logits.shape, 1)
        w = jax.nn.sigmoid(jnp.sum(jnp.where(chosen, logits, 0.0), axis=1, keepdims=True))
        w_cols[...] = jnp.broadcast_to(w, w_cols.shape)
        coef = jnp.where(target_cols[:, 0:1] < 0, w, 0.0)
        coefs[0] = jnp.broadcast_to(as_row(coef), coefs.shape[1:])
        c_of["coef"] = [cp.remote(coefs.at[0], coefs.at[(4 - d) % 4], at(d)) for d in (2, 1, -1)]

    def unpack_rows():
        exchanged(pack1, got1, 0, False)
        cp.placed(c_of["own1"])
        flat = got1[...].reshape(4 * n, quarter)
        key = iota((n, 1), 0).astype(f32)
        for q in range(4):
            rows_in[:, q * quarter : (q + 1) * quarter] = dot(unpacked(q, key), flat).astype(bf)

    def home_in(j):
        for acc, own, sign in ((home_g, own_g, 1), (home_u, own_u, -1)):
            cp.placed(own_copy[0 if sign == 1 else 1, j])
            a = rows_in[:, pl.ds(pl.multiple_of(block(sign, j) * rows, rows), rows)]
            v = dot(a, own[j])
            acc[...] = v if j == 0 else acc[...] + v

    def home_mid():
        home_hid[...] = (silu(home_g[...]) * home_u[...]).astype(bf)

    def home_out(q):
        cp.placed(c_of["down"])
        lanes = slice(q * quarter, (q + 1) * quarter)
        v = jnp.zeros((n, quarter), f32)
        for i in range(NX):
            wd = own_d[i, :, :, :, lanes].reshape(cols, quarter)
            v += dot(home_hid[:, i * cols : (i + 1) * cols], wd)
        acc_rows = v.astype(bf)
        row = iota((1, n), 1).astype(f32)
        for c in range(4):
            a = slice(c * blocks_at_once, (c + 1) * blocks_at_once)
            p = dot(packed(c, q, row), acc_rows).astype(bf).reshape(blocks_at_once, 16, quarter)
            pack2[a] = p if q == 0 else pack2[a] + p

    def home_back():
        exchanged(pack2, got2, groups, False)
        cp.placed(c_of["own2"])
        flat = got2[...].reshape(4 * n, quarter)
        key = target_cols[:, 0:1]
        for q in range(4):
            back = dot(unpacked(q, key), flat)
            psum[0, q] = psum[0, q] + w_cols[:, 0:1] * back

    def quad_in(lanes, w_gate, w_up, first):
        a = tk[:, :, lanes].reshape(NX * n, -1)
        for acc, wt in ((acc_g, w_gate), (acc_u, w_up)):
            v = dot(a, wt)
            acc[...] = v if first else acc[...] + v

    def shared_in(k):
        quad_in(
            slice(k * rows, (k + 1) * rows),
            sh[0, k].reshape(rows, cols), sh[1, k].reshape(rows, cols), k == 0,
        )

    def shared_mid():
        sh_hid[...] = (silu(acc_g[...]) * acc_u[...]).astype(bf)

    def shared_out(q):
        wt = sh[2, q].reshape(quarter, cols)
        v = lax.dot_general(
            sh_hid[...], wt, (((1,), (1,)), ((), ())), preferred_element_type=f32
        )
        psum[:, q] = v.reshape(NX, n, quarter)

    def hot_in(h, k):
        off, r = parts[h]
        lanes = slice(k * rows + off, k * rows + off + r)
        quad_in(lanes, hg[lanes], hu[lanes], h == 0 and k == 0)

    def send_back():
        c_of["own2"] = exchange(pack2, got2, groups)

    def shared_first():
        cp.got(*c_of["sh_z"])
        shared_in(0)

    d_z, d_y, d_y2 = [], [], []

    def d_z_send():
        d_z.extend(cp.remote(xd.at[r, 2], hd.at[y, r], at(0, 0, 1)) for r in (0, 1))

    def d_spread():
        for r in (0, 1):
            d_z[r].wait_recv()
            choose(fz, xd.shape[2], 16, lambda i, r=r: xd[r, 2, i], hd.at[y, r])
            d_y.append([cp.remote(hd.at[y, r], hd.at[y, r], at(0, d)) for d in (1, -1)])

    def d_forward():
        cp.got(d_y[0][0], d_y[1][1])
        d_y2.append(cp.remote(hd.at[lo, 0], hd.at[lo, 0], at(0, 1)))
        d_y2.append(cp.remote(hd.at[hi, 1], hd.at[hi, 1], at(0, -1)))

    def hot_part(h):
        hot_arrived(h)
        for k in range(4):
            hot_in(h, k)

    def end():
        cp.got(*c_of["coef"], d_y[0][1], d_y[1][0], *d_y2)

    tasks = {
        "tok0": own_tokens, "tokx": quad_tokens, "tt": quad_across, "tf": quad_relay,
        "tq": quad_done, "own0": own_loads, "df": d_first, "dz0": d_z_send, "dy1": d_spread,
        "dy2": d_forward, "sx": sh_x, "s1": sh_1, "s2": sh_2, "s3": sh_3, "route": route,
        "pack": pack, "wts": weights, "unpack": unpack_rows, "hm": home_mid, "ex2": send_back,
        "si0": shared_first, "sm": shared_mid, "hb": home_back, "end": end,
    }
    for name in ORDER:
        if name in tasks:
            tasks[name]()
            continue
        kind, at_ = name.rstrip("0123456789"), [int(c) for c in name.lstrip("abcdefghijklmnopqrstuvwxyz")]
        if kind == "xf":
            x_first(at_[0], at_[1:])
        else:
            {
                "x": x_step, "y": y_step, "sy": spread_y, "fy": forward_y, "hot": hot_part,
                "d": d_step, "dx": dx_step, "hi": home_in, "ho": home_out,
                "si": shared_in, "so": shared_out,
            }[kind](*at_)

    first, rest = slice(0, SPLIT), slice(SPLIT, quarter)
    to_c, by_x, by_z = {}, [], {}
    order = (2, 1, 3, 0)
    for d in order:
        a = slice(d * n, (d + 1) * n)
        hot_hid[a] = (silu(acc_g[a]) * acc_u[a] * as_col(coefs[d, 0:1])).astype(bf)
        for q in range(4):
            lanes = slice(q * quarter, (q + 1) * quarter)
            wd = hd[:, :, :, lanes].reshape(cols, quarter)
            psum[d, q] = psum[d, q] + dot(hot_hid[a], wd)
        to_core[d, 0] = psum[d, 1 - core].astype(bf)
        to_core[d, 1] = psum[d, 3 - core].astype(bf)
        to_c[d] = cp.remote(to_core.at[d], from_core.at[d], other)

    def on_chip(d, side, lanes):
        return psum[d, 2 * side + core, :, lanes] + from_core[d, side, :, lanes].astype(f32)

    for d in order:
        to_c[d].wait_recv()
        if d:
            for side in (0, 1):
                mid[d, side, :, first] = on_chip(d, side, first).astype(bf)
            by_x.append(cp.remote(mid.at[d, :, :, first], from_x.at[d - 1], at(d)))
        mid[d, 1 - z_hi, :, rest] = on_chip(d, 1 - z_hi, rest).astype(bf)
        by_z[d] = cp.remote(mid.at[d, 1 - z_hi, :, rest], from_zb.at[d], across)
    by_xb = []
    for d in order[:3]:
        by_z[d].wait_recv()
        mid_b[d - 1] = (on_chip(d, z_hi, rest) + from_zb[d].astype(f32)).astype(bf)
        by_xb.append(cp.remote(mid_b.at[d - 1], from_xb.at[d - 1], at(d)))
    for c in by_x:
        c.wait_recv()

    def total(side):
        v = on_chip(0, side, first)
        for i in range(3):
            v += from_x[i, side].astype(f32)
        return v

    half[...] = total(1 - z_hi).astype(bf)
    last = cp.remote(half, from_z, across)
    own_total = total(z_hi)
    by_z[0].wait_recv()
    v = on_chip(0, z_hi, rest) + from_zb[0].astype(f32)
    for c in by_xb:
        c.wait_recv()
    for i in range(3):
        v += from_xb[i].astype(f32)
    out[:, rest] = v
    last.wait_recv()
    out[:, first] = own_total + from_z[...].astype(f32)
    for c in cp.started:
        c.wait_send()
    exchanged(pack1, got1, 0, True)
    exchanged(pack2, got2, groups, True)


def local(
    tokens, slot, mask, hot_group, router_weight,
    exp_gate, exp_up, exp_down, sh_gate, sh_up, sh_down,
):
    bf, f32 = jnp.bfloat16, jnp.float32
    x, y, z = coords()
    hot = hot_group[0]
    hx, hy, hz = hot // (NY * NZ), (hot // NZ) % NY, hot % NZ
    scalars = jnp.stack(
        [(hx == x).astype(jnp.int32), (hy == y).astype(jnp.int32), (hz == z).astype(jnp.int32), hot]
    )
    n, quarter = tokens.shape
    d, h = exp_gate.shape[1:]
    rows, cols = d // NY, h // NX
    part = cols // (2 * NY)
    groups = NX * NY * NZ
    any_spec = pl.BlockSpec(memory_space=pl.ANY)
    vmem = pl.BlockSpec(memory_space=pltpu.VMEM)
    blocks = pltpu.VMEM((groups, 16, quarter), bf)
    summed = pl.pallas_call(
        layer_kernel,
        out_shape=jax.ShapeDtypeStruct((n, quarter), f32),
        in_specs=[pl.BlockSpec(memory_space=pltpu.SMEM), any_spec, vmem, vmem] + [any_spec] * 6,
        out_specs=vmem,
        scratch_shapes=[
            pltpu.VMEM((NY, rows, h), bf),
            pltpu.VMEM((NY, rows, h), bf),
            pltpu.VMEM((NX, NY, 2, part, d), bf),
            pltpu.VMEM((NY, 3, rows, cols), bf),
            pltpu.VMEM((NY, 3, rows, cols), bf),
            pltpu.VMEM((3, rows, cols), bf),
            pltpu.VMEM((3, rows, cols), bf),
            pltpu.VMEM((2, 3, NX, part, d), bf),
            pltpu.VMEM((2, 3, part, d), bf),
            pltpu.VMEM((d, cols), bf),
            pltpu.VMEM((d, cols), bf),
            pltpu.VMEM((NY, 2, part, d), bf),
            pltpu.VMEM((3, NX, NY, NZ, sh_gate.shape[0], cols), bf),
            pltpu.VMEM((NX, n, d), bf),
            pltpu.VMEM((NX, 8, n), f32),
            blocks, blocks, blocks, blocks,
            pltpu.VMEM((n, d), bf),
            pltpu.VMEM((n, h), f32),
            pltpu.VMEM((n, h), f32),
            pltpu.VMEM((n, h), bf),
            pltpu.VMEM((NX * n, cols), f32),
            pltpu.VMEM((NX * n, cols), f32),
            pltpu.VMEM((NX * n, cols), bf),
            pltpu.VMEM((NX * n, cols), bf),
            pltpu.VMEM((NX, NT, n, quarter), f32),
            pltpu.VMEM((NX, 2, n, quarter), bf),
            pltpu.VMEM((NX, 2, n, quarter), bf),
            pltpu.VMEM((NX, 2, n, quarter), bf),
            pltpu.VMEM((3, 2, n, SPLIT), bf),
            pltpu.VMEM((n, SPLIT), bf),
            pltpu.VMEM((n, SPLIT), bf),
            pltpu.VMEM((NX, n, quarter - SPLIT), bf),
            pltpu.VMEM((3, n, quarter - SPLIT), bf),
            pltpu.VMEM((3, n, quarter - SPLIT), bf),
            pltpu.VMEM((n, 128), f32),
            pltpu.VMEM((n, 128), f32),
            pltpu.VMEM((n, 128), jnp.int32),
            pltpu.SemaphoreType.DMA((SENDS,)),
            pltpu.SemaphoreType.DMA((SENDS,)),
            pltpu.SemaphoreType.DMA((16,)),
            pltpu.SemaphoreType.DMA((2 * groups,)),
            pltpu.SemaphoreType.DMA((2 * groups,)),
        ],
        compiler_params=pltpu.CompilerParams(
            collective_id=0, has_side_effects=True, vmem_limit_bytes=62 * 2**20
        ),
    )(
        scalars, tokens, slot.reshape(1, n), router_weight.T,
        exp_gate[0], exp_up[0], exp_down[0].reshape(NX, NY, 2, part, d), sh_gate, sh_up, sh_down.T,
    )
    return (mask.astype(f32)[:, None] * summed).astype(bf)


def solution(mesh):
    in_specs = (
        P("expert", "tensor"),
        P("expert", None),
        P("expert"),
        P(),
        P(),
        P("expert", None, "tensor"),
        P("expert", None, "tensor"),
        P("expert", "tensor", None),
        P("expert", "tensor"),
        P("expert", "tensor"),
        P("tensor", "expert"),
    )
    out_specs = P("expert", "tensor")
    return jax.shard_map(local, mesh=mesh, in_specs=in_specs, out_specs=out_specs, check_vma=False)
```

```python
import jax
import jax.numpy as jnp
from jax import lax
from jax.experimental import pallas as pl
from jax.experimental.pallas import tpu as pltpu
from jax.sharding import PartitionSpec as P

MESH = pl.DeviceIdType.MESH
NX, NY, NZ, NT, CAP = 4, 4, 2, 4, 4

PARTS = ((0, 384), (384, 128), (512, 128))
SPLIT = 384
SENDS = 240
ORDER = (
    "tok0", "df", "tokx", "own0", "own1t", "pack", "sx", "route", "wts", "tt", "xf00", "xf01", "s1",
    "d0", "unpack", "x000", "tf", "xf02", "x010", "tq", "x001", "s2", "x020", "rf", "x011", "hi0",
    "hi1", "hi2", "hi3", "d1", "x002", "y00", "x021", "hm", "ho0", "ho1", "s3", "xf03", "ho2",
    "x012", "ho3", "hr1", "xf10", "x022", "xf20", "hr2", "xf11", "xf21", "x030", "x100", "x200",
    "x110", "d2", "dx0", "x210", "y01", "si0", "x031", "x101", "si1", "si2", "si3", "y02", "x201",
    "x111", "sm", "so0", "x211", "so1", "so2", "so3", "x032", "y03", "x102", "y10", "dx1", "ex2",
    "x202", "y20", "x212", "x112", "y11", "xf12", "xf22", "dx2", "y21", "sy0", "x120", "x220", "hb",
    "xf13", "xf23", "dx3", "dz0", "fy0", "x121", "x221", "x130", "x230", "x122", "y12", "x222",
    "y22", "dy1", "x131", "hot0", "x231", "x132", "y13", "dy2", "x232", "y23", "sy1", "sy2", "fy1",
    "fy2", "hot1", "hot2", "end",
)


def coords():
    e = lax.axis_index("expert")
    return lax.div(e, NY * NZ), lax.rem(lax.div(e, NZ), NY), lax.rem(e, NZ)


def group_of(x, y, z):
    return (x * NY + y) * NZ + z


def turn(i, n=4):
    return lax.rem(i + 2 * n, n)


class Copies:
    def __init__(self, send, recv, local):
        self.send, self.recv, self.local = send, recv, local
        self.sent, self.kept = 0, 0
        self.started = []
        self.waited = set()

    def remote(self, src, dst, device):
        c = pltpu.make_async_remote_copy(
            src_ref=src,
            dst_ref=dst,
            send_sem=self.send.at[self.sent],
            recv_sem=self.recv.at[self.sent],
            device_id=device,
            device_id_type=MESH,
        )
        self.sent += 1
        c.start()
        self.started.append(c)
        return c

    def here(self, src, dst):
        c = pltpu.make_async_copy(src, dst, self.local.at[self.kept])
        self.kept += 1
        c.start()
        return c

    def once(self, c, remote):
        if id(c) not in self.waited:
            self.waited.add(id(c))
            if remote:
                c.wait_recv()
            else:
                c.wait()

    def got(self, *copies):
        for c in copies:
            self.once(c, True)

    def placed(self, *copies):
        for c in copies:
            self.once(c, False)


def choose(flag, rows, step, mine, into):
    def body(i, carry):
        at = pl.ds(pl.multiple_of(i * step, step), step)
        into[at] = jnp.where(flag == 1, mine(at), into[at])
        return carry

    lax.fori_loop(0, rows // step, body, 0)


def dot(a, b):
    return jnp.dot(a, b, preferred_element_type=jnp.float32)


def silu(v):
    return v / (1.0 + jnp.exp(-v))


def layer_kernel(
    scalars, tok, slot, router, gate, up, down, sh_gate, sh_up, sh_down,
    out,
    own_g, own_u, own_d, xg, xu, yg, yu, yd, xd, hg, hu, hd, sh, tk, coefs,
    pack1, got1, pack2, got2, rows_in, home_g, home_u, home_hid,
    acc_g, acc_u, sh_hid, hot_hid, psum, to_core, from_core, mid, from_x, half, from_z, from_zb, mid_b, from_xb,
    w_cols, target_cols, expert_cols,
    tok_here, home_part, home_send, home_core, home_half, home_z, back,
    send, recv, local, a2a_send, a2a_recv,
):
    x, y, z = coords()
    e = lax.axis_index("expert")
    groups = lax.axis_size("expert")
    t = lax.axis_index("tensor")
    core, z_hi = lax.rem(t, 2), lax.div(t, 2)
    cp = Copies(send, recv, local)
    rows, cols = xg.shape[2], xg.shape[3]
    n, quarter = tok.shape
    bf, f32 = jnp.bfloat16, jnp.float32
    parts = PARTS

    def at(dx=0, dy=0, dz=0):
        return {"expert": group_of(turn(x + dx), turn(y + dy), turn(z + dz, 2)), "tensor": t}

    other_t = z_hi * 2 + (1 - core)
    across_t = (1 - z_hi) * 2 + core
    other = {"expert": e, "tensor": other_t}
    across = {"expert": e, "tensor": across_t}

    def of_quarter(i):
        return pl.ds(pl.multiple_of(i * quarter, quarter), quarter)

    barrier = pltpu.get_barrier_semaphore()

    def greet(k, carry):
        d = {"expert": lax.rem(e + k, groups), "tensor": t}
        pl.semaphore_signal(barrier, inc=1, device_id=d, device_id_type=MESH)
        return carry

    lax.fori_loop(1, groups, greet, 0)
    for d in (other, across):
        pl.semaphore_signal(barrier, inc=1, device_id=d, device_id_type=MESH)
    pl.semaphore_wait(barrier, groups + 1)
    fx, fy, fz, hot = scalars[0], scalars[1], scalars[2], scalars[3]

    streams = ((gate, own_g, xg, yg, hg, 1), (up, own_u, xu, yu, hu, -1))

    def block(sign, j):
        return turn(y - sign * (1 + j))

    x_copy, own_copy, y_copy, z_copy = {}, {}, {}, {}

    def x_first(h, js):
        off, r = parts[h]
        for j in js:
            for s, (w, _, xb, _, _, sign) in enumerate(streams):
                lanes = pl.ds(pl.multiple_of(turn(x - sign) * cols, cols), cols)
                src = w.at[pl.ds(pl.multiple_of(block(sign, j) * rows + off, 128), r), lanes]
                x_copy[h, s, j, 0] = cp.remote(src, xb.at[j, 0, pl.ds(off, r)], at(sign))

    def own_load(j):
        for s, (w, own, _, _, _, sign) in enumerate(streams):
            src = w.at[pl.ds(pl.multiple_of(block(sign, j) * rows, rows), rows), :]
            own_copy[s, j] = cp.here(src, own.at[j])

    def x_step(h, j, step):
        off, r = parts[h]
        for s, (_, own, xb, _, _, sign) in enumerate(streams):
            x_copy[h, s, j, step].wait_recv()
            cp.placed(own_copy[s, j])
            lanes = pl.ds(pl.multiple_of(turn(x - sign * (2 + step)) * cols, cols), cols)
            mine = own.at[j, pl.ds(off, r)]
            into = xb.at[j, step, pl.ds(off, r)]
            choose(fx, r, 128, lambda a, mine=mine, lanes=lanes: mine[a, lanes], into)
            if step < 2:
                nxt = xb.at[j, step + 1, pl.ds(off, r)]
                x_copy[h, s, j, step + 1] = cp.remote(into, nxt, at(sign))

    def y_step(h, j):
        off, r = parts[h]
        for s, (_, _, xb, yb, hb, sign) in enumerate(streams):
            mine = xb.at[j, 2, pl.ds(off, r)]
            if j == 0:
                y_copy[h, s, 0] = cp.remote(mine, yb.at[0, pl.ds(off, r)], at(0, sign))
                continue
            into = yb.at[j - 1, pl.ds(off, r)]
            y_copy[h, s, j - 1].wait_recv()
            choose(fy, r, 128, lambda a, mine=mine: mine[a], into)
            if j < 3:
                y_copy[h, s, j] = cp.remote(into, yb.at[j, pl.ds(off, r)], at(0, sign))
            else:
                z_copy[h, s] = cp.remote(into, hot_rows(hb, h, y), at(0, 0, 1))

    def hot_rows(ref, h, v):
        off, r = parts[h]
        return ref.at[pl.ds(pl.multiple_of(v * rows + off, 128), r)]

    near, far2 = {}, {}

    def spread_y(h):
        off, r = parts[h]
        for s, (_, _, _, yb, hb, sign) in enumerate(streams):
            into = hot_rows(hb, h, y)
            mine = yb.at[2, pl.ds(off, r)]
            z_copy[h, s].wait_recv()
            choose(fz, r, 128, lambda a, mine=mine: mine[a], into)
            near[h, s] = [cp.remote(into, into, at(0, d)) for d in (sign, -sign)]

    def forward_y(h):
        for s, (_, _, _, _, hb, sign) in enumerate(streams):
            near[h, s][0].wait_recv()
            a = hot_rows(hb, h, turn(y - sign))
            far2[h, s] = cp.remote(a, a, at(0, sign))

    def hot_arrived(h):
        for s in (0, 1):
            near[h, s][1].wait_recv()
            far2[h, s].wait_recv()

    d_copy, dx_copy = {}, {}

    def d_first():
        for r, sign in ((0, 1), (1, -1)):
            d_copy[r, 0] = cp.remote(down.at[:, turn(y - sign), r], yd.at[r, 0], at(0, sign))

    def d_step(step):
        for r, sign in ((0, 1), (1, -1)):
            d_copy[r, step].wait_recv()
            cp.placed(c_of["down"])
            yp = turn(y - sign * (2 + step))
            choose(fy, NX, 1, lambda i, yp=yp, r=r: own_d[i, yp, r], yd.at[r, step])
            if step < 2:
                d_copy[r, step + 1] = cp.remote(yd.at[r, step], yd.at[r, step + 1], at(0, sign))

    def dx_step(step):
        for r, sign in ((0, 1), (1, -1)):
            if step == 0:
                dx_copy[r, 0] = cp.remote(yd.at[r, 2, turn(x - sign)], xd.at[r, 0], at(sign))
                continue
            dx_copy[r, step - 1].wait_recv()
            xp = turn(x - sign * (1 + step))
            choose(
                fx, xd.shape[2], 16, lambda i, xp=xp, r=r: yd[r, 2, xp, i], xd.at[r, step - 1]
            )
            if step < 3:
                dx_copy[r, step] = cp.remote(xd.at[r, step - 1], xd.at[r, step], at(sign))

    def exchange(src, dst, base):
        def go(k, carry):
            to = lax.rem(e + k, groups)
            pltpu.make_async_remote_copy(
                src_ref=src.at[to], dst_ref=dst.at[e],
                send_sem=a2a_send.at[base + k], recv_sem=a2a_recv.at[base + k],
                device_id={"expert": to, "tensor": t}, device_id_type=MESH,
            ).start()
            return carry

        lax.fori_loop(1, groups, go, 0)
        return cp.here(src.at[e], dst.at[e])

    def exchanged(src, dst, base, sends):
        def done(k, carry):
            to = lax.rem(e + k, groups)
            frm = lax.rem(e + groups - k, groups)
            c = pltpu.make_async_remote_copy(
                src_ref=src.at[to], dst_ref=dst.at[frm],
                send_sem=a2a_send.at[base + k], recv_sem=a2a_recv.at[base + k],
                device_id={"expert": to, "tensor": t}, device_id_type=MESH,
            )
            if sends:
                c.wait_send()
            else:
                c.wait_recv()
            return carry

        lax.fori_loop(1, groups, done, 0)

    def iota(shape, dim):
        return lax.broadcasted_iota(jnp.int32, shape, dim)

    def as_row(col):
        eye = iota((n, n), 0) == iota((n, n), 1)
        return jnp.sum(jnp.where(eye, col, 0.0), axis=0, keepdims=True)

    def as_col(row):
        eye = iota((n, n), 0) == iota((n, n), 1)
        return jnp.sum(jnp.where(eye, row, 0.0), axis=1, keepdims=True)

    groups_here = NX * NY * NZ

    depth = pack1.shape[1]
    tiles = quarter // 128

    def packed(c, i, key):
        r = iota((n, n), 0) + c * n
        of = (r // depth) * CAP + r % CAP
        return ((of.astype(f32) == key) & ((r % depth) // CAP == i)).astype(bf)

    def pack_into(into, v, key):
        for c in range(groups_here * depth // n):
            acc = jnp.zeros((n, 128), f32)
            for i in range(tiles):
                acc += dot(packed(c, i, key), v[:, i * 128 : (i + 1) * 128])
            into[c * n // depth : (c + 1) * n // depth] = acc.astype(bf).reshape(
                n // depth, depth, 128
            )

    def unpacked(flat, i, key):
        r = iota((n, groups_here * depth), 1)
        of = (r // depth) * CAP + r % CAP
        pick = ((of.astype(f32) == key) & ((r % depth) // CAP == i)).astype(bf)
        return dot(pick, flat)

    mine = of_quarter(t)
    theirs = of_quarter(across_t)
    c_of = {}

    def own_tokens():
        c_of["peer"] = [cp.remote(tok, tk.at[0, :, mine], d) for d in (other, across)]
        c_of["own"] = cp.here(tok, tk.at[0, :, mine])
        c_of["here"] = cp.here(tok, tok_here)

    def quad_tokens():
        c_of["quad"] = [cp.remote(tok, tk.at[(4 - d) % 4, :, mine], at(d)) for d in (2, 1, -1)]

    def quad_across():
        cp.got(*c_of["quad"])
        a = tk.at[1:4, :, mine]
        c_of["quad_peer"] = [cp.remote(a, a, d) for d in (other, across)]

    def quad_relay():
        cp.got(c_of["quad_peer"][1])
        a = tk.at[1:4, :, theirs]
        c_of["quad_relay"] = cp.remote(a, a, other)

    def quad_done():
        cp.got(c_of["quad_peer"][0], c_of["quad_relay"])

    def own_loads():
        for j in range(4):
            own_load(j)
            if j == 0:
                c_of["down"] = cp.here(down, own_d)

    sh_refs = (sh_gate, sh_up, sh_down)

    def sh_piece(i, xp):
        return sh_refs[i].at[:, pl.ds(pl.multiple_of(xp * cols, cols), cols)]

    lo, hi, opp = turn(y - 1), turn(y + 1), turn(y + 2)

    def sh_x():
        c_of["sh_x"] = [
            cp.remote(sh_piece(i, turn(x + d)), sh.at[i, x, y, z], at(d))
            for d in (2, 1, -1)
            for i in range(3)
        ]
        c_of["sh_own"] = [cp.here(sh_piece(i, x), sh.at[i, x, y, z]) for i in range(3)]

    def sh_to(a, device):
        return cp.remote(a, a, device)

    def sh_1():
        cp.got(*c_of["sh_x"])
        cp.placed(*c_of["sh_own"])
        c_of["sh_y"] = [sh_to(sh.at[:, :, y, z], at(0, d)) for d in (1, -1)]
        c_of["sh_z"] = [sh_to(sh.at[:, :, y, z], at(0, 0, 1))]

    def sh_2():
        cp.got(*c_of["sh_y"])
        c_of["sh_y2"] = [
            sh_to(sh.at[:, 0:2, lo, z], at(0, 1)), sh_to(sh.at[:, 2:4, hi, z], at(0, -1))
        ]
        c_of["sh_z"] += [sh_to(sh.at[:, :, v, z], at(0, 0, 1)) for v in (lo, hi)]

    def sh_3():
        cp.got(*c_of["sh_y2"])
        c_of["sh_z"].append(sh_to(sh.at[:, :, opp, z], at(0, 0, 1)))

    def positions():
        cp.placed(c_of["here"])
        ids_row = slot[...].astype(f32)
        ids_f = as_col(ids_row)
        ids = ids_f.astype(jnp.int32)
        same = jnp.where((ids_f == ids_row) & (iota((n, n), 1) < iota((n, n), 0)), 1.0, 0.0)
        position = jnp.sum(same, axis=1, keepdims=True)
        spare = (ids & 1) == 1
        target = jnp.where(spare, -1.0, (ids >> 1).astype(f32) * CAP + position)
        target_cols[...] = jnp.broadcast_to(target, target_cols.shape)
        expert = jnp.where(spare, hot, ids >> 1)
        expert_cols[...] = jnp.broadcast_to(expert, expert_cols.shape)

    def relay():
        cp.placed(c_of["own"])
        cp.got(c_of["peer"][1])
        a = tk.at[0, :, theirs]
        c_of["relay"] = cp.remote(a, a, other)

    def pack():
        pack_into(pack1, tok_here, as_row(target_cols[:, 0:1]))
        c_of["own1"] = exchange(pack1, got1, 0)

    def weights():
        cp.got(c_of["peer"][0], c_of["relay"])
        logits = lax.dot_general(
            tk[0], router[...], (((1,), (1,)), ((), ())), preferred_element_type=f32
        )
        chosen = expert_cols[:, 0 : logits.shape[1]] == iota(logits.shape, 1)
        w = jax.nn.sigmoid(jnp.sum(jnp.where(chosen, logits, 0.0), axis=1, keepdims=True))
        w_cols[...] = jnp.broadcast_to(w, w_cols.shape)
        coef = jnp.where(target_cols[:, 0:1] < 0, w, 0.0)
        coefs[0] = jnp.broadcast_to(as_row(coef), coefs.shape[1:])
        c_of["coef"] = [cp.remote(coefs.at[0], coefs.at[(4 - d) % 4], at(d)) for d in (2, 1, -1)]

    def unpack_rows():
        exchanged(pack1, got1, 0, False)
        cp.placed(c_of["own1"])
        flat = got1[...].reshape(groups_here * depth, 128)
        key = iota((n, 1), 0).astype(f32)
        for i in range(tiles):
            lanes = pl.ds(pl.multiple_of(t * quarter + i * 128, 128), 128)
            rows_in[:, lanes] = unpacked(flat, i, key).astype(bf)
        a = rows_in.at[:, mine]
        c_of["rows"] = [cp.remote(a, a, d) for d in (other, across)]

    def rows_relay():
        cp.got(c_of["rows"][1])
        a = rows_in.at[:, theirs]
        c_of["rows_relay"] = cp.remote(a, a, other)

    def home_in(j):
        if j == 0:
            cp.got(c_of["rows"][0], c_of["rows_relay"])
        for acc, own, sign in ((home_g, own_g, 1), (home_u, own_u, -1)):
            cp.placed(own_copy[0 if sign == 1 else 1, j])
            a = rows_in[:, pl.ds(pl.multiple_of(block(sign, j) * rows, rows), rows)]
            v = dot(a, own[j])
            acc[...] = v if j == 0 else acc[...] + v

    def home_mid():
        home_hid[...] = (silu(home_g[...]) * home_u[...]).astype(bf)

    def home_out(q):
        cp.placed(c_of["down"])
        lanes = slice(q * quarter, (q + 1) * quarter)
        v = jnp.zeros((n, quarter), f32)
        for i in range(NX):
            wd = own_d[i, :, :, :, lanes].reshape(cols, quarter)
            v += dot(home_hid[:, i * cols : (i + 1) * cols], wd)
        home_part[q] = v

    def home_sum_core():
        for side in (0, 1):
            home_send[side] = home_part[2 * side + 1 - core].astype(bf)
        c_of["home_core"] = cp.remote(home_send, home_core, other)

    def home_sum_across():
        cp.got(c_of["home_core"])
        v = home_part[2 * (1 - z_hi) + core] + home_core[1 - z_hi].astype(f32)
        home_half[...] = v.astype(bf)
        c_of["home_z"] = cp.remote(home_half, home_z, across)

    def send_back():
        cp.got(c_of["home_z"])
        v = home_part[2 * z_hi + core] + home_core[z_hi].astype(f32) + home_z[...].astype(f32)
        row = iota((1, n), 1).astype(f32)
        pack_into(pack2, v.astype(bf), row)
        c_of["own2"] = exchange(pack2, got2, groups)

    def home_back():
        exchanged(pack2, got2, groups, False)
        cp.placed(c_of["own2"])
        flat = got2[...].reshape(groups_here * depth, 128)
        key = target_cols[:, 0:1]
        for i in range(tiles):
            lanes = slice(i * 128, (i + 1) * 128)
            back[:, lanes] = w_cols[:, 0:1] * unpacked(flat, i, key)

    def quad_in(lanes, w_gate, w_up, first):
        a = tk[:, :, lanes].reshape(NX * n, -1)
        for acc, wt in ((acc_g, w_gate), (acc_u, w_up)):
            v = dot(a, wt)
            acc[...] = v if first else acc[...] + v

    def shared_in(k):
        quad_in(
            slice(k * rows, (k + 1) * rows),
            sh[0, k].reshape(rows, cols), sh[1, k].reshape(rows, cols), k == 0,
        )

    def shared_mid():
        sh_hid[...] = (silu(acc_g[...]) * acc_u[...]).astype(bf)

    def shared_out(q):
        wt = sh[2, q].reshape(quarter, cols)
        v = lax.dot_general(
            sh_hid[...], wt, (((1,), (1,)), ((), ())), preferred_element_type=f32
        )
        psum[:, q] = v.reshape(NX, n, quarter)

    def hot_in(h, k):
        off, r = parts[h]
        lanes = slice(k * rows + off, k * rows + off + r)
        quad_in(lanes, hg[lanes], hu[lanes], h == 0 and k == 0)

    def shared_first():
        cp.got(*c_of["sh_z"])
        shared_in(0)

    d_z, d_y, d_y2 = [], [], []

    def d_z_send():
        d_z.extend(cp.remote(xd.at[r, 2], hd.at[y, r], at(0, 0, 1)) for r in (0, 1))

    def d_spread():
        for r in (0, 1):
            d_z[r].wait_recv()
            choose(fz, xd.shape[2], 16, lambda i, r=r: xd[r, 2, i], hd.at[y, r])
            d_y.append([cp.remote(hd.at[y, r], hd.at[y, r], at(0, d)) for d in (1, -1)])

    def d_forward():
        cp.got(d_y[0][0], d_y[1][1])
        d_y2.append(cp.remote(hd.at[lo, 0], hd.at[lo, 0], at(0, 1)))
        d_y2.append(cp.remote(hd.at[hi, 1], hd.at[hi, 1], at(0, -1)))

    def hot_part(h):
        hot_arrived(h)
        for k in range(4):
            hot_in(h, k)

    def end():
        cp.got(*c_of["coef"], d_y[0][1], d_y[1][0], *d_y2)

    tasks = {
        "tok0": own_tokens, "tokx": quad_tokens, "tt": quad_across, "tf": quad_relay,
        "tq": quad_done, "own0": own_loads, "df": d_first, "dz0": d_z_send, "dy1": d_spread,
        "dy2": d_forward, "sx": sh_x, "s1": sh_1, "s2": sh_2, "s3": sh_3, "own1t": positions, "route": relay, "rf": rows_relay, "hr1": home_sum_core,
        "hr2": home_sum_across,
        "pack": pack, "wts": weights, "unpack": unpack_rows, "hm": home_mid, "ex2": send_back,
        "si0": shared_first, "sm": shared_mid, "hb": home_back, "end": end,
    }
    for name in ORDER:
        if name in tasks:
            tasks[name]()
            continue
        kind, at_ = name.rstrip("0123456789"), [int(c) for c in name.lstrip("abcdefghijklmnopqrstuvwxyz")]
        if kind == "xf":
            x_first(at_[0], at_[1:])
        else:
            {
                "x": x_step, "y": y_step, "sy": spread_y, "fy": forward_y, "hot": hot_part,
                "d": d_step, "dx": dx_step, "hi": home_in, "ho": home_out,
                "si": shared_in, "so": shared_out,
            }[kind](*at_)

    first, rest = slice(0, SPLIT), slice(SPLIT, quarter)
    to_c, by_x, by_z = {}, [], {}
    order = (2, 1, 3, 0)
    for d in order:
        a = slice(d * n, (d + 1) * n)
        hot_hid[a] = (silu(acc_g[a]) * acc_u[a] * as_col(coefs[d, 0:1])).astype(bf)
        for q in range(4):
            lanes = slice(q * quarter, (q + 1) * quarter)
            wd = hd[:, :, :, lanes].reshape(cols, quarter)
            psum[d, q] = psum[d, q] + dot(hot_hid[a], wd)
        to_core[d, 0] = psum[d, 1 - core].astype(bf)
        to_core[d, 1] = psum[d, 3 - core].astype(bf)
        to_c[d] = cp.remote(to_core.at[d], from_core.at[d], other)

    def on_chip(d, side, lanes):
        return psum[d, 2 * side + core, :, lanes] + from_core[d, side, :, lanes].astype(f32)

    for d in order:
        to_c[d].wait_recv()
        if d:
            for side in (0, 1):
                mid[d, side, :, first] = on_chip(d, side, first).astype(bf)
            by_x.append(cp.remote(mid.at[d, :, :, first], from_x.at[d - 1], at(d)))
        mid[d, 1 - z_hi, :, rest] = on_chip(d, 1 - z_hi, rest).astype(bf)
        by_z[d] = cp.remote(mid.at[d, 1 - z_hi, :, rest], from_zb.at[d], across)
    by_xb = []
    for d in order[:3]:
        by_z[d].wait_recv()
        mid_b[d - 1] = (on_chip(d, z_hi, rest) + from_zb[d].astype(f32)).astype(bf)
        by_xb.append(cp.remote(mid_b.at[d - 1], from_xb.at[d - 1], at(d)))
    for c in by_x:
        c.wait_recv()

    def total(side):
        v = on_chip(0, side, first)
        for i in range(3):
            v += from_x[i, side].astype(f32)
        return v

    half[...] = total(1 - z_hi).astype(bf)
    last = cp.remote(half, from_z, across)
    own_total = total(z_hi) + back[:, first]
    by_z[0].wait_recv()
    v = on_chip(0, z_hi, rest) + from_zb[0].astype(f32) + back[:, rest]
    for c in by_xb:
        c.wait_recv()
    for i in range(3):
        v += from_xb[i].astype(f32)
    out[:, rest] = v
    last.wait_recv()
    out[:, first] = own_total + from_z[...].astype(f32)
    for c in cp.started:
        c.wait_send()
    exchanged(pack1, got1, 0, True)
    exchanged(pack2, got2, groups, True)


def local(
    tokens, slot, mask, hot_group, router_weight,
    exp_gate, exp_up, exp_down, sh_gate, sh_up, sh_down,
):
    bf, f32 = jnp.bfloat16, jnp.float32
    x, y, z = coords()
    hot = hot_group[0]
    hx, hy, hz = hot // (NY * NZ), (hot // NZ) % NY, hot % NZ
    scalars = jnp.stack(
        [(hx == x).astype(jnp.int32), (hy == y).astype(jnp.int32), (hz == z).astype(jnp.int32), hot]
    )
    n, quarter = tokens.shape
    d, h = exp_gate.shape[1:]
    rows, cols = d // NY, h // NX
    part = cols // (2 * NY)
    groups = NX * NY * NZ
    any_spec = pl.BlockSpec(memory_space=pl.ANY)
    vmem = pl.BlockSpec(memory_space=pltpu.VMEM)
    depth = -(-CAP * quarter // 128 // 16) * 16
    blocks = pltpu.VMEM((groups, depth, 128), bf)
    summed = pl.pallas_call(
        layer_kernel,
        out_shape=jax.ShapeDtypeStruct((n, quarter), f32),
        in_specs=[pl.BlockSpec(memory_space=pltpu.SMEM), any_spec, vmem, vmem] + [any_spec] * 6,
        out_specs=vmem,
        scratch_shapes=[
            pltpu.VMEM((NY, rows, h), bf),
            pltpu.VMEM((NY, rows, h), bf),
            pltpu.VMEM((NX, NY, 2, part, d), bf),
            pltpu.VMEM((NY, 3, rows, cols), bf),
            pltpu.VMEM((NY, 3, rows, cols), bf),
            pltpu.VMEM((3, rows, cols), bf),
            pltpu.VMEM((3, rows, cols), bf),
            pltpu.VMEM((2, 3, NX, part, d), bf),
            pltpu.VMEM((2, 3, part, d), bf),
            pltpu.VMEM((d, cols), bf),
            pltpu.VMEM((d, cols), bf),
            pltpu.VMEM((NY, 2, part, d), bf),
            pltpu.VMEM((3, NX, NY, NZ, sh_gate.shape[0], cols), bf),
            pltpu.VMEM((NX, n, d), bf),
            pltpu.VMEM((NX, 8, n), f32),
            blocks, blocks, blocks, blocks,
            pltpu.VMEM((n, d), bf),
            pltpu.VMEM((n, h), f32),
            pltpu.VMEM((n, h), f32),
            pltpu.VMEM((n, h), bf),
            pltpu.VMEM((NX * n, cols), f32),
            pltpu.VMEM((NX * n, cols), f32),
            pltpu.VMEM((NX * n, cols), bf),
            pltpu.VMEM((NX * n, cols), bf),
            pltpu.VMEM((NX, NT, n, quarter), f32),
            pltpu.VMEM((NX, 2, n, quarter), bf),
            pltpu.VMEM((NX, 2, n, quarter), bf),
            pltpu.VMEM((NX, 2, n, quarter), bf),
            pltpu.VMEM((3, 2, n, SPLIT), bf),
            pltpu.VMEM((n, SPLIT), bf),
            pltpu.VMEM((n, SPLIT), bf),
            pltpu.VMEM((NX, n, quarter - SPLIT), bf),
            pltpu.VMEM((3, n, quarter - SPLIT), bf),
            pltpu.VMEM((3, n, quarter - SPLIT), bf),
            pltpu.VMEM((n, 128), f32),
            pltpu.VMEM((n, 128), f32),
            pltpu.VMEM((n, 128), jnp.int32),
            pltpu.VMEM((n, quarter), bf),
            pltpu.VMEM((NT, n, quarter), f32),
            pltpu.VMEM((2, n, quarter), bf),
            pltpu.VMEM((2, n, quarter), bf),
            pltpu.VMEM((n, quarter), bf),
            pltpu.VMEM((n, quarter), bf),
            pltpu.VMEM((n, quarter), f32),
            pltpu.SemaphoreType.DMA((SENDS,)),
            pltpu.SemaphoreType.DMA((SENDS,)),
            pltpu.SemaphoreType.DMA((16,)),
            pltpu.SemaphoreType.DMA((2 * groups,)),
            pltpu.SemaphoreType.DMA((2 * groups,)),
        ],
        compiler_params=pltpu.CompilerParams(
            collective_id=0, has_side_effects=True, vmem_limit_bytes=62 * 2**20
        ),
    )(
        scalars, tokens, slot.reshape(1, n), router_weight.T,
        exp_gate[0], exp_up[0], exp_down[0].reshape(NX, NY, 2, part, d), sh_gate, sh_up, sh_down.T,
    )
    return (mask.astype(f32)[:, None] * summed).astype(bf)


def solution(mesh):
    in_specs = (
        P("expert", "tensor"),
        P("expert", None),
        P("expert"),
        P(),
        P(),
        P("expert", None, "tensor"),
        P("expert", None, "tensor"),
        P("expert", "tensor", None),
        P("expert", "tensor"),
        P("expert", "tensor"),
        P("tensor", "expert"),
    )
    out_specs = P("expert", "tensor")
    return jax.shard_map(local, mesh=mesh, in_specs=in_specs, out_specs=out_specs, check_vma=False)
```

```python
import jax
import jax.numpy as jnp
from jax import lax
from jax.experimental import pallas as pl
from jax.experimental.pallas import tpu as pltpu
from jax.sharding import PartitionSpec as P

MESH = pl.DeviceIdType.MESH
NX, NY, NZ, NT, CAP = 4, 4, 2, 4, 4

PARTS = ((0, 384), (384, 128), (512, 128))
SPLIT = 384
SENDS = 240
ORDER = (
    "df", "tok0", "tokx", "sx", "xf00", "own0", "own1t", "pack", "xf01", "route", "wts", "tt",
    "xf02", "s1", "xf03", "d0", "x000", "unpack", "xf12", "xf10", "tf", "x010", "tq", "xf11",
    "x020", "s2", "x030", "x001", "rf", "x120", "x100", "hi0", "hi1", "d1", "x011", "hi2", "x110",
    "hi3", "s3", "hm", "ho0", "ho1", "ho2", "ho3", "hr1", "x021", "x031", "x002", "y00", "hr2",
    "x121", "xf20", "x101", "d2", "dx0", "x012", "y01", "x111", "xf21", "si0", "si1", "x022", "si2",
    "y02", "si3", "x032", "x122", "sm", "so0", "so1", "x102", "y03", "y10", "so2", "dx1", "x112",
    "so3", "y11", "x200", "x210", "ex2", "dx2", "y12", "x201", "xf13", "xf22", "xf23", "sy0",
    "x211", "hb", "dx3", "dz0", "x202", "y20", "fy0", "x130", "x220", "x230", "x212", "y21", "x131",
    "x221", "dy1", "x231", "hot0", "x132", "y13", "x222", "y22", "x232", "dy2", "sy1", "y23", "fy1",
    "sy2", "hot1", "fy2", "hot2", "end",
)


def coords():
    e = lax.axis_index("expert")
    return lax.div(e, NY * NZ), lax.rem(lax.div(e, NZ), NY), lax.rem(e, NZ)


def group_of(x, y, z):
    return (x * NY + y) * NZ + z


def turn(i, n=4):
    return lax.rem(i + 2 * n, n)


class Copies:
    def __init__(self, send, recv, local):
        self.send, self.recv, self.local = send, recv, local
        self.sent, self.kept = 0, 0
        self.started = []
        self.waited = set()

    def remote(self, src, dst, device):
        c = pltpu.make_async_remote_copy(
            src_ref=src,
            dst_ref=dst,
            send_sem=self.send.at[self.sent],
            recv_sem=self.recv.at[self.sent],
            device_id=device,
            device_id_type=MESH,
        )
        self.sent += 1
        c.start()
        self.started.append(c)
        return c

    def here(self, src, dst):
        c = pltpu.make_async_copy(src, dst, self.local.at[self.kept])
        self.kept += 1
        c.start()
        return c

    def once(self, c, remote):
        if id(c) not in self.waited:
            self.waited.add(id(c))
            if remote:
                c.wait_recv()
            else:
                c.wait()

    def got(self, *copies):
        for c in copies:
            self.once(c, True)

    def placed(self, *copies):
        for c in copies:
            self.once(c, False)


def choose(flag, rows, step, mine, into):
    def body(i, carry):
        at = pl.ds(pl.multiple_of(i * step, step), step)
        into[at] = jnp.where(flag == 1, mine(at), into[at])
        return carry

    lax.fori_loop(0, rows // step, body, 0)


def dot(a, b):
    return jnp.dot(a, b, preferred_element_type=jnp.float32)


def silu(v):
    return v / (1.0 + jnp.exp(-v))


def layer_kernel(
    scalars, tok, slot, router, gate, up, down, sh_gate, sh_up, sh_down,
    out,
    own_g, own_u, own_d, xg, xu, yg, yu, yd, xd, hg, hu, hd, sh, tk, coefs,
    pack1, got1, pack2, got2, rows_in, home_g, home_u, home_hid,
    acc_g, acc_u, sh_hid, hot_hid, psum, to_core, from_core, mid, from_x, half, from_z, from_zb, mid_b, from_xb,
    w_cols, target_cols, expert_cols,
    tok_here, home_part, home_send, home_core, home_half, home_z, back,
    send, recv, local, a2a_send, a2a_recv,
):
    x, y, z = coords()
    e = lax.axis_index("expert")
    groups = lax.axis_size("expert")
    t = lax.axis_index("tensor")
    core, z_hi = lax.rem(t, 2), lax.div(t, 2)
    cp = Copies(send, recv, local)
    rows, cols = xg.shape[2], xg.shape[3]
    n, quarter = tok.shape
    bf, f32 = jnp.bfloat16, jnp.float32
    parts = PARTS

    def at(dx=0, dy=0, dz=0):
        return {"expert": group_of(turn(x + dx), turn(y + dy), turn(z + dz, 2)), "tensor": t}

    other_t = z_hi * 2 + (1 - core)
    across_t = (1 - z_hi) * 2 + core
    other = {"expert": e, "tensor": other_t}
    across = {"expert": e, "tensor": across_t}

    def of_quarter(i):
        return pl.ds(pl.multiple_of(i * quarter, quarter), quarter)

    barrier = pltpu.get_barrier_semaphore()

    def greet(k, carry):
        d = {"expert": lax.rem(e + k, groups), "tensor": t}
        pl.semaphore_signal(barrier, inc=1, device_id=d, device_id_type=MESH)
        return carry

    lax.fori_loop(1, groups, greet, 0)
    for d in (other, across):
        pl.semaphore_signal(barrier, inc=1, device_id=d, device_id_type=MESH)
    pl.semaphore_wait(barrier, groups + 1)
    fx, fy, fz, hot = scalars[0], scalars[1], scalars[2], scalars[3]

    streams = ((gate, own_g, xg, yg, hg, 1), (up, own_u, xu, yu, hu, -1))

    def block(sign, j):
        return turn(y - sign * (1 + j))

    x_copy, own_copy, y_copy, z_copy = {}, {}, {}, {}

    def x_first(h, js):
        off, r = parts[h]
        for j in js:
            for s, (w, _, xb, _, _, sign) in enumerate(streams):
                lanes = pl.ds(pl.multiple_of(turn(x - sign) * cols, cols), cols)
                src = w.at[pl.ds(pl.multiple_of(block(sign, j) * rows + off, 128), r), lanes]
                x_copy[h, s, j, 0] = cp.remote(src, xb.at[j, 0, pl.ds(off, r)], at(sign))

    def own_load(j):
        for s, (w, own, _, _, _, sign) in enumerate(streams):
            src = w.at[pl.ds(pl.multiple_of(block(sign, j) * rows, rows), rows), :]
            own_copy[s, j] = cp.here(src, own.at[j])

    def x_step(h, j, step):
        off, r = parts[h]
        for s, (_, own, xb, _, _, sign) in enumerate(streams):
            x_copy[h, s, j, step].wait_recv()
            cp.placed(own_copy[s, j])
            lanes = pl.ds(pl.multiple_of(turn(x - sign * (2 + step)) * cols, cols), cols)
            mine = own.at[j, pl.ds(off, r)]
            into = xb.at[j, step, pl.ds(off, r)]
            choose(fx, r, 128, lambda a, mine=mine, lanes=lanes: mine[a, lanes], into)
            if step < 2:
                nxt = xb.at[j, step + 1, pl.ds(off, r)]
                x_copy[h, s, j, step + 1] = cp.remote(into, nxt, at(sign))

    def y_step(h, j):
        off, r = parts[h]
        for s, (_, _, xb, yb, hb, sign) in enumerate(streams):
            mine = xb.at[j, 2, pl.ds(off, r)]
            if j == 0:
                y_copy[h, s, 0] = cp.remote(mine, yb.at[0, pl.ds(off, r)], at(0, sign))
                continue
            into = yb.at[j - 1, pl.ds(off, r)]
            y_copy[h, s, j - 1].wait_recv()
            choose(fy, r, 128, lambda a, mine=mine: mine[a], into)
            if j < 3:
                y_copy[h, s, j] = cp.remote(into, yb.at[j, pl.ds(off, r)], at(0, sign))
            else:
                z_copy[h, s] = cp.remote(into, hot_rows(hb, h, y), at(0, 0, 1))

    def hot_rows(ref, h, v):
        off, r = parts[h]
        return ref.at[pl.ds(pl.multiple_of(v * rows + off, 128), r)]

    near, far2 = {}, {}

    def spread_y(h):
        off, r = parts[h]
        for s, (_, _, _, yb, hb, sign) in enumerate(streams):
            into = hot_rows(hb, h, y)
            mine = yb.at[2, pl.ds(off, r)]
            z_copy[h, s].wait_recv()
            choose(fz, r, 128, lambda a, mine=mine: mine[a], into)
            near[h, s] = [cp.remote(into, into, at(0, d)) for d in (sign, -sign)]

    def forward_y(h):
        for s, (_, _, _, _, hb, sign) in enumerate(streams):
            near[h, s][0].wait_recv()
            a = hot_rows(hb, h, turn(y - sign))
            far2[h, s] = cp.remote(a, a, at(0, sign))

    def hot_arrived(h):
        for s in (0, 1):
            near[h, s][1].wait_recv()
            far2[h, s].wait_recv()

    d_copy, dx_copy = {}, {}

    def d_first():
        for r, sign in ((0, 1), (1, -1)):
            d_copy[r, 0] = cp.remote(down.at[:, turn(y - sign), r], yd.at[r, 0], at(0, sign))

    def d_step(step):
        for r, sign in ((0, 1), (1, -1)):
            d_copy[r, step].wait_recv()
            cp.placed(c_of["down"])
            yp = turn(y - sign * (2 + step))
            choose(fy, NX, 1, lambda i, yp=yp, r=r: own_d[i, yp, r], yd.at[r, step])
            if step < 2:
                d_copy[r, step + 1] = cp.remote(yd.at[r, step], yd.at[r, step + 1], at(0, sign))

    def dx_step(step):
        for r, sign in ((0, 1), (1, -1)):
            if step == 0:
                dx_copy[r, 0] = cp.remote(yd.at[r, 2, turn(x - sign)], xd.at[r, 0], at(sign))
                continue
            dx_copy[r, step - 1].wait_recv()
            xp = turn(x - sign * (1 + step))
            choose(
                fx, xd.shape[2], 16, lambda i, xp=xp, r=r: yd[r, 2, xp, i], xd.at[r, step - 1]
            )
            if step < 3:
                dx_copy[r, step] = cp.remote(xd.at[r, step - 1], xd.at[r, step], at(sign))

    def exchange(src, dst, base):
        def go(k, carry):
            to = lax.rem(e + k, groups)
            pltpu.make_async_remote_copy(
                src_ref=src.at[to], dst_ref=dst.at[e],
                send_sem=a2a_send.at[base + k], recv_sem=a2a_recv.at[base + k],
                device_id={"expert": to, "tensor": t}, device_id_type=MESH,
            ).start()
            return carry

        lax.fori_loop(1, groups, go, 0)
        return cp.here(src.at[e], dst.at[e])

    def exchanged(src, dst, base, sends):
        def done(k, carry):
            to = lax.rem(e + k, groups)
            frm = lax.rem(e + groups - k, groups)
            c = pltpu.make_async_remote_copy(
                src_ref=src.at[to], dst_ref=dst.at[frm],
                send_sem=a2a_send.at[base + k], recv_sem=a2a_recv.at[base + k],
                device_id={"expert": to, "tensor": t}, device_id_type=MESH,
            )
            if sends:
                c.wait_send()
            else:
                c.wait_recv()
            return carry

        lax.fori_loop(1, groups, done, 0)

    def iota(shape, dim):
        return lax.broadcasted_iota(jnp.int32, shape, dim)

    def as_row(col):
        eye = iota((n, n), 0) == iota((n, n), 1)
        return jnp.sum(jnp.where(eye, col, 0.0), axis=0, keepdims=True)

    def as_col(row):
        eye = iota((n, n), 0) == iota((n, n), 1)
        return jnp.sum(jnp.where(eye, row, 0.0), axis=1, keepdims=True)

    groups_here = NX * NY * NZ

    depth = pack1.shape[1]
    tiles = quarter // 128

    def packed(c, i, key):
        r = iota((n, n), 0) + c * n
        of = (r // depth) * CAP + r % CAP
        return ((of.astype(f32) == key) & ((r % depth) // CAP == i)).astype(bf)

    def pack_into(into, v, key):
        for c in range(groups_here * depth // n):
            acc = jnp.zeros((n, 128), f32)
            for i in range(tiles):
                acc += dot(packed(c, i, key), v[:, i * 128 : (i + 1) * 128])
            into[c * n // depth : (c + 1) * n // depth] = acc.astype(bf).reshape(
                n // depth, depth, 128
            )

    def unpacked(flat, i, key):
        r = iota((n, groups_here * depth), 1)
        of = (r // depth) * CAP + r % CAP
        pick = ((of.astype(f32) == key) & ((r % depth) // CAP == i)).astype(bf)
        return dot(pick, flat)

    mine = of_quarter(t)
    theirs = of_quarter(across_t)
    c_of = {}

    def own_tokens():
        c_of["peer"] = [cp.remote(tok, tk.at[0, :, mine], d) for d in (other, across)]
        c_of["own"] = cp.here(tok, tk.at[0, :, mine])
        c_of["here"] = cp.here(tok, tok_here)

    def quad_tokens():
        c_of["quad"] = [cp.remote(tok, tk.at[(4 - d) % 4, :, mine], at(d)) for d in (2, 1, -1)]

    def quad_across():
        cp.got(*c_of["quad"])
        a = tk.at[1:4, :, mine]
        c_of["quad_peer"] = [cp.remote(a, a, d) for d in (other, across)]

    def quad_relay():
        cp.got(c_of["quad_peer"][1])
        a = tk.at[1:4, :, theirs]
        c_of["quad_relay"] = cp.remote(a, a, other)

    def quad_done():
        cp.got(c_of["quad_peer"][0], c_of["quad_relay"])

    def own_loads():
        for j in range(4):
            own_load(j)
            if j == 0:
                c_of["down"] = cp.here(down, own_d)

    sh_refs = (sh_gate, sh_up, sh_down)

    def sh_piece(i, xp):
        return sh_refs[i].at[:, pl.ds(pl.multiple_of(xp * cols, cols), cols)]

    lo, hi, opp = turn(y - 1), turn(y + 1), turn(y + 2)

    def sh_x():
        c_of["sh_x"] = [
            cp.remote(sh_piece(i, turn(x + d)), sh.at[i, x, y, z], at(d))
            for d in (2, 1, -1)
            for i in range(3)
        ]
        c_of["sh_own"] = [cp.here(sh_piece(i, x), sh.at[i, x, y, z]) for i in range(3)]

    def sh_to(a, device):
        return cp.remote(a, a, device)

    def sh_1():
        cp.got(*c_of["sh_x"])
        cp.placed(*c_of["sh_own"])
        c_of["sh_y"] = [sh_to(sh.at[:, :, y, z], at(0, d)) for d in (1, -1)]
        c_of["sh_z"] = [sh_to(sh.at[:, :, y, z], at(0, 0, 1))]

    def sh_2():
        cp.got(*c_of["sh_y"])
        c_of["sh_y2"] = [
            sh_to(sh.at[:, 0:2, lo, z], at(0, 1)), sh_to(sh.at[:, 2:4, hi, z], at(0, -1))
        ]
        c_of["sh_z"] += [sh_to(sh.at[:, :, v, z], at(0, 0, 1)) for v in (lo, hi)]

    def sh_3():
        cp.got(*c_of["sh_y2"])
        c_of["sh_z"].append(sh_to(sh.at[:, :, opp, z], at(0, 0, 1)))

    def positions():
        cp.placed(c_of["here"])
        ids_row = slot[...].astype(f32)
        ids_f = as_col(ids_row)
        ids = ids_f.astype(jnp.int32)
        same = jnp.where((ids_f == ids_row) & (iota((n, n), 1) < iota((n, n), 0)), 1.0, 0.0)
        position = jnp.sum(same, axis=1, keepdims=True)
        spare = (ids & 1) == 1
        target = jnp.where(spare, -1.0, (ids >> 1).astype(f32) * CAP + position)
        target_cols[...] = jnp.broadcast_to(target, target_cols.shape)
        expert = jnp.where(spare, hot, ids >> 1)
        expert_cols[...] = jnp.broadcast_to(expert, expert_cols.shape)

    def relay():
        cp.placed(c_of["own"])
        cp.got(c_of["peer"][1])
        a = tk.at[0, :, theirs]
        c_of["relay"] = cp.remote(a, a, other)

    def pack():
        pack_into(pack1, tok_here, as_row(target_cols[:, 0:1]))
        c_of["own1"] = exchange(pack1, got1, 0)

    def weights():
        cp.got(c_of["peer"][0], c_of["relay"])
        logits = lax.dot_general(
            tk[0], router[...], (((1,), (1,)), ((), ())), preferred_element_type=f32
        )
        chosen = expert_cols[:, 0 : logits.shape[1]] == iota(logits.shape, 1)
        w = jax.nn.sigmoid(jnp.sum(jnp.where(chosen, logits, 0.0), axis=1, keepdims=True))
        w_cols[...] = jnp.broadcast_to(w, w_cols.shape)
        coef = jnp.where(target_cols[:, 0:1] < 0, w, 0.0)
        coefs[0] = jnp.broadcast_to(as_row(coef), coefs.shape[1:])
        c_of["coef"] = [cp.remote(coefs.at[0], coefs.at[(4 - d) % 4], at(d)) for d in (2, 1, -1)]

    def unpack_rows():
        exchanged(pack1, got1, 0, False)
        cp.placed(c_of["own1"])
        flat = got1[...].reshape(groups_here * depth, 128)
        key = iota((n, 1), 0).astype(f32)
        for i in range(tiles):
            lanes = pl.ds(pl.multiple_of(t * quarter + i * 128, 128), 128)
            rows_in[:, lanes] = unpacked(flat, i, key).astype(bf)
        a = rows_in.at[:, mine]
        c_of["rows"] = [cp.remote(a, a, d) for d in (other, across)]

    def rows_relay():
        cp.got(c_of["rows"][1])
        a = rows_in.at[:, theirs]
        c_of["rows_relay"] = cp.remote(a, a, other)

    def home_in(j):
        if j == 0:
            cp.got(c_of["rows"][0], c_of["rows_relay"])
        for acc, own, sign in ((home_g, own_g, 1), (home_u, own_u, -1)):
            cp.placed(own_copy[0 if sign == 1 else 1, j])
            a = rows_in[:, pl.ds(pl.multiple_of(block(sign, j) * rows, rows), rows)]
            v = dot(a, own[j])
            acc[...] = v if j == 0 else acc[...] + v

    def home_mid():
        home_hid[...] = (silu(home_g[...]) * home_u[...]).astype(bf)

    def home_out(q):
        cp.placed(c_of["down"])
        lanes = slice(q * quarter, (q + 1) * quarter)
        v = jnp.zeros((n, quarter), f32)
        for i in range(NX):
            wd = own_d[i, :, :, :, lanes].reshape(cols, quarter)
            v += dot(home_hid[:, i * cols : (i + 1) * cols], wd)
        home_part[q] = v

    def home_sum_core():
        for side in (0, 1):
            home_send[side] = home_part[2 * side + 1 - core].astype(bf)
        c_of["home_core"] = cp.remote(home_send, home_core, other)

    def home_sum_across():
        cp.got(c_of["home_core"])
        v = home_part[2 * (1 - z_hi) + core] + home_core[1 - z_hi].astype(f32)
        home_half[...] = v.astype(bf)
        c_of["home_z"] = cp.remote(home_half, home_z, across)

    def send_back():
        cp.got(c_of["home_z"])
        v = home_part[2 * z_hi + core] + home_core[z_hi].astype(f32) + home_z[...].astype(f32)
        row = iota((1, n), 1).astype(f32)
        pack_into(pack2, v.astype(bf), row)
        c_of["own2"] = exchange(pack2, got2, groups)

    def home_back():
        exchanged(pack2, got2, groups, False)
        cp.placed(c_of["own2"])
        flat = got2[...].reshape(groups_here * depth, 128)
        key = target_cols[:, 0:1]
        for i in range(tiles):
            lanes = slice(i * 128, (i + 1) * 128)
            back[:, lanes] = w_cols[:, 0:1] * unpacked(flat, i, key)

    def quad_in(lanes, w_gate, w_up, first):
        a = tk[:, :, lanes].reshape(NX * n, -1)
        for acc, wt in ((acc_g, w_gate), (acc_u, w_up)):
            v = dot(a, wt)
            acc[...] = v if first else acc[...] + v

    def shared_in(k):
        quad_in(
            slice(k * rows, (k + 1) * rows),
            sh[0, k].reshape(rows, cols), sh[1, k].reshape(rows, cols), k == 0,
        )

    def shared_mid():
        sh_hid[...] = (silu(acc_g[...]) * acc_u[...]).astype(bf)

    def shared_out(q):
        wt = sh[2, q].reshape(quarter, cols)
        v = lax.dot_general(
            sh_hid[...], wt, (((1,), (1,)), ((), ())), preferred_element_type=f32
        )
        psum[:, q] = v.reshape(NX, n, quarter)

    def hot_in(h, k):
        off, r = parts[h]
        lanes = slice(k * rows + off, k * rows + off + r)
        quad_in(lanes, hg[lanes], hu[lanes], h == 0 and k == 0)

    def shared_first():
        cp.got(*c_of["sh_z"])
        shared_in(0)

    d_z, d_y, d_y2 = [], [], []

    def d_z_send():
        d_z.extend(cp.remote(xd.at[r, 2], hd.at[y, r], at(0, 0, 1)) for r in (0, 1))

    def d_spread():
        for r in (0, 1):
            d_z[r].wait_recv()
            choose(fz, xd.shape[2], 16, lambda i, r=r: xd[r, 2, i], hd.at[y, r])
            d_y.append([cp.remote(hd.at[y, r], hd.at[y, r], at(0, d)) for d in (1, -1)])

    def d_forward():
        cp.got(d_y[0][0], d_y[1][1])
        d_y2.append(cp.remote(hd.at[lo, 0], hd.at[lo, 0], at(0, 1)))
        d_y2.append(cp.remote(hd.at[hi, 1], hd.at[hi, 1], at(0, -1)))

    def hot_part(h):
        hot_arrived(h)
        for k in range(4):
            hot_in(h, k)

    def end():
        cp.got(*c_of["coef"], d_y[0][1], d_y[1][0], *d_y2)

    tasks = {
        "tok0": own_tokens, "tokx": quad_tokens, "tt": quad_across, "tf": quad_relay,
        "tq": quad_done, "own0": own_loads, "df": d_first, "dz0": d_z_send, "dy1": d_spread,
        "dy2": d_forward, "sx": sh_x, "s1": sh_1, "s2": sh_2, "s3": sh_3, "own1t": positions, "route": relay, "rf": rows_relay, "hr1": home_sum_core,
        "hr2": home_sum_across,
        "pack": pack, "wts": weights, "unpack": unpack_rows, "hm": home_mid, "ex2": send_back,
        "si0": shared_first, "sm": shared_mid, "hb": home_back, "end": end,
    }
    for name in ORDER:
        if name in tasks:
            tasks[name]()
            continue
        kind, at_ = name.rstrip("0123456789"), [int(c) for c in name.lstrip("abcdefghijklmnopqrstuvwxyz")]
        if kind == "xf":
            x_first(at_[0], at_[1:])
        else:
            {
                "x": x_step, "y": y_step, "sy": spread_y, "fy": forward_y, "hot": hot_part,
                "d": d_step, "dx": dx_step, "hi": home_in, "ho": home_out,
                "si": shared_in, "so": shared_out,
            }[kind](*at_)

    first, rest = slice(0, SPLIT), slice(SPLIT, quarter)
    to_c, by_x, by_z = {}, [], {}
    order = (2, 1, 3, 0)

    def product(d):
        a = slice(d * n, (d + 1) * n)
        hot_hid[a] = (silu(acc_g[a]) * acc_u[a] * as_col(coefs[d, 0:1])).astype(bf)
        for q in range(4):
            lanes = slice(q * quarter, (q + 1) * quarter)
            wd = hd[:, :, :, lanes].reshape(cols, quarter)
            psum[d, q] = psum[d, q] + dot(hot_hid[a], wd)
        to_core[d, 0] = psum[d, 1 - core].astype(bf)
        to_core[d, 1] = psum[d, 3 - core].astype(bf)
        to_c[d] = cp.remote(to_core.at[d], from_core.at[d], other)

    def on_chip(d, side, lanes):
        return psum[d, 2 * side + core, :, lanes] + from_core[d, side, :, lanes].astype(f32)

    def onward(d):
        to_c[d].wait_recv()
        if d:
            for side in (0, 1):
                mid[d, side, :, first] = on_chip(d, side, first).astype(bf)
            by_x.append(cp.remote(mid.at[d, :, :, first], from_x.at[d - 1], at(d)))
        mid[d, 1 - z_hi, :, rest] = on_chip(d, 1 - z_hi, rest).astype(bf)
        by_z[d] = cp.remote(mid.at[d, 1 - z_hi, :, rest], from_zb.at[d], across)

    product(order[0])
    for i in (1, 2, 3):
        product(order[i])
        onward(order[i - 1])
    onward(order[3])
    by_xb = []
    for d in order[:3]:
        by_z[d].wait_recv()
        mid_b[d - 1] = (on_chip(d, z_hi, rest) + from_zb[d].astype(f32)).astype(bf)
        by_xb.append(cp.remote(mid_b.at[d - 1], from_xb.at[d - 1], at(d)))
    for c in by_x:
        c.wait_recv()

    def total(side):
        v = on_chip(0, side, first)
        for i in range(3):
            v += from_x[i, side].astype(f32)
        return v

    half[...] = total(1 - z_hi).astype(bf)
    last = cp.remote(half, from_z, across)
    own_total = total(z_hi) + back[:, first]
    by_z[0].wait_recv()
    v = on_chip(0, z_hi, rest) + from_zb[0].astype(f32) + back[:, rest]
    for c in by_xb:
        c.wait_recv()
    for i in range(3):
        v += from_xb[i].astype(f32)
    out[:, rest] = v
    last.wait_recv()
    out[:, first] = own_total + from_z[...].astype(f32)
    for c in cp.started:
        c.wait_send()
    exchanged(pack1, got1, 0, True)
    exchanged(pack2, got2, groups, True)


def local(
    tokens, slot, mask, hot_group, router_weight,
    exp_gate, exp_up, exp_down, sh_gate, sh_up, sh_down,
):
    bf, f32 = jnp.bfloat16, jnp.float32
    x, y, z = coords()
    hot = hot_group[0]
    hx, hy, hz = hot // (NY * NZ), (hot // NZ) % NY, hot % NZ
    scalars = jnp.stack(
        [(hx == x).astype(jnp.int32), (hy == y).astype(jnp.int32), (hz == z).astype(jnp.int32), hot]
    )
    n, quarter = tokens.shape
    d, h = exp_gate.shape[1:]
    rows, cols = d // NY, h // NX
    part = cols // (2 * NY)
    groups = NX * NY * NZ
    any_spec = pl.BlockSpec(memory_space=pl.ANY)
    vmem = pl.BlockSpec(memory_space=pltpu.VMEM)
    depth = -(-CAP * quarter // 128 // 16) * 16
    blocks = pltpu.VMEM((groups, depth, 128), bf)
    summed = pl.pallas_call(
        layer_kernel,
        out_shape=jax.ShapeDtypeStruct((n, quarter), f32),
        in_specs=[pl.BlockSpec(memory_space=pltpu.SMEM), any_spec, vmem, vmem] + [any_spec] * 6,
        out_specs=vmem,
        scratch_shapes=[
            pltpu.VMEM((NY, rows, h), bf),
            pltpu.VMEM((NY, rows, h), bf),
            pltpu.VMEM((NX, NY, 2, part, d), bf),
            pltpu.VMEM((NY, 3, rows, cols), bf),
            pltpu.VMEM((NY, 3, rows, cols), bf),
            pltpu.VMEM((3, rows, cols), bf),
            pltpu.VMEM((3, rows, cols), bf),
            pltpu.VMEM((2, 3, NX, part, d), bf),
            pltpu.VMEM((2, 3, part, d), bf),
            pltpu.VMEM((d, cols), bf),
            pltpu.VMEM((d, cols), bf),
            pltpu.VMEM((NY, 2, part, d), bf),
            pltpu.VMEM((3, NX, NY, NZ, sh_gate.shape[0], cols), bf),
            pltpu.VMEM((NX, n, d), bf),
            pltpu.VMEM((NX, 8, n), f32),
            blocks, blocks, blocks, blocks,
            pltpu.VMEM((n, d), bf),
            pltpu.VMEM((n, h), f32),
            pltpu.VMEM((n, h), f32),
            pltpu.VMEM((n, h), bf),
            pltpu.VMEM((NX * n, cols), f32),
            pltpu.VMEM((NX * n, cols), f32),
            pltpu.VMEM((NX * n, cols), bf),
            pltpu.VMEM((NX * n, cols), bf),
            pltpu.VMEM((NX, NT, n, quarter), f32),
            pltpu.VMEM((NX, 2, n, quarter), bf),
            pltpu.VMEM((NX, 2, n, quarter), bf),
            pltpu.VMEM((NX, 2, n, quarter), bf),
            pltpu.VMEM((3, 2, n, SPLIT), bf),
            pltpu.VMEM((n, SPLIT), bf),
            pltpu.VMEM((n, SPLIT), bf),
            pltpu.VMEM((NX, n, quarter - SPLIT), bf),
            pltpu.VMEM((3, n, quarter - SPLIT), bf),
            pltpu.VMEM((3, n, quarter - SPLIT), bf),
            pltpu.VMEM((n, 128), f32),
            pltpu.VMEM((n, 128), f32),
            pltpu.VMEM((n, 128), jnp.int32),
            pltpu.VMEM((n, quarter), bf),
            pltpu.VMEM((NT, n, quarter), f32),
            pltpu.VMEM((2, n, quarter), bf),
            pltpu.VMEM((2, n, quarter), bf),
            pltpu.VMEM((n, quarter), bf),
            pltpu.VMEM((n, quarter), bf),
            pltpu.VMEM((n, quarter), f32),
            pltpu.SemaphoreType.DMA((SENDS,)),
            pltpu.SemaphoreType.DMA((SENDS,)),
            pltpu.SemaphoreType.DMA((16,)),
            pltpu.SemaphoreType.DMA((2 * groups,)),
            pltpu.SemaphoreType.DMA((2 * groups,)),
        ],
        compiler_params=pltpu.CompilerParams(
            collective_id=0, has_side_effects=True, vmem_limit_bytes=62 * 2**20
        ),
    )(
        scalars, tokens, slot.reshape(1, n), router_weight.T,
        exp_gate[0], exp_up[0], exp_down[0].reshape(NX, NY, 2, part, d), sh_gate, sh_up, sh_down.T,
    )
    return (mask.astype(f32)[:, None] * summed).astype(bf)


def solution(mesh):
    in_specs = (
        P("expert", "tensor"),
        P("expert", None),
        P("expert"),
        P(),
        P(),
        P("expert", None, "tensor"),
        P("expert", None, "tensor"),
        P("expert", "tensor", None),
        P("expert", "tensor"),
        P("expert", "tensor"),
        P("tensor", "expert"),
    )
    out_specs = P("expert", "tensor")
    return jax.shard_map(local, mesh=mesh, in_specs=in_specs, out_specs=out_specs, check_vma=False)
```

```python
import jax
import jax.numpy as jnp
from jax import lax
from jax.experimental import pallas as pl
from jax.experimental.pallas import tpu as pltpu
from jax.sharding import PartitionSpec as P

MESH = pl.DeviceIdType.MESH
NX, NY, NZ, NT, CAP = 4, 4, 2, 4, 4

PARTS = ((0, 384), (384, 128), (512, 128))
SPLIT = 384
SENDS = 240
ORDER = (
    "df", "tok0", "tokx", "sx", "xf00", "own0", "own1t", "pack", "xf01", "route", "wts", "tt",
    "xf02", "s1", "xf03", "d0", "x000", "unpack", "xf12", "xf10", "tf", "x010", "tq", "xf11",
    "x020", "s2", "x030", "x001", "rf", "x120", "x100", "hi0", "hi1", "d1", "x011", "hi2", "x110",
    "hi3", "s3", "hm", "ho0", "ho1", "ho2", "ho3", "hr1", "x021", "x031", "x002", "y00", "hr2",
    "x121", "xf20", "x101", "d2", "dx0", "x012", "y01", "x111", "xf21", "si0", "si1", "x022", "si2",
    "y02", "si3", "x032", "x122", "sm", "so0", "so1", "x102", "y03", "y10", "so2", "dx1", "x112",
    "so3", "y11", "x200", "x210", "ex2", "dx2", "y12", "x201", "xf13", "xf22", "xf23", "sy0",
    "x211", "hb", "dx3", "dz0", "x202", "y20", "fy0", "x130", "x220", "x230", "x212", "y21", "x131",
    "x221", "dy1", "x231", "hot0", "x132", "y13", "x222", "y22", "x232", "dy2", "sy1", "y23", "fy1",
    "sy2", "hot1", "fy2", "hot2", "end",
)


def coords():
    e = lax.axis_index("expert")
    return lax.div(e, NY * NZ), lax.rem(lax.div(e, NZ), NY), lax.rem(e, NZ)


def group_of(x, y, z):
    return (x * NY + y) * NZ + z


def turn(i, n=4):
    return lax.rem(i + 2 * n, n)


class Copies:
    def __init__(self, send, recv, local):
        self.send, self.recv, self.local = send, recv, local
        self.sent, self.kept = 0, 0
        self.started = []
        self.waited = set()

    def remote(self, src, dst, device):
        c = pltpu.make_async_remote_copy(
            src_ref=src,
            dst_ref=dst,
            send_sem=self.send.at[self.sent],
            recv_sem=self.recv.at[self.sent],
            device_id=device,
            device_id_type=MESH,
        )
        self.sent += 1
        c.start()
        self.started.append(c)
        return c

    def here(self, src, dst):
        c = pltpu.make_async_copy(src, dst, self.local.at[self.kept])
        self.kept += 1
        c.start()
        return c

    def once(self, c, remote):
        if id(c) not in self.waited:
            self.waited.add(id(c))
            if remote:
                c.wait_recv()
            else:
                c.wait()

    def got(self, *copies):
        for c in copies:
            self.once(c, True)

    def placed(self, *copies):
        for c in copies:
            self.once(c, False)


def choose(flag, rows, step, mine, into):
    def body(i, carry):
        at = pl.ds(pl.multiple_of(i * step, step), step)
        into[at] = jnp.where(flag == 1, mine(at), into[at])
        return carry

    lax.fori_loop(0, rows // step, body, 0)


def dot(a, b):
    return jnp.dot(a, b, preferred_element_type=jnp.float32)


def silu(v):
    return v / (1.0 + jnp.exp(-v))


def layer_kernel(
    scalars, tok, slot, router, gate, up, down, sh_gate, sh_up, sh_down,
    out,
    own_g, own_u, own_d, xg, xu, yg, yu, yd, xd, hg, hu, hd, sh, tk, coefs,
    pack1, got1, pack2, got2, rows_in, home_g, home_u, home_hid,
    acc_g, acc_u, sh_hid, hot_hid, psum, to_core, from_core, mid, from_x, half, from_z, from_zb, mid_b, from_xb,
    w_cols, target_cols, expert_cols,
    tok_here, home_part, home_send, home_core, home_half, home_z, back,
    send, recv, local, a2a_send, a2a_recv,
):
    x, y, z = coords()
    e = lax.axis_index("expert")
    groups = lax.axis_size("expert")
    t = lax.axis_index("tensor")
    core, z_hi = lax.rem(t, 2), lax.div(t, 2)
    cp = Copies(send, recv, local)
    rows, cols = xg.shape[2], xg.shape[3]
    n, quarter = tok.shape
    bf, f32 = jnp.bfloat16, jnp.float32
    parts = PARTS

    def at(dx=0, dy=0, dz=0):
        return {"expert": group_of(turn(x + dx), turn(y + dy), turn(z + dz, 2)), "tensor": t}

    other_t = z_hi * 2 + (1 - core)
    across_t = (1 - z_hi) * 2 + core
    other = {"expert": e, "tensor": other_t}
    across = {"expert": e, "tensor": across_t}

    def of_quarter(i):
        return pl.ds(pl.multiple_of(i * quarter, quarter), quarter)

    barrier = pltpu.get_barrier_semaphore()

    def greet(k, carry):
        d = {"expert": lax.rem(e + k, groups), "tensor": t}
        pl.semaphore_signal(barrier, inc=1, device_id=d, device_id_type=MESH)
        return carry

    lax.fori_loop(1, groups, greet, 0)
    for d in (other, across):
        pl.semaphore_signal(barrier, inc=1, device_id=d, device_id_type=MESH)
    pl.semaphore_wait(barrier, groups + 1)
    fx, fy, fz, hot = scalars[0], scalars[1], scalars[2], scalars[3]

    streams = ((gate, own_g, xg, yg, hg, 1), (up, own_u, xu, yu, hu, -1))

    def block(sign, j):
        return turn(y - sign * (1 + j))

    x_copy, own_copy, y_copy, z_copy = {}, {}, {}, {}

    def x_first(h, js):
        off, r = parts[h]
        for j in js:
            for s, (w, _, xb, _, _, sign) in enumerate(streams):
                lanes = pl.ds(pl.multiple_of(turn(x - sign) * cols, cols), cols)
                src = w.at[pl.ds(pl.multiple_of(block(sign, j) * rows + off, 128), r), lanes]
                x_copy[h, s, j, 0] = cp.remote(src, xb.at[j, 0, pl.ds(off, r)], at(sign))

    def own_load(j):
        for s, (w, own, _, _, _, sign) in enumerate(streams):
            src = w.at[pl.ds(pl.multiple_of(block(sign, j) * rows, rows), rows), :]
            own_copy[s, j] = cp.here(src, own.at[j])

    def x_step(h, j, step):
        off, r = parts[h]
        for s, (_, own, xb, _, _, sign) in enumerate(streams):
            x_copy[h, s, j, step].wait_recv()
            cp.placed(own_copy[s, j])
            lanes = pl.ds(pl.multiple_of(turn(x - sign * (2 + step)) * cols, cols), cols)
            mine = own.at[j, pl.ds(off, r)]
            into = xb.at[j, step, pl.ds(off, r)]
            choose(fx, r, 128, lambda a, mine=mine, lanes=lanes: mine[a, lanes], into)
            if step < 2:
                nxt = xb.at[j, step + 1, pl.ds(off, r)]
                x_copy[h, s, j, step + 1] = cp.remote(into, nxt, at(sign))

    def y_step(h, j):
        off, r = parts[h]
        for s, (_, _, xb, yb, hb, sign) in enumerate(streams):
            mine = xb.at[j, 2, pl.ds(off, r)]
            if j == 0:
                y_copy[h, s, 0] = cp.remote(mine, yb.at[0, pl.ds(off, r)], at(0, sign))
                continue
            into = yb.at[j - 1, pl.ds(off, r)]
            y_copy[h, s, j - 1].wait_recv()
            choose(fy, r, 128, lambda a, mine=mine: mine[a], into)
            if j < 3:
                y_copy[h, s, j] = cp.remote(into, yb.at[j, pl.ds(off, r)], at(0, sign))
            else:
                z_copy[h, s] = cp.remote(into, hot_rows(hb, h, y), at(0, 0, 1))

    def hot_rows(ref, h, v):
        off, r = parts[h]
        return ref.at[pl.ds(pl.multiple_of(v * rows + off, 128), r)]

    near, far2 = {}, {}

    def spread_y(h):
        off, r = parts[h]
        for s, (_, _, _, yb, hb, sign) in enumerate(streams):
            into = hot_rows(hb, h, y)
            mine = yb.at[2, pl.ds(off, r)]
            z_copy[h, s].wait_recv()
            choose(fz, r, 128, lambda a, mine=mine: mine[a], into)
            near[h, s] = [cp.remote(into, into, at(0, d)) for d in (sign, -sign)]

    def forward_y(h):
        for s, (_, _, _, _, hb, sign) in enumerate(streams):
            near[h, s][0].wait_recv()
            a = hot_rows(hb, h, turn(y - sign))
            far2[h, s] = cp.remote(a, a, at(0, sign))

    d_copy, dx_copy = {}, {}

    def d_first():
        for r, sign in ((0, 1), (1, -1)):
            d_copy[r, 0] = cp.remote(down.at[:, turn(y - sign), r], yd.at[r, 0], at(0, sign))

    def d_step(step):
        for r, sign in ((0, 1), (1, -1)):
            d_copy[r, step].wait_recv()
            cp.placed(c_of["down"])
            yp = turn(y - sign * (2 + step))
            choose(fy, NX, 1, lambda i, yp=yp, r=r: own_d[i, yp, r], yd.at[r, step])
            if step < 2:
                d_copy[r, step + 1] = cp.remote(yd.at[r, step], yd.at[r, step + 1], at(0, sign))

    def dx_step(step):
        for r, sign in ((0, 1), (1, -1)):
            if step == 0:
                dx_copy[r, 0] = cp.remote(yd.at[r, 2, turn(x - sign)], xd.at[r, 0], at(sign))
                continue
            dx_copy[r, step - 1].wait_recv()
            xp = turn(x - sign * (1 + step))
            choose(
                fx, xd.shape[2], 16, lambda i, xp=xp, r=r: yd[r, 2, xp, i], xd.at[r, step - 1]
            )
            if step < 3:
                dx_copy[r, step] = cp.remote(xd.at[r, step - 1], xd.at[r, step], at(sign))

    def exchange(src, dst, base):
        def go(k, carry):
            to = lax.rem(e + k, groups)
            pltpu.make_async_remote_copy(
                src_ref=src.at[to], dst_ref=dst.at[e],
                send_sem=a2a_send.at[base + k], recv_sem=a2a_recv.at[base + k],
                device_id={"expert": to, "tensor": t}, device_id_type=MESH,
            ).start()
            return carry

        lax.fori_loop(1, groups, go, 0)
        return cp.here(src.at[e], dst.at[e])

    def exchanged(src, dst, base, sends):
        def done(k, carry):
            to = lax.rem(e + k, groups)
            frm = lax.rem(e + groups - k, groups)
            c = pltpu.make_async_remote_copy(
                src_ref=src.at[to], dst_ref=dst.at[frm],
                send_sem=a2a_send.at[base + k], recv_sem=a2a_recv.at[base + k],
                device_id={"expert": to, "tensor": t}, device_id_type=MESH,
            )
            if sends:
                c.wait_send()
            else:
                c.wait_recv()
            return carry

        lax.fori_loop(1, groups, done, 0)

    def iota(shape, dim):
        return lax.broadcasted_iota(jnp.int32, shape, dim)

    def as_row(col):
        eye = iota((n, n), 0) == iota((n, n), 1)
        return jnp.sum(jnp.where(eye, col, 0.0), axis=0, keepdims=True)

    def as_col(row):
        eye = iota((n, n), 0) == iota((n, n), 1)
        return jnp.sum(jnp.where(eye, row, 0.0), axis=1, keepdims=True)

    groups_here = NX * NY * NZ

    depth = pack1.shape[1]
    tiles = quarter // 128

    def packed(c, i, key):
        r = iota((n, n), 0) + c * n
        of = (r // depth) * CAP + r % CAP
        return ((of.astype(f32) == key) & ((r % depth) // CAP == i)).astype(bf)

    def pack_into(into, v, key):
        for c in range(groups_here * depth // n):
            acc = jnp.zeros((n, 128), f32)
            for i in range(tiles):
                acc += dot(packed(c, i, key), v[:, i * 128 : (i + 1) * 128])
            into[c * n // depth : (c + 1) * n // depth] = acc.astype(bf).reshape(
                n // depth, depth, 128
            )

    def unpacked(flat, i, key):
        r = iota((n, groups_here * depth), 1)
        of = (r // depth) * CAP + r % CAP
        pick = ((of.astype(f32) == key) & ((r % depth) // CAP == i)).astype(bf)
        return dot(pick, flat)

    mine = of_quarter(t)
    theirs = of_quarter(across_t)
    c_of = {}

    def own_tokens():
        c_of["peer"] = [cp.remote(tok, tk.at[0, :, mine], d) for d in (other, across)]
        c_of["own"] = cp.here(tok, tk.at[0, :, mine])
        c_of["here"] = cp.here(tok, tok_here)

    def quad_tokens():
        c_of["quad"] = [cp.remote(tok, tk.at[(4 - d) % 4, :, mine], at(d)) for d in (2, 1, -1)]

    def quad_across():
        cp.got(*c_of["quad"])
        a = tk.at[1:4, :, mine]
        c_of["quad_peer"] = [cp.remote(a, a, d) for d in (other, across)]

    def quad_relay():
        cp.got(c_of["quad_peer"][1])
        a = tk.at[1:4, :, theirs]
        c_of["quad_relay"] = cp.remote(a, a, other)

    def quad_done():
        cp.got(c_of["quad_peer"][0], c_of["quad_relay"])

    def own_loads():
        for j in range(4):
            own_load(j)
            if j == 0:
                c_of["down"] = cp.here(down, own_d)

    sh_refs = (sh_gate, sh_up, sh_down)

    def sh_piece(i, xp):
        return sh_refs[i].at[:, pl.ds(pl.multiple_of(xp * cols, cols), cols)]

    lo, hi, opp = turn(y - 1), turn(y + 1), turn(y + 2)

    def sh_x():
        c_of["sh_x"] = [
            cp.remote(sh_piece(i, turn(x + d)), sh.at[i, x, y, z], at(d))
            for d in (2, 1, -1)
            for i in range(3)
        ]
        c_of["sh_own"] = [cp.here(sh_piece(i, x), sh.at[i, x, y, z]) for i in range(3)]

    def sh_to(a, device):
        return cp.remote(a, a, device)

    def sh_1():
        cp.got(*c_of["sh_x"])
        cp.placed(*c_of["sh_own"])
        c_of["sh_y"] = [sh_to(sh.at[:, :, y, z], at(0, d)) for d in (1, -1)]
        c_of["sh_z"] = [sh_to(sh.at[:, :, y, z], at(0, 0, 1))]

    def sh_2():
        cp.got(*c_of["sh_y"])
        c_of["sh_y2"] = [
            sh_to(sh.at[:, 0:2, lo, z], at(0, 1)), sh_to(sh.at[:, 2:4, hi, z], at(0, -1))
        ]
        c_of["sh_z"] += [sh_to(sh.at[:, :, v, z], at(0, 0, 1)) for v in (lo, hi)]

    def sh_3():
        cp.got(*c_of["sh_y2"])
        c_of["sh_z"].append(sh_to(sh.at[:, :, opp, z], at(0, 0, 1)))

    def positions():
        cp.placed(c_of["here"])
        ids_row = slot[...].astype(f32)
        ids_f = as_col(ids_row)
        ids = ids_f.astype(jnp.int32)
        same = jnp.where((ids_f == ids_row) & (iota((n, n), 1) < iota((n, n), 0)), 1.0, 0.0)
        position = jnp.sum(same, axis=1, keepdims=True)
        spare = (ids & 1) == 1
        target = jnp.where(spare, -1.0, (ids >> 1).astype(f32) * CAP + position)
        target_cols[...] = jnp.broadcast_to(target, target_cols.shape)
        expert = jnp.where(spare, hot, ids >> 1)
        expert_cols[...] = jnp.broadcast_to(expert, expert_cols.shape)

    def relay():
        cp.placed(c_of["own"])
        cp.got(c_of["peer"][1])
        a = tk.at[0, :, theirs]
        c_of["relay"] = cp.remote(a, a, other)

    def pack():
        pack_into(pack1, tok_here, as_row(target_cols[:, 0:1]))
        c_of["own1"] = exchange(pack1, got1, 0)

    def weights():
        cp.got(c_of["peer"][0], c_of["relay"])
        logits = lax.dot_general(
            tk[0], router[...], (((1,), (1,)), ((), ())), preferred_element_type=f32
        )
        chosen = expert_cols[:, 0 : logits.shape[1]] == iota(logits.shape, 1)
        w = jax.nn.sigmoid(jnp.sum(jnp.where(chosen, logits, 0.0), axis=1, keepdims=True))
        w_cols[...] = jnp.broadcast_to(w, w_cols.shape)
        coef = jnp.where(target_cols[:, 0:1] < 0, w, 0.0)
        coefs[0] = jnp.broadcast_to(as_row(coef), coefs.shape[1:])
        c_of["coef"] = [cp.remote(coefs.at[0], coefs.at[(4 - d) % 4], at(d)) for d in (2, 1, -1)]

    def unpack_rows():
        exchanged(pack1, got1, 0, False)
        cp.placed(c_of["own1"])
        flat = got1[...].reshape(groups_here * depth, 128)
        key = iota((n, 1), 0).astype(f32)
        for i in range(tiles):
            lanes = pl.ds(pl.multiple_of(t * quarter + i * 128, 128), 128)
            rows_in[:, lanes] = unpacked(flat, i, key).astype(bf)
        a = rows_in.at[:, mine]
        c_of["rows"] = [cp.remote(a, a, d) for d in (other, across)]

    def rows_relay():
        cp.got(c_of["rows"][1])
        a = rows_in.at[:, theirs]
        c_of["rows_relay"] = cp.remote(a, a, other)

    def home_in(j):
        if j == 0:
            cp.got(c_of["rows"][0], c_of["rows_relay"])
        for acc, own, sign in ((home_g, own_g, 1), (home_u, own_u, -1)):
            cp.placed(own_copy[0 if sign == 1 else 1, j])
            a = rows_in[:, pl.ds(pl.multiple_of(block(sign, j) * rows, rows), rows)]
            v = dot(a, own[j])
            acc[...] = v if j == 0 else acc[...] + v

    def home_mid():
        home_hid[...] = (silu(home_g[...]) * home_u[...]).astype(bf)

    def home_out(q):
        cp.placed(c_of["down"])
        lanes = slice(q * quarter, (q + 1) * quarter)
        v = jnp.zeros((n, quarter), f32)
        for i in range(NX):
            wd = own_d[i, :, :, :, lanes].reshape(cols, quarter)
            v += dot(home_hid[:, i * cols : (i + 1) * cols], wd)
        home_part[q] = v

    def home_sum_core():
        for side in (0, 1):
            home_send[side] = home_part[2 * side + 1 - core].astype(bf)
        c_of["home_core"] = cp.remote(home_send, home_core, other)

    def home_sum_across():
        cp.got(c_of["home_core"])
        v = home_part[2 * (1 - z_hi) + core] + home_core[1 - z_hi].astype(f32)
        home_half[...] = v.astype(bf)
        c_of["home_z"] = cp.remote(home_half, home_z, across)

    def send_back():
        cp.got(c_of["home_z"])
        v = home_part[2 * z_hi + core] + home_core[z_hi].astype(f32) + home_z[...].astype(f32)
        row = iota((1, n), 1).astype(f32)
        pack_into(pack2, v.astype(bf), row)
        c_of["own2"] = exchange(pack2, got2, groups)

    def home_back():
        exchanged(pack2, got2, groups, False)
        cp.placed(c_of["own2"])
        flat = got2[...].reshape(groups_here * depth, 128)
        key = target_cols[:, 0:1]
        for i in range(tiles):
            lanes = slice(i * 128, (i + 1) * 128)
            back[:, lanes] = w_cols[:, 0:1] * unpacked(flat, i, key)

    def quad_in(lanes, w_gate, w_up, first):
        a = tk[:, :, lanes].reshape(NX * n, -1)
        for acc, wt in ((acc_g, w_gate), (acc_u, w_up)):
            v = dot(a, wt)
            acc[...] = v if first else acc[...] + v

    def shared_in(k):
        quad_in(
            slice(k * rows, (k + 1) * rows),
            sh[0, k].reshape(rows, cols), sh[1, k].reshape(rows, cols), k == 0,
        )

    def shared_mid():
        sh_hid[...] = (silu(acc_g[...]) * acc_u[...]).astype(bf)

    def shared_out(q):
        wt = sh[2, q].reshape(quarter, cols)
        v = lax.dot_general(
            sh_hid[...], wt, (((1,), (1,)), ((), ())), preferred_element_type=f32
        )
        psum[:, q] = v.reshape(NX, n, quarter)

    def hot_in(h, v, is_first):
        off, r = parts[h]
        lanes = pl.ds(pl.multiple_of(v * rows + off, 128), r)
        quad_in(lanes, hg[lanes], hu[lanes], is_first)

    def shared_first():
        cp.got(*c_of["sh_z"])
        shared_in(0)

    d_z, d_y, d_y2 = [], [], []

    def d_z_send():
        d_z.extend(cp.remote(xd.at[r, 2], hd.at[y, r], at(0, 0, 1)) for r in (0, 1))

    def d_spread():
        for r in (0, 1):
            d_z[r].wait_recv()
            choose(fz, xd.shape[2], 16, lambda i, r=r: xd[r, 2, i], hd.at[y, r])
            d_y.append([cp.remote(hd.at[y, r], hd.at[y, r], at(0, d)) for d in (1, -1)])

    def d_forward():
        cp.got(d_y[0][0], d_y[1][1])
        d_y2.append(cp.remote(hd.at[lo, 0], hd.at[lo, 0], at(0, 1)))
        d_y2.append(cp.remote(hd.at[hi, 1], hd.at[hi, 1], at(0, -1)))

    def hot_part(h):
        hot_in(h, y, h == 0)
        for c in (near[h, 0][1], near[h, 1][1]):
            c.wait_recv()
        hot_in(h, lo, False)
        hot_in(h, hi, False)
        for c in (far2[h, 0], far2[h, 1]):
            c.wait_recv()
        hot_in(h, opp, False)

    def end():
        cp.got(*c_of["coef"], d_y[0][1], d_y[1][0], *d_y2)

    tasks = {
        "tok0": own_tokens, "tokx": quad_tokens, "tt": quad_across, "tf": quad_relay,
        "tq": quad_done, "own0": own_loads, "df": d_first, "dz0": d_z_send, "dy1": d_spread,
        "dy2": d_forward, "sx": sh_x, "s1": sh_1, "s2": sh_2, "s3": sh_3, "own1t": positions, "route": relay, "rf": rows_relay, "hr1": home_sum_core,
        "hr2": home_sum_across,
        "pack": pack, "wts": weights, "unpack": unpack_rows, "hm": home_mid, "ex2": send_back,
        "si0": shared_first, "sm": shared_mid, "hb": home_back, "end": end,
    }
    for name in ORDER:
        if name in tasks:
            tasks[name]()
            continue
        kind, at_ = name.rstrip("0123456789"), [int(c) for c in name.lstrip("abcdefghijklmnopqrstuvwxyz")]
        if kind == "xf":
            x_first(at_[0], at_[1:])
        else:
            {
                "x": x_step, "y": y_step, "sy": spread_y, "fy": forward_y, "hot": hot_part,
                "d": d_step, "dx": dx_step, "hi": home_in, "ho": home_out,
                "si": shared_in, "so": shared_out,
            }[kind](*at_)

    first, rest = slice(0, SPLIT), slice(SPLIT, quarter)
    to_c, by_x, by_z = {}, [], {}
    order = (2, 1, 3, 0)

    def grown(d, a, q):
        wd = hd[:, :, :, of_quarter(q)].reshape(cols, quarter)
        return psum[d, q] + dot(hot_hid[a], wd)

    def product(d):
        a = slice(d * n, (d + 1) * n)
        hot_hid[a] = (silu(acc_g[a]) * acc_u[a] * as_col(coefs[d, 0:1])).astype(bf)
        for side in (0, 1):
            to_core[d, side] = grown(d, a, 2 * side + 1 - core).astype(bf)
        to_c[d] = cp.remote(to_core.at[d], from_core.at[d], other)
        for side in (0, 1):
            q = 2 * side + core
            psum[d, q] = grown(d, a, q)

    def on_chip(d, side, lanes):
        return psum[d, 2 * side + core, :, lanes] + from_core[d, side, :, lanes].astype(f32)

    def onward(d):
        to_c[d].wait_recv()
        if d:
            for side in (0, 1):
                mid[d, side, :, first] = on_chip(d, side, first).astype(bf)
            by_x.append(cp.remote(mid.at[d, :, :, first], from_x.at[d - 1], at(d)))
        mid[d, 1 - z_hi, :, rest] = on_chip(d, 1 - z_hi, rest).astype(bf)
        by_z[d] = cp.remote(mid.at[d, 1 - z_hi, :, rest], from_zb.at[d], across)

    product(order[0])
    for i in (1, 2, 3):
        product(order[i])
        onward(order[i - 1])
    onward(order[3])
    by_xb = []
    for d in order[:3]:
        by_z[d].wait_recv()
        mid_b[d - 1] = (on_chip(d, z_hi, rest) + from_zb[d].astype(f32)).astype(bf)
        by_xb.append(cp.remote(mid_b.at[d - 1], from_xb.at[d - 1], at(d)))
    for c in by_x:
        c.wait_recv()

    def total(side):
        v = on_chip(0, side, first)
        for i in range(3):
            v += from_x[i, side].astype(f32)
        return v

    half[...] = total(1 - z_hi).astype(bf)
    last = cp.remote(half, from_z, across)
    own_total = total(z_hi) + back[:, first]
    by_z[0].wait_recv()
    v = on_chip(0, z_hi, rest) + from_zb[0].astype(f32) + back[:, rest]
    for c in by_xb:
        c.wait_recv()
    for i in range(3):
        v += from_xb[i].astype(f32)
    out[:, rest] = v
    last.wait_recv()
    out[:, first] = own_total + from_z[...].astype(f32)
    for c in cp.started:
        c.wait_send()
    exchanged(pack1, got1, 0, True)
    exchanged(pack2, got2, groups, True)


def local(
    tokens, slot, mask, hot_group, router_weight,
    exp_gate, exp_up, exp_down, sh_gate, sh_up, sh_down,
):
    bf, f32 = jnp.bfloat16, jnp.float32
    x, y, z = coords()
    hot = hot_group[0]
    hx, hy, hz = hot // (NY * NZ), (hot // NZ) % NY, hot % NZ
    scalars = jnp.stack(
        [(hx == x).astype(jnp.int32), (hy == y).astype(jnp.int32), (hz == z).astype(jnp.int32), hot]
    )
    n, quarter = tokens.shape
    d, h = exp_gate.shape[1:]
    rows, cols = d // NY, h // NX
    part = cols // (2 * NY)
    groups = NX * NY * NZ
    any_spec = pl.BlockSpec(memory_space=pl.ANY)
    vmem = pl.BlockSpec(memory_space=pltpu.VMEM)
    depth = -(-CAP * quarter // 128 // 16) * 16
    blocks = pltpu.VMEM((groups, depth, 128), bf)
    summed = pl.pallas_call(
        layer_kernel,
        out_shape=jax.ShapeDtypeStruct((n, quarter), f32),
        in_specs=[pl.BlockSpec(memory_space=pltpu.SMEM), any_spec, vmem, vmem] + [any_spec] * 6,
        out_specs=vmem,
        scratch_shapes=[
            pltpu.VMEM((NY, rows, h), bf),
            pltpu.VMEM((NY, rows, h), bf),
            pltpu.VMEM((NX, NY, 2, part, d), bf),
            pltpu.VMEM((NY, 3, rows, cols), bf),
            pltpu.VMEM((NY, 3, rows, cols), bf),
            pltpu.VMEM((3, rows, cols), bf),
            pltpu.VMEM((3, rows, cols), bf),
            pltpu.VMEM((2, 3, NX, part, d), bf),
            pltpu.VMEM((2, 3, part, d), bf),
            pltpu.VMEM((d, cols), bf),
            pltpu.VMEM((d, cols), bf),
            pltpu.VMEM((NY, 2, part, d), bf),
            pltpu.VMEM((3, NX, NY, NZ, sh_gate.shape[0], cols), bf),
            pltpu.VMEM((NX, n, d), bf),
            pltpu.VMEM((NX, 8, n), f32),
            blocks, blocks, blocks, blocks,
            pltpu.VMEM((n, d), bf),
            pltpu.VMEM((n, h), f32),
            pltpu.VMEM((n, h), f32),
            pltpu.VMEM((n, h), bf),
            pltpu.VMEM((NX * n, cols), f32),
            pltpu.VMEM((NX * n, cols), f32),
            pltpu.VMEM((NX * n, cols), bf),
            pltpu.VMEM((NX * n, cols), bf),
            pltpu.VMEM((NX, NT, n, quarter), f32),
            pltpu.VMEM((NX, 2, n, quarter), bf),
            pltpu.VMEM((NX, 2, n, quarter), bf),
            pltpu.VMEM((NX, 2, n, quarter), bf),
            pltpu.VMEM((3, 2, n, SPLIT), bf),
            pltpu.VMEM((n, SPLIT), bf),
            pltpu.VMEM((n, SPLIT), bf),
            pltpu.VMEM((NX, n, quarter - SPLIT), bf),
            pltpu.VMEM((3, n, quarter - SPLIT), bf),
            pltpu.VMEM((3, n, quarter - SPLIT), bf),
            pltpu.VMEM((n, 128), f32),
            pltpu.VMEM((n, 128), f32),
            pltpu.VMEM((n, 128), jnp.int32),
            pltpu.VMEM((n, quarter), bf),
            pltpu.VMEM((NT, n, quarter), f32),
            pltpu.VMEM((2, n, quarter), bf),
            pltpu.VMEM((2, n, quarter), bf),
            pltpu.VMEM((n, quarter), bf),
            pltpu.VMEM((n, quarter), bf),
            pltpu.VMEM((n, quarter), f32),
            pltpu.SemaphoreType.DMA((SENDS,)),
            pltpu.SemaphoreType.DMA((SENDS,)),
            pltpu.SemaphoreType.DMA((16,)),
            pltpu.SemaphoreType.DMA((2 * groups,)),
            pltpu.SemaphoreType.DMA((2 * groups,)),
        ],
        compiler_params=pltpu.CompilerParams(
            collective_id=0, has_side_effects=True, vmem_limit_bytes=62 * 2**20
        ),
    )(
        scalars, tokens, slot.reshape(1, n), router_weight.T,
        exp_gate[0], exp_up[0], exp_down[0].reshape(NX, NY, 2, part, d), sh_gate, sh_up, sh_down.T,
    )
    return (mask.astype(f32)[:, None] * summed).astype(bf)


def solution(mesh):
    in_specs = (
        P("expert", "tensor"),
        P("expert", None),
        P("expert"),
        P(),
        P(),
        P("expert", None, "tensor"),
        P("expert", None, "tensor"),
        P("expert", "tensor", None),
        P("expert", "tensor"),
        P("expert", "tensor"),
        P("tensor", "expert"),
    )
    out_specs = P("expert", "tensor")
    return jax.shard_map(local, mesh=mesh, in_specs=in_specs, out_specs=out_specs, check_vma=False)
```

```python
import jax
import jax.numpy as jnp
from jax import lax
from jax.experimental import pallas as pl
from jax.experimental.pallas import tpu as pltpu
from jax.sharding import PartitionSpec as P

MESH = pl.DeviceIdType.MESH
NX, NY, NZ, NT, CAP = 4, 4, 2, 4, 4

PARTS = ((0, 384), (384, 128), (512, 128))
SPLIT = 384
SENDS = 240
ORDER = (
    "df", "tok0", "tokx", "sx", "xf00", "own0", "own1t", "pack", "xf01", "route", "wts", "tt",
    "xf02", "s1", "xf03", "d0", "x000", "unpack", "xf12", "xf10", "tf", "x010", "tq", "xf11",
    "x020", "s2", "x030", "x001", "rf", "x120", "x100", "hi0", "hi1", "d1", "x011", "hi2", "x110",
    "hi3", "s3", "hm", "ho0", "ho1", "ho2", "ho3", "hr1", "x021", "x031", "x002", "y00", "hr2",
    "x121", "xf20", "x101", "d2", "dx0", "x012", "y01", "x111", "xf21", "si0", "si1", "x022", "si2",
    "y02", "si3", "x032", "x122", "sm", "so0", "so1", "x102", "y03", "y10", "so2", "dx1", "x112",
    "so3", "y11", "x200", "x210", "ex2", "dx2", "y12", "x201", "xf13", "xf22", "xf23", "sy0",
    "x211", "hb", "dx3", "dz0", "x202", "y20", "fy0", "x130", "x220", "x230", "x212", "y21", "x131",
    "x221", "dy1", "x231", "hot0", "x132", "y13", "x222", "y22", "x232", "dy2", "sy1", "y23", "fy1",
    "sy2", "hot1", "fy2", "hot2", "end",
)


def coords():
    e = lax.axis_index("expert")
    return lax.div(e, NY * NZ), lax.rem(lax.div(e, NZ), NY), lax.rem(e, NZ)


def group_of(x, y, z):
    return (x * NY + y) * NZ + z


def turn(i, n=4):
    return lax.rem(i + 2 * n, n)


class Copies:
    def __init__(self, send, recv, local):
        self.send, self.recv, self.local = send, recv, local
        self.sent, self.kept = 0, 0
        self.started = []
        self.waited = set()

    def remote(self, src, dst, device):
        c = pltpu.make_async_remote_copy(
            src_ref=src,
            dst_ref=dst,
            send_sem=self.send.at[self.sent],
            recv_sem=self.recv.at[self.sent],
            device_id=device,
            device_id_type=MESH,
        )
        self.sent += 1
        c.start()
        self.started.append(c)
        return c

    def here(self, src, dst):
        c = pltpu.make_async_copy(src, dst, self.local.at[self.kept])
        self.kept += 1
        c.start()
        return c

    def once(self, c, remote):
        if id(c) not in self.waited:
            self.waited.add(id(c))
            if remote:
                c.wait_recv()
            else:
                c.wait()

    def got(self, *copies):
        for c in copies:
            self.once(c, True)

    def placed(self, *copies):
        for c in copies:
            self.once(c, False)


def choose(flag, rows, step, mine, into):
    def body(i, carry):
        at = pl.ds(pl.multiple_of(i * step, step), step)
        into[at] = jnp.where(flag == 1, mine(at), into[at])
        return carry

    lax.fori_loop(0, rows // step, body, 0)


def dot(a, b):
    return jnp.dot(a, b, preferred_element_type=jnp.float32)


def silu(v):
    return v / (1.0 + jnp.exp(-v))


def layer_kernel(
    scalars, tok, slot, router, gate, up, down, sh_gate, sh_up, sh_down,
    out,
    own_g, own_u, own_d, xg, xu, yg, yu, yd, xd, hg, hu, hd, sh, tk, coefs,
    pack1, got1, pack2, got2, rows_in, home_g, home_u, home_hid,
    acc_g, acc_u, sh_hid, hot_hid, psum, to_core, from_core, mid, from_x, half, from_z, from_zb, mid_b, from_xb,
    w_cols, target_cols, expert_cols,
    tok_here, home_part, home_send, home_core, home_half, home_z, back,
    send, recv, local, a2a_send, a2a_recv,
):
    x, y, z = coords()
    e = lax.axis_index("expert")
    groups = lax.axis_size("expert")
    t = lax.axis_index("tensor")
    core, z_hi = lax.rem(t, 2), lax.div(t, 2)
    cp = Copies(send, recv, local)
    rows, cols = xg.shape[2], xg.shape[3]
    n, quarter = tok.shape
    bf, f32 = jnp.bfloat16, jnp.float32
    parts = PARTS

    def at(dx=0, dy=0, dz=0):
        return {"expert": group_of(turn(x + dx), turn(y + dy), turn(z + dz, 2)), "tensor": t}

    other_t = z_hi * 2 + (1 - core)
    across_t = (1 - z_hi) * 2 + core
    other = {"expert": e, "tensor": other_t}
    across = {"expert": e, "tensor": across_t}

    def of_quarter(i):
        return pl.ds(pl.multiple_of(i * quarter, quarter), quarter)

    barrier = pltpu.get_barrier_semaphore()

    def greet(k, carry):
        d = {"expert": lax.rem(e + k, groups), "tensor": t}
        pl.semaphore_signal(barrier, inc=1, device_id=d, device_id_type=MESH)
        return carry

    lax.fori_loop(1, groups, greet, 0)
    for d in (other, across):
        pl.semaphore_signal(barrier, inc=1, device_id=d, device_id_type=MESH)
    fx, fy, fz, hot = scalars[0], scalars[1], scalars[2], scalars[3]

    streams = ((gate, own_g, xg, yg, hg, 1), (up, own_u, xu, yu, hu, -1))

    def block(sign, j):
        return turn(y - sign * (1 + j))

    x_copy, own_copy, y_copy, z_copy = {}, {}, {}, {}

    def x_first(h, js):
        off, r = parts[h]
        for j in js:
            for s, (w, _, xb, _, _, sign) in enumerate(streams):
                lanes = pl.ds(pl.multiple_of(turn(x - sign) * cols, cols), cols)
                src = w.at[pl.ds(pl.multiple_of(block(sign, j) * rows + off, 128), r), lanes]
                x_copy[h, s, j, 0] = cp.remote(src, xb.at[j, 0, pl.ds(off, r)], at(sign))

    def own_load(j):
        for s, (w, own, _, _, _, sign) in enumerate(streams):
            src = w.at[pl.ds(pl.multiple_of(block(sign, j) * rows, rows), rows), :]
            own_copy[s, j] = cp.here(src, own.at[j])

    def x_step(h, j, step):
        off, r = parts[h]
        for s, (_, own, xb, _, _, sign) in enumerate(streams):
            x_copy[h, s, j, step].wait_recv()
            cp.placed(own_copy[s, j])
            lanes = pl.ds(pl.multiple_of(turn(x - sign * (2 + step)) * cols, cols), cols)
            mine = own.at[j, pl.ds(off, r)]
            into = xb.at[j, step, pl.ds(off, r)]
            choose(fx, r, 128, lambda a, mine=mine, lanes=lanes: mine[a, lanes], into)
            if step < 2:
                nxt = xb.at[j, step + 1, pl.ds(off, r)]
                x_copy[h, s, j, step + 1] = cp.remote(into, nxt, at(sign))

    def y_step(h, j):
        off, r = parts[h]
        for s, (_, _, xb, yb, hb, sign) in enumerate(streams):
            mine = xb.at[j, 2, pl.ds(off, r)]
            if j == 0:
                y_copy[h, s, 0] = cp.remote(mine, yb.at[0, pl.ds(off, r)], at(0, sign))
                continue
            into = yb.at[j - 1, pl.ds(off, r)]
            y_copy[h, s, j - 1].wait_recv()
            choose(fy, r, 128, lambda a, mine=mine: mine[a], into)
            if j < 3:
                y_copy[h, s, j] = cp.remote(into, yb.at[j, pl.ds(off, r)], at(0, sign))
            else:
                z_copy[h, s] = cp.remote(into, hot_rows(hb, h, y), at(0, 0, 1))

    def hot_rows(ref, h, v):
        off, r = parts[h]
        return ref.at[pl.ds(pl.multiple_of(v * rows + off, 128), r)]

    near, far2 = {}, {}

    def spread_y(h):
        off, r = parts[h]
        for s, (_, _, _, yb, hb, sign) in enumerate(streams):
            into = hot_rows(hb, h, y)
            mine = yb.at[2, pl.ds(off, r)]
            z_copy[h, s].wait_recv()
            choose(fz, r, 128, lambda a, mine=mine: mine[a], into)
            near[h, s] = [cp.remote(into, into, at(0, d)) for d in (sign, -sign)]

    def forward_y(h):
        for s, (_, _, _, _, hb, sign) in enumerate(streams):
            near[h, s][0].wait_recv()
            a = hot_rows(hb, h, turn(y - sign))
            far2[h, s] = cp.remote(a, a, at(0, sign))

    d_copy, dx_copy = {}, {}

    def d_first():
        for r, sign in ((0, 1), (1, -1)):
            d_copy[r, 0] = cp.remote(down.at[:, turn(y - sign), r], yd.at[r, 0], at(0, sign))

    def d_step(step):
        for r, sign in ((0, 1), (1, -1)):
            d_copy[r, step].wait_recv()
            cp.placed(c_of["down"])
            yp = turn(y - sign * (2 + step))
            choose(fy, NX, 1, lambda i, yp=yp, r=r: own_d[i, yp, r], yd.at[r, step])
            if step < 2:
                d_copy[r, step + 1] = cp.remote(yd.at[r, step], yd.at[r, step + 1], at(0, sign))

    def dx_step(step):
        for r, sign in ((0, 1), (1, -1)):
            if step == 0:
                dx_copy[r, 0] = cp.remote(yd.at[r, 2, turn(x - sign)], xd.at[r, 0], at(sign))
                continue
            dx_copy[r, step - 1].wait_recv()
            xp = turn(x - sign * (1 + step))
            choose(
                fx, xd.shape[2], 16, lambda i, xp=xp, r=r: yd[r, 2, xp, i], xd.at[r, step - 1]
            )
            if step < 3:
                dx_copy[r, step] = cp.remote(xd.at[r, step - 1], xd.at[r, step], at(sign))

    def exchange(src, dst, base):
        def go(k, carry):
            to = lax.rem(e + k, groups)
            pltpu.make_async_remote_copy(
                src_ref=src.at[to], dst_ref=dst.at[e],
                send_sem=a2a_send.at[base + k], recv_sem=a2a_recv.at[base + k],
                device_id={"expert": to, "tensor": t}, device_id_type=MESH,
            ).start()
            return carry

        lax.fori_loop(1, groups, go, 0)
        return cp.here(src.at[e], dst.at[e])

    def exchanged(src, dst, base, sends):
        def done(k, carry):
            to = lax.rem(e + k, groups)
            frm = lax.rem(e + groups - k, groups)
            c = pltpu.make_async_remote_copy(
                src_ref=src.at[to], dst_ref=dst.at[frm],
                send_sem=a2a_send.at[base + k], recv_sem=a2a_recv.at[base + k],
                device_id={"expert": to, "tensor": t}, device_id_type=MESH,
            )
            if sends:
                c.wait_send()
            else:
                c.wait_recv()
            return carry

        lax.fori_loop(1, groups, done, 0)

    def iota(shape, dim):
        return lax.broadcasted_iota(jnp.int32, shape, dim)

    def as_row(col):
        eye = iota((n, n), 0) == iota((n, n), 1)
        return jnp.sum(jnp.where(eye, col, 0.0), axis=0, keepdims=True)

    def as_col(row):
        eye = iota((n, n), 0) == iota((n, n), 1)
        return jnp.sum(jnp.where(eye, row, 0.0), axis=1, keepdims=True)

    groups_here = NX * NY * NZ

    depth = pack1.shape[1]
    tiles = quarter // 128

    def packed(c, i, key):
        r = iota((n, n), 0) + c * n
        of = (r // depth) * CAP + r % CAP
        return ((of.astype(f32) == key) & ((r % depth) // CAP == i)).astype(bf)

    def pack_into(into, v, key):
        for c in range(groups_here * depth // n):
            acc = jnp.zeros((n, 128), f32)
            for i in range(tiles):
                acc += dot(packed(c, i, key), v[:, i * 128 : (i + 1) * 128])
            into[c * n // depth : (c + 1) * n // depth] = acc.astype(bf).reshape(
                n // depth, depth, 128
            )

    def unpacked(flat, i, key):
        r = iota((n, groups_here * depth), 1)
        of = (r // depth) * CAP + r % CAP
        pick = ((of.astype(f32) == key) & ((r % depth) // CAP == i)).astype(bf)
        return dot(pick, flat)

    mine = of_quarter(t)
    theirs = of_quarter(across_t)
    c_of = {}

    def own_tokens():
        c_of["peer"] = [cp.remote(tok, tk.at[0, :, mine], d) for d in (other, across)]

    def quad_tokens():
        c_of["quad"] = [cp.remote(tok, tk.at[(4 - d) % 4, :, mine], at(d)) for d in (2, 1, -1)]

    def quad_across():
        cp.got(*c_of["quad"])
        a = tk.at[1:4, :, mine]
        c_of["quad_peer"] = [cp.remote(a, a, d) for d in (other, across)]

    def quad_relay():
        cp.got(c_of["quad_peer"][1])
        a = tk.at[1:4, :, theirs]
        c_of["quad_relay"] = cp.remote(a, a, other)

    def quad_done():
        cp.got(c_of["quad_peer"][0], c_of["quad_relay"])

    def own_loads():
        for j in range(4):
            own_load(j)
            if j == 0:
                c_of["down"] = cp.here(down, own_d)

    sh_refs = (sh_gate, sh_up, sh_down)

    def sh_piece(i, xp):
        return sh_refs[i].at[:, pl.ds(pl.multiple_of(xp * cols, cols), cols)]

    lo, hi, opp = turn(y - 1), turn(y + 1), turn(y + 2)

    def sh_x():
        c_of["sh_x"] = [
            cp.remote(sh_piece(i, turn(x + d)), sh.at[i, x, y, z], at(d))
            for d in (2, 1, -1)
            for i in range(3)
        ]
        c_of["sh_own"] = [cp.here(sh_piece(i, x), sh.at[i, x, y, z]) for i in range(3)]

    def sh_to(a, device):
        return cp.remote(a, a, device)

    def sh_1():
        cp.got(*c_of["sh_x"])
        cp.placed(*c_of["sh_own"])
        c_of["sh_y"] = [sh_to(sh.at[:, :, y, z], at(0, d)) for d in (1, -1)]
        c_of["sh_z"] = [sh_to(sh.at[:, :, y, z], at(0, 0, 1))]

    def sh_2():
        cp.got(*c_of["sh_y"])
        c_of["sh_y2"] = [
            sh_to(sh.at[:, 0:2, lo, z], at(0, 1)), sh_to(sh.at[:, 2:4, hi, z], at(0, -1))
        ]
        c_of["sh_z"] += [sh_to(sh.at[:, :, v, z], at(0, 0, 1)) for v in (lo, hi)]

    def sh_3():
        cp.got(*c_of["sh_y2"])
        c_of["sh_z"].append(sh_to(sh.at[:, :, opp, z], at(0, 0, 1)))

    def positions():
        cp.placed(c_of["here"])
        ids_row = slot[...].astype(f32)
        ids_f = as_col(ids_row)
        ids = ids_f.astype(jnp.int32)
        same = jnp.where((ids_f == ids_row) & (iota((n, n), 1) < iota((n, n), 0)), 1.0, 0.0)
        position = jnp.sum(same, axis=1, keepdims=True)
        spare = (ids & 1) == 1
        target = jnp.where(spare, -1.0, (ids >> 1).astype(f32) * CAP + position)
        target_cols[...] = jnp.broadcast_to(target, target_cols.shape)
        expert = jnp.where(spare, hot, ids >> 1)
        expert_cols[...] = jnp.broadcast_to(expert, expert_cols.shape)

    def relay():
        cp.placed(c_of["own"])
        cp.got(c_of["peer"][1])
        a = tk.at[0, :, theirs]
        c_of["relay"] = cp.remote(a, a, other)

    def pack():
        pack_into(pack1, tok_here, as_row(target_cols[:, 0:1]))
        c_of["own1"] = exchange(pack1, got1, 0)

    def weights():
        cp.got(c_of["peer"][0], c_of["relay"])
        logits = lax.dot_general(
            tk[0], router[...], (((1,), (1,)), ((), ())), preferred_element_type=f32
        )
        chosen = expert_cols[:, 0 : logits.shape[1]] == iota(logits.shape, 1)
        w = jax.nn.sigmoid(jnp.sum(jnp.where(chosen, logits, 0.0), axis=1, keepdims=True))
        w_cols[...] = jnp.broadcast_to(w, w_cols.shape)
        coef = jnp.where(target_cols[:, 0:1] < 0, w, 0.0)
        coefs[0] = jnp.broadcast_to(as_row(coef), coefs.shape[1:])
        c_of["coef"] = [cp.remote(coefs.at[0], coefs.at[(4 - d) % 4], at(d)) for d in (2, 1, -1)]

    def unpack_rows():
        exchanged(pack1, got1, 0, False)
        cp.placed(c_of["own1"])
        flat = got1[...].reshape(groups_here * depth, 128)
        key = iota((n, 1), 0).astype(f32)
        for i in range(tiles):
            lanes = pl.ds(pl.multiple_of(t * quarter + i * 128, 128), 128)
            rows_in[:, lanes] = unpacked(flat, i, key).astype(bf)
        a = rows_in.at[:, mine]
        c_of["rows"] = [cp.remote(a, a, d) for d in (other, across)]

    def rows_relay():
        cp.got(c_of["rows"][1])
        a = rows_in.at[:, theirs]
        c_of["rows_relay"] = cp.remote(a, a, other)

    def home_in(j):
        if j == 0:
            cp.got(c_of["rows"][0], c_of["rows_relay"])
        for acc, own, sign in ((home_g, own_g, 1), (home_u, own_u, -1)):
            cp.placed(own_copy[0 if sign == 1 else 1, j])
            a = rows_in[:, pl.ds(pl.multiple_of(block(sign, j) * rows, rows), rows)]
            v = dot(a, own[j])
            acc[...] = v if j == 0 else acc[...] + v

    def home_mid():
        home_hid[...] = (silu(home_g[...]) * home_u[...]).astype(bf)

    def home_out(q):
        cp.placed(c_of["down"])
        lanes = slice(q * quarter, (q + 1) * quarter)
        v = jnp.zeros((n, quarter), f32)
        for i in range(NX):
            wd = own_d[i, :, :, :, lanes].reshape(cols, quarter)
            v += dot(home_hid[:, i * cols : (i + 1) * cols], wd)
        home_part[q] = v

    def home_sum_core():
        for side in (0, 1):
            home_send[side] = home_part[2 * side + 1 - core].astype(bf)
        c_of["home_core"] = cp.remote(home_send, home_core, other)

    def home_sum_across():
        cp.got(c_of["home_core"])
        v = home_part[2 * (1 - z_hi) + core] + home_core[1 - z_hi].astype(f32)
        home_half[...] = v.astype(bf)
        c_of["home_z"] = cp.remote(home_half, home_z, across)

    def send_back():
        cp.got(c_of["home_z"])
        v = home_part[2 * z_hi + core] + home_core[z_hi].astype(f32) + home_z[...].astype(f32)
        row = iota((1, n), 1).astype(f32)
        pack_into(pack2, v.astype(bf), row)
        c_of["own2"] = exchange(pack2, got2, groups)

    def home_back():
        exchanged(pack2, got2, groups, False)
        cp.placed(c_of["own2"])
        flat = got2[...].reshape(groups_here * depth, 128)
        key = target_cols[:, 0:1]
        for i in range(tiles):
            lanes = slice(i * 128, (i + 1) * 128)
            back[:, lanes] = w_cols[:, 0:1] * unpacked(flat, i, key)

    def quad_in(lanes, w_gate, w_up, first):
        a = tk[:, :, lanes].reshape(NX * n, -1)
        for acc, wt in ((acc_g, w_gate), (acc_u, w_up)):
            v = dot(a, wt)
            acc[...] = v if first else acc[...] + v

    def shared_in(k):
        quad_in(
            slice(k * rows, (k + 1) * rows),
            sh[0, k].reshape(rows, cols), sh[1, k].reshape(rows, cols), k == 0,
        )

    def shared_mid():
        sh_hid[...] = (silu(acc_g[...]) * acc_u[...]).astype(bf)

    def shared_out(q):
        wt = sh[2, q].reshape(quarter, cols)
        v = lax.dot_general(
            sh_hid[...], wt, (((1,), (1,)), ((), ())), preferred_element_type=f32
        )
        psum[:, q] = v.reshape(NX, n, quarter)

    def hot_in(h, v, is_first):
        off, r = parts[h]
        lanes = pl.ds(pl.multiple_of(v * rows + off, 128), r)
        quad_in(lanes, hg[lanes], hu[lanes], is_first)

    def shared_first():
        cp.got(*c_of["sh_z"])
        shared_in(0)

    d_z, d_y, d_y2 = [], [], []

    def d_z_send():
        d_z.extend(cp.remote(xd.at[r, 2], hd.at[y, r], at(0, 0, 1)) for r in (0, 1))

    def d_spread():
        for r in (0, 1):
            d_z[r].wait_recv()
            choose(fz, xd.shape[2], 16, lambda i, r=r: xd[r, 2, i], hd.at[y, r])
            d_y.append([cp.remote(hd.at[y, r], hd.at[y, r], at(0, d)) for d in (1, -1)])

    def d_forward():
        cp.got(d_y[0][0], d_y[1][1])
        d_y2.append(cp.remote(hd.at[lo, 0], hd.at[lo, 0], at(0, 1)))
        d_y2.append(cp.remote(hd.at[hi, 1], hd.at[hi, 1], at(0, -1)))

    def hot_part(h):
        hot_in(h, y, h == 0)
        for c in (near[h, 0][1], near[h, 1][1]):
            c.wait_recv()
        hot_in(h, lo, False)
        hot_in(h, hi, False)
        for c in (far2[h, 0], far2[h, 1]):
            c.wait_recv()
        hot_in(h, opp, False)

    def end():
        cp.got(*c_of["coef"], d_y[0][1], d_y[1][0], *d_y2)

    tasks = {
        "tok0": own_tokens, "tokx": quad_tokens, "tt": quad_across, "tf": quad_relay,
        "tq": quad_done, "own0": own_loads, "df": d_first, "dz0": d_z_send, "dy1": d_spread,
        "dy2": d_forward, "sx": sh_x, "s1": sh_1, "s2": sh_2, "s3": sh_3, "own1t": positions, "route": relay, "rf": rows_relay, "hr1": home_sum_core,
        "hr2": home_sum_across,
        "pack": pack, "wts": weights, "unpack": unpack_rows, "hm": home_mid, "ex2": send_back,
        "si0": shared_first, "sm": shared_mid, "hb": home_back, "end": end,
    }
    c_of["here"] = cp.here(tok, tok_here)
    c_of["own"] = cp.here(tok, tk.at[0, :, mine])
    own_loads()
    positions()
    pl.semaphore_wait(barrier, groups + 1)
    for name in ORDER:
        if name in ("own0", "own1t"):
            continue
        if name in tasks:
            tasks[name]()
            continue
        kind, at_ = name.rstrip("0123456789"), [int(c) for c in name.lstrip("abcdefghijklmnopqrstuvwxyz")]
        if kind == "xf":
            x_first(at_[0], at_[1:])
        else:
            {
                "x": x_step, "y": y_step, "sy": spread_y, "fy": forward_y, "hot": hot_part,
                "d": d_step, "dx": dx_step, "hi": home_in, "ho": home_out,
                "si": shared_in, "so": shared_out,
            }[kind](*at_)

    first, rest = slice(0, SPLIT), slice(SPLIT, quarter)
    to_c, by_x, by_z = {}, [], {}
    order = (2, 1, 3, 0)

    def grown(d, a, q):
        wd = hd[:, :, :, of_quarter(q)].reshape(cols, quarter)
        return psum[d, q] + dot(hot_hid[a], wd)

    def product(d):
        a = slice(d * n, (d + 1) * n)
        hot_hid[a] = (silu(acc_g[a]) * acc_u[a] * as_col(coefs[d, 0:1])).astype(bf)
        for side in (0, 1):
            to_core[d, side] = grown(d, a, 2 * side + 1 - core).astype(bf)
        to_c[d] = cp.remote(to_core.at[d], from_core.at[d], other)
        for side in (0, 1):
            q = 2 * side + core
            psum[d, q] = grown(d, a, q)

    def on_chip(d, side, lanes):
        return psum[d, 2 * side + core, :, lanes] + from_core[d, side, :, lanes].astype(f32)

    def onward(d):
        to_c[d].wait_recv()
        if d:
            for side in (0, 1):
                mid[d, side, :, first] = on_chip(d, side, first).astype(bf)
            by_x.append(cp.remote(mid.at[d, :, :, first], from_x.at[d - 1], at(d)))
        mid[d, 1 - z_hi, :, rest] = on_chip(d, 1 - z_hi, rest).astype(bf)
        by_z[d] = cp.remote(mid.at[d, 1 - z_hi, :, rest], from_zb.at[d], across)

    product(order[0])
    for i in (1, 2, 3):
        product(order[i])
        onward(order[i - 1])
    onward(order[3])
    by_xb = []
    for d in order[:3]:
        by_z[d].wait_recv()
        mid_b[d - 1] = (on_chip(d, z_hi, rest) + from_zb[d].astype(f32)).astype(bf)
        by_xb.append(cp.remote(mid_b.at[d - 1], from_xb.at[d - 1], at(d)))
    for c in by_x:
        c.wait_recv()

    def total(side):
        v = on_chip(0, side, first)
        for i in range(3):
            v += from_x[i, side].astype(f32)
        return v

    half[...] = total(1 - z_hi).astype(bf)
    last = cp.remote(half, from_z, across)
    own_total = total(z_hi) + back[:, first]
    by_z[0].wait_recv()
    v = on_chip(0, z_hi, rest) + from_zb[0].astype(f32) + back[:, rest]
    for c in by_xb:
        c.wait_recv()
    for i in range(3):
        v += from_xb[i].astype(f32)
    out[:, rest] = v
    last.wait_recv()
    out[:, first] = own_total + from_z[...].astype(f32)
    for c in cp.started:
        c.wait_send()
    exchanged(pack1, got1, 0, True)
    exchanged(pack2, got2, groups, True)


def local(
    tokens, slot, mask, hot_group, router_weight,
    exp_gate, exp_up, exp_down, sh_gate, sh_up, sh_down,
):
    bf, f32 = jnp.bfloat16, jnp.float32
    x, y, z = coords()
    hot = hot_group[0]
    hx, hy, hz = hot // (NY * NZ), (hot // NZ) % NY, hot % NZ
    scalars = jnp.stack(
        [(hx == x).astype(jnp.int32), (hy == y).astype(jnp.int32), (hz == z).astype(jnp.int32), hot]
    )
    n, quarter = tokens.shape
    d, h = exp_gate.shape[1:]
    rows, cols = d // NY, h // NX
    part = cols // (2 * NY)
    groups = NX * NY * NZ
    any_spec = pl.BlockSpec(memory_space=pl.ANY)
    vmem = pl.BlockSpec(memory_space=pltpu.VMEM)
    depth = -(-CAP * quarter // 128 // 16) * 16
    blocks = pltpu.VMEM((groups, depth, 128), bf)
    summed = pl.pallas_call(
        layer_kernel,
        out_shape=jax.ShapeDtypeStruct((n, quarter), f32),
        in_specs=[pl.BlockSpec(memory_space=pltpu.SMEM), any_spec, vmem, vmem] + [any_spec] * 6,
        out_specs=vmem,
        scratch_shapes=[
            pltpu.VMEM((NY, rows, h), bf),
            pltpu.VMEM((NY, rows, h), bf),
            pltpu.VMEM((NX, NY, 2, part, d), bf),
            pltpu.VMEM((NY, 3, rows, cols), bf),
            pltpu.VMEM((NY, 3, rows, cols), bf),
            pltpu.VMEM((3, rows, cols), bf),
            pltpu.VMEM((3, rows, cols), bf),
            pltpu.VMEM((2, 3, NX, part, d), bf),
            pltpu.VMEM((2, 3, part, d), bf),
            pltpu.VMEM((d, cols), bf),
            pltpu.VMEM((d, cols), bf),
            pltpu.VMEM((NY, 2, part, d), bf),
            pltpu.VMEM((3, NX, NY, NZ, sh_gate.shape[0], cols), bf),
            pltpu.VMEM((NX, n, d), bf),
            pltpu.VMEM((NX, 8, n), f32),
            blocks, blocks, blocks, blocks,
            pltpu.VMEM((n, d), bf),
            pltpu.VMEM((n, h), f32),
            pltpu.VMEM((n, h), f32),
            pltpu.VMEM((n, h), bf),
            pltpu.VMEM((NX * n, cols), f32),
            pltpu.VMEM((NX * n, cols), f32),
            pltpu.VMEM((NX * n, cols), bf),
            pltpu.VMEM((NX * n, cols), bf),
            pltpu.VMEM((NX, NT, n, quarter), f32),
            pltpu.VMEM((NX, 2, n, quarter), bf),
            pltpu.VMEM((NX, 2, n, quarter), bf),
            pltpu.VMEM((NX, 2, n, quarter), bf),
            pltpu.VMEM((3, 2, n, SPLIT), bf),
            pltpu.VMEM((n, SPLIT), bf),
            pltpu.VMEM((n, SPLIT), bf),
            pltpu.VMEM((NX, n, quarter - SPLIT), bf),
            pltpu.VMEM((3, n, quarter - SPLIT), bf),
            pltpu.VMEM((3, n, quarter - SPLIT), bf),
            pltpu.VMEM((n, 128), f32),
            pltpu.VMEM((n, 128), f32),
            pltpu.VMEM((n, 128), jnp.int32),
            pltpu.VMEM((n, quarter), bf),
            pltpu.VMEM((NT, n, quarter), f32),
            pltpu.VMEM((2, n, quarter), bf),
            pltpu.VMEM((2, n, quarter), bf),
            pltpu.VMEM((n, quarter), bf),
            pltpu.VMEM((n, quarter), bf),
            pltpu.VMEM((n, quarter), f32),
            pltpu.SemaphoreType.DMA((SENDS,)),
            pltpu.SemaphoreType.DMA((SENDS,)),
            pltpu.SemaphoreType.DMA((16,)),
            pltpu.SemaphoreType.DMA((2 * groups,)),
            pltpu.SemaphoreType.DMA((2 * groups,)),
        ],
        compiler_params=pltpu.CompilerParams(
            collective_id=0, has_side_effects=True, vmem_limit_bytes=62 * 2**20
        ),
    )(
        scalars, tokens, slot.reshape(1, n), router_weight.T,
        exp_gate[0], exp_up[0], exp_down[0].reshape(NX, NY, 2, part, d), sh_gate, sh_up, sh_down.T,
    )
    return (mask.astype(f32)[:, None] * summed).astype(bf)


def solution(mesh):
    in_specs = (
        P("expert", "tensor"),
        P("expert", None),
        P("expert"),
        P(),
        P(),
        P("expert", None, "tensor"),
        P("expert", None, "tensor"),
        P("expert", "tensor", None),
        P("expert", "tensor"),
        P("expert", "tensor"),
        P("tensor", "expert"),
    )
    out_specs = P("expert", "tensor")
    return jax.shard_map(local, mesh=mesh, in_specs=in_specs, out_specs=out_specs, check_vma=False)
```
